32 devices in a mesh: cell: 2 (over core), blk: 16 (over z, y, x).
Axes of the slice: x: 2, y: 2, z: 4, core: 2. Of those that a mesh axis runs over, the one named last changes fastest.
Arguments:
- node_scalars: float32 [4096, 128], P(('cell', 'blk')), parts along dimension 0, may hold values from -6 to 6
- node_vectors: float32 [3, 4096, 128], P(None, ('cell', 'blk')), parts along dimension 1, may hold values from -6 to 6
- positions: float32 [3, 4096], P(None, ('cell', 'blk')), parts along dimension 1, may hold values from 0 to 1
- species: int32 [4096], P(('cell', 'blk')), parts along dimension 0, may hold values from 0 to 3
- edge_senders: int32 [32, 5, 1024], P(('cell', 'blk')), parts along dimension 0, may hold values from 0 to 127
- edge_receivers: int32 [32, 5, 1024], P(('cell', 'blk')), parts along dimension 0, may hold values from 0 to 127
- edge_shifts: int32 [32, 5, 3, 1024], P(('cell', 'blk')), parts along dimension 0, may hold values from -1 to 1
- bucket_counts: int32 [32, 5], P(('cell', 'blk')), parts along dimension 0, may hold values from 256 to 1024, as said below
- w_up: float32 [2, 128, 128], replicated, may hold values from -0.5 to 0.5
- w_rad_in: float32 [8, 64], replicated, may hold values from -4 to 4
- w_rad_mid: float32 [2, 64, 64], replicated, may hold values from -1.5 to 1.5
- w_rad_out: float32 [64, 896], replicated, may hold values from -1.5 to 1.5
- w_lin: float32 [4, 128, 128], replicated, may hold values from -0.5 to 0.5
- w_sc_scalar: float32 [4, 9, 128], replicated, may hold values from -0.6 to 0.6
- w_sc_vector: float32 [4, 5, 128], replicated, may hold values from -1.8 to 1.8
- w_prod: float32 [2, 128, 128], replicated, may hold values from -0.5 to 0.5
- w_skip: float32 [2, 4, 128, 128], replicated, may hold values from -0.5 to 0.5
- w_read: float32 [128], replicated, may hold values from -0.5 to 0.5
- cot_scalars: float32 [4096, 128], P(('cell', 'blk')), parts along dimension 0, may hold values from -6 to 6
- cot_vectors: float32 [3, 4096, 128], P(None, ('cell', 'blk')), parts along dimension 1, may hold values from -6 to 6
- cot_energy: float32 [4096], P(('cell', 'blk')), parts along dimension 0, may hold values from -6 to 6
Outputs:
- new_scalars: float32 [4096, 128], P(('cell', 'blk')), parts along dimension 0
- new_vectors: float32 [3, 4096, 128], P(None, ('cell', 'blk')), parts along dimension 1
- atom_energy: float32 [4096], P(('cell', 'blk')), parts along dimension 0
- grad_scalars: float32 [4096, 128], P(('cell', 'blk')), parts along dimension 0
- grad_vectors: float32 [3, 4096, 128], P(None, ('cell', 'blk')), parts along dimension 1
- grad_w_up: float32 [2, 2, 128, 128], P('cell'), parts along dimension 0
- grad_w_rad_in: float32 [2, 8, 64], P('cell'), parts along dimension 0
- grad_w_rad_mid: float32 [2, 2, 64, 64], P('cell'), parts along dimension 0
- grad_w_rad_out: float32 [2, 64, 896], P('cell'), parts along dimension 0
- grad_w_lin: float32 [2, 4, 128, 128], P('cell'), parts along dimension 0
- grad_w_sc_scalar: float32 [2, 4, 9, 128], P('cell'), parts along dimension 0
- grad_w_sc_vector: float32 [2, 4, 5, 128], P('cell'), parts along dimension 0
- grad_w_prod: float32 [2, 2, 128, 128], P('cell'), parts along dimension 0
- grad_w_skip: float32 [2, 2, 4, 128, 128], P('cell'), parts along dimension 0
- grad_w_read: float32 [2, 128], P('cell'), parts along dimension 0
The draws below stay inside these ranges and needn't reach their ends.
There are 2 independent parts, one for each index of `cell`. The reference program is written for one: setup_inputs(seed, part) draws one part's arguments, and reference() takes and returns one part's arrays. A program takes and returns all parts, laid end to end along the dimension named above; an argument that names none is the same for every part. Nothing has to cross between parts.
Inputs may be any that keep to these rules, and one draw needn't show every extreme that they name: bucket_counts[r, k] edges fill the leading slots of bucket k of slab r; the other slots are padding. On every slab some bucket is full (1024).
All inputs are finite; a program needn't handle non-finite values.
Results may differ from the reference program's by a relative error of at most 0.0003.
Values sent between devices are 32-bit elements; how exact they have to be, the bound alone decides.
No kernel may reach another device: no remote copies, remote signals or barrier semaphores. Data moves between devices by JAX's collectives and lax.ppermute only.
A program may use at most 256 MiB of HBM per device.

```python
import math
import jax
import jax.numpy as jnp
from jax import lax

C = 128
NBASIS = 8
RAD_HID = 64
NSPEC = 4
PATHS = 7
ATOM_DEV = 128
REACH = 2
NB = 5
EB = 1024
ATOMS = 2048
N_BLK = 16


def draw_bucket_counts(key, part):
    key = jax.random.fold_in(key, 11)
    first_key, second_key = jax.random.split(key)
    counts = jax.random.randint(first_key, (N_BLK, NB), EB // 4, EB + 1)
    full_slot = jax.random.randint(second_key, (N_BLK, 1), 0, NB)
    chosen = jnp.arange(NB, dtype=jnp.int32)[None, :] == full_slot
    return jnp.where(chosen, EB, counts).astype(jnp.int32)


def touch_ends(entries, own_key, smallest, high):
    longest = entries.shape.index(max(entries.shape))
    spots = []
    for shift in (0, 1):
        where = [jax.random.randint(jax.random.fold_in(own_key, axis), (), 0, length) for axis, length in enumerate(entries.shape)]
        where[longest] = (where[longest] + shift) % entries.shape[longest]
        spots.append(tuple(where))
    return entries.at[spots[0]].set(smallest).at[spots[1]].set(high)


def level_of(rng, extent, pieces, smallest, largest):
    gain, own = 1.0, jax.random.fold_in(rng, 6)
    for axis_at, blocks in pieces:
        steps = jnp.exp(jax.random.uniform(jax.random.fold_in(own, axis_at), (blocks,), jnp.float32, smallest / len(pieces), largest / len(pieces)))
        gain = gain * jnp.repeat(steps, extent[axis_at] // blocks).reshape([-1 if axis == axis_at else 1 for axis in range(len(extent))])
    return gain


def noise(rng, shape, spread, most, cuts=(), kind=jnp.bfloat16):
    result = spread * jax.random.normal(rng, shape, jnp.float32)
    if cuts:
        result = result * level_of(rng, shape, cuts, -0.22, 0.18)
    return jnp.clip(result, -most, most).astype(kind)


def setup_inputs(seed: int = 0, part: int = 0) -> dict:
    keys = jax.random.split(jax.random.key(seed), 22)
    part_splits = jax.random.split(jax.random.fold_in(keys[21], part), 22)
    return {
        "node_scalars": noise(part_splits[0], (ATOMS, C), 1.0, 6.0, ((0, 16),), jnp.float32),
        "node_vectors": noise(part_splits[1], (3, ATOMS, C), 1.0, 6.0, ((1, 16),), jnp.float32),
        "positions": jnp.clip(1.0 * jax.random.uniform(part_splits[2], (3, ATOMS), jnp.float32) ** level_of(part_splits[2], (3, ATOMS), ((1, 16),), -0.2, 0.2), 0.0, 1.0),
        "species": touch_ends(jax.random.randint(part_splits[3], (ATOMS,), 0, NSPEC), jax.random.fold_in(part_splits[3], 1), 0, NSPEC - 1).astype(jnp.int32),
        "edge_senders": touch_ends(jax.random.randint(part_splits[4], (N_BLK, NB, EB), 0, ATOM_DEV), jax.random.fold_in(part_splits[4], 1), 0, ATOM_DEV - 1).astype(jnp.int32),
        "edge_receivers": touch_ends(jax.random.randint(part_splits[5], (N_BLK, NB, EB), 0, ATOM_DEV), jax.random.fold_in(part_splits[5], 1), 0, ATOM_DEV - 1).astype(jnp.int32),
        "edge_shifts": touch_ends(jax.random.randint(part_splits[6], (N_BLK, NB, 3, EB), -1, 2), jax.random.fold_in(part_splits[6], 1), -1, 1).astype(jnp.int32),
        "bucket_counts": draw_bucket_counts(jax.random.fold_in(jax.random.fold_in(keys[21], part), 71), part),
        "w_up": noise(keys[8], (2, C, C), C ** -0.5, 0.5, (), jnp.float32),
        "w_rad_in": noise(keys[9], (NBASIS, RAD_HID), 2 ** -0.5, 4.0, (), jnp.float32),
        "w_rad_mid": noise(keys[10], (2, RAD_HID, RAD_HID), 16 ** -0.5, 1.5, (), jnp.float32),
        "w_rad_out": noise(keys[11], (RAD_HID, PATHS * C), 16 ** -0.5, 1.5, (), jnp.float32),
        "w_lin": noise(keys[12], (4, C, C), C ** -0.5, 0.5, (), jnp.float32),
        "w_sc_scalar": noise(keys[13], (NSPEC, 9, C), 0.1, 0.6, (), jnp.float32),
        "w_sc_vector": noise(keys[14], (NSPEC, 5, C), 0.3, 1.8, (), jnp.float32),
        "w_prod": noise(keys[15], (2, C, C), C ** -0.5, 0.5, (), jnp.float32),
        "w_skip": noise(keys[16], (2, NSPEC, C, C), C ** -0.5, 0.5, (), jnp.float32),
        "w_read": noise(keys[17], (C,), C ** -0.5, 0.5, (), jnp.float32),
        "cot_scalars": noise(part_splits[18], (ATOMS, C), 1.0, 6.0, ((0, 16),), jnp.float32),
        "cot_vectors": noise(part_splits[19], (3, ATOMS, C), 1.0, 6.0, ((1, 16),), jnp.float32),
        "cot_energy": noise(part_splits[20], (ATOMS,), 1.0, 6.0, ((0, 16),), jnp.float32),
    }


cutoff = 5.0
box_side = 1.0
soften_sq = 0.1
neigh_scale = 0.17677669529663687
precise = lax.Precision.HIGHEST

@jax.custom_vjp
def low(v):
    return lax.optimization_barrier(v.astype(jnp.bfloat16)).astype(jnp.float32)

@jax.custom_vjp
def low_back(v):
    return v

def low_keep(v):
    return (low(v), None)

def low_pass(kept, grad):
    return (grad,)

def back_keep(v):
    return (v, None)

def back_low(kept, grad):
    return (low(grad),)
low.defvjp(low_keep, low_pass)
low_back.defvjp(back_keep, back_low)

def harmonics(direction):
    coord_x, coord_y, coord_z = (direction[0], direction[1], direction[2])
    square_x = coord_x * coord_x
    square_y = coord_y * coord_y
    square_z = coord_z * coord_z
    planar = square_x + square_y
    return jnp.stack([jnp.ones_like(coord_x), math.sqrt(3.0) * coord_x, math.sqrt(3.0) * coord_y, math.sqrt(3.0) * coord_z, math.sqrt(15.0) * coord_x * coord_y, math.sqrt(15.0) * coord_y * coord_z, 0.5 * math.sqrt(5.0) * (2.0 * square_z - planar), math.sqrt(15.0) * coord_x * coord_z, 0.5 * math.sqrt(15.0) * (square_x - square_y), math.sqrt(35.0 / 8.0) * (3.0 * square_x - square_y) * coord_y, math.sqrt(105.0) * coord_x * coord_y * coord_z, math.sqrt(21.0 / 8.0) * coord_y * (4.0 * square_z - planar), 0.5 * math.sqrt(7.0) * coord_z * (2.0 * square_z - 3.0 * planar), math.sqrt(21.0 / 8.0) * coord_x * (4.0 * square_z - planar), 0.5 * math.sqrt(105.0) * coord_z * (square_x - square_y), math.sqrt(35.0 / 8.0) * (square_x - 3.0 * square_y) * coord_x])

def contract_first(weight, values):
    return lax.dot_general(weight, values, (((0,), (0,)), ((), ())), precision=precise)

def messages(gathered, sender_pos, receiver_pos, shift_rows, valid_mask, w_rad_in, w_rad_mid, w_rad_out):
    relative = sender_pos - receiver_pos + box_side * shift_rows.astype(jnp.float32)
    distance = jnp.sqrt(lax.optimization_barrier(jnp.sum(relative * relative, axis=0)) + soften_sq)
    direction = relative / distance[None, :]
    harmonic = harmonics(direction)
    orders = jnp.arange(1, w_rad_in.shape[0] + 1).astype(jnp.float32)[:, None]
    bessel = math.sqrt(2.0 / cutoff) * jnp.sin(orders * math.pi * distance[None, :] / cutoff) / distance[None, :]
    scaled = distance / cutoff
    scaled_six = scaled * scaled * scaled * scaled * scaled * scaled
    envelope = 1.0 - 28.0 * scaled_six + 48.0 * scaled_six * scaled - 21.0 * scaled_six * scaled * scaled
    hidden = jax.nn.silu(contract_first(w_rad_in, bessel))
    hidden = jax.nn.silu(contract_first(w_rad_mid[0], hidden))
    hidden = jax.nn.silu(contract_first(w_rad_mid[1], hidden))
    channels = gathered.shape[2]
    radial = contract_first(hidden, w_rad_out).reshape(-1, 7, channels)
    radial = radial * (envelope * valid_mask)[:, None, None]
    sender_scalars = gathered[0]
    sender_vectors = gathered[1:4]
    first_order = harmonic[1:4][:, :, None]
    inner_dot = lax.optimization_barrier(jnp.sum(first_order * sender_vectors, axis=0))
    cross_term = jnp.stack([first_order[1] * sender_vectors[2] - first_order[2] * sender_vectors[1], first_order[2] * sender_vectors[0] - first_order[0] * sender_vectors[2], first_order[0] * sender_vectors[1] - first_order[1] * sender_vectors[0]])
    order_zero = radial[:, 0] * sender_scalars + radial[:, 4] * inner_dot
    order_one = (radial[:, 1] * sender_scalars)[None] * first_order + radial[:, 5][None] * sender_vectors + radial[:, 6][None] * cross_term
    order_two = (radial[:, 2] * sender_scalars)[None] * harmonic[4:9][:, :, None]
    order_three = (radial[:, 3] * sender_scalars)[None] * harmonic[9:16][:, :, None]
    return jnp.concatenate([order_zero[None], order_one, order_two, order_three], axis=0)

def up_project(scalars, vectors, w_up):
    lifted_scalars = jnp.dot(scalars, w_up[0], precision=precise)
    lifted_vectors = jnp.einsum('mac,cd->mad', vectors, w_up[1], precision=precise)
    return jnp.concatenate([lifted_scalars[None], lifted_vectors], axis=0)

def node_update(amplitudes, scalars, vectors, species_table, w_lin, w_sc_scalar, w_sc_vector, w_prod, w_skip, w_read):
    linear_zero = jnp.dot(amplitudes[0], w_lin[0], precision=precise)
    linear_one = jnp.einsum('mac,cd->mad', amplitudes[1:4], w_lin[1], precision=precise)
    linear_two = jnp.einsum('mac,cd->mad', amplitudes[4:9], w_lin[2], precision=precise)
    linear_three = jnp.einsum('mac,cd->mad', amplitudes[9:16], w_lin[3], precision=precise)
    norm_one = lax.optimization_barrier(jnp.sum(linear_one * linear_one, axis=0))
    norm_two = lax.optimization_barrier(jnp.sum(linear_two * linear_two, axis=0))
    norm_three = lax.optimization_barrier(jnp.sum(linear_three * linear_three, axis=0))
    zero_square = linear_zero * linear_zero
    invariants = jnp.stack([linear_zero, zero_square, norm_one, norm_two, norm_three, zero_square * linear_zero, linear_zero * norm_one, linear_zero * norm_two, linear_zero * norm_three])
    scalar_weights = jnp.einsum('as,spc->pac', species_table, w_sc_scalar, precision=precise)
    mixed_scalars = lax.optimization_barrier(jnp.sum(scalar_weights * invariants, axis=0))
    factors = jnp.stack([jnp.ones_like(linear_zero), linear_zero, zero_square, norm_one, norm_two])
    vector_weights = jnp.einsum('as,spc->pac', species_table, w_sc_vector, precision=precise)
    mixed_vectors = linear_one * lax.optimization_barrier(jnp.sum(vector_weights * factors, axis=0))[None]
    skip_scalars = jnp.einsum('as,sad->ad', species_table, jnp.einsum('ac,scd->sad', scalars, w_skip[0], precision=precise), precision=precise)
    skip_vectors = jnp.einsum('as,smad->mad', species_table, jnp.einsum('mac,scd->smad', vectors, w_skip[1], precision=precise), precision=precise)
    new_scalars = jnp.dot(mixed_scalars, w_prod[0], precision=precise) + skip_scalars
    new_vectors = jnp.einsum('mac,cd->mad', mixed_vectors, w_prod[1], precision=precise) + skip_vectors
    energy = jnp.dot(new_scalars, w_read, precision=precise)
    return (new_scalars, new_vectors, energy)

def reference(node_scalars, node_vectors, positions, species, edge_senders, edge_receivers, edge_shifts, bucket_counts, w_up, w_rad_in, w_rad_mid, w_rad_out, w_lin, w_sc_scalar, w_sc_vector, w_prod, w_skip, w_read, cot_scalars, cot_vectors, cot_energy):
    species_table = (species[:, None] == jnp.arange(NSPEC, dtype=jnp.int32)[None, :]).astype(jnp.float32)
    block_index = jnp.arange(N_BLK, dtype=jnp.int32)
    offset_row = jnp.arange(NB, dtype=jnp.int32) - REACH
    slot_row = jnp.arange(EB, dtype=jnp.int32)

    def forward(scalars, vectors, up_weights, rad_in, rad_mid, rad_out, lin_weights, sc_scalar, sc_vector, prod_weights, skip_weights, read_weights):
        lifted = up_project(scalars, vectors, up_weights)

        def one_block(inputs):
            index, send_rows, recv_rows, shift_rows, filled = inputs
            shards = (index + offset_row) % N_BLK
            global_send = (shards[:, None] * ATOM_DEV + send_rows).reshape(-1)
            global_recv = (index * ATOM_DEV + recv_rows).reshape(-1)
            gathered = lifted[:, global_send, :]
            valid_mask = (slot_row[None, :] < filled[:, None]).astype(jnp.float32).reshape(-1)
            shift_flat = jnp.moveaxis(shift_rows, 1, 0).reshape(3, -1)
            message = messages(gathered, positions[:, global_send], positions[:, global_recv], shift_flat, valid_mask, rad_in, rad_mid, rad_out)
            summed = jax.ops.segment_sum(jnp.moveaxis(message, 1, 0), recv_rows.reshape(-1), num_segments=ATOM_DEV)
            return jnp.moveaxis(summed, 0, 1) * neigh_scale
        blocks = lax.map(jax.checkpoint(one_block), (block_index, edge_senders, edge_receivers, edge_shifts, bucket_counts))
        amplitudes = jnp.moveaxis(blocks, 0, 1).reshape(16, N_BLK * ATOM_DEV, C)
        return node_update(amplitudes, scalars, vectors, species_table, lin_weights, sc_scalar, sc_vector, prod_weights, skip_weights, read_weights)
    outputs, backward = jax.vjp(forward, node_scalars, node_vectors, w_up, w_rad_in, w_rad_mid, w_rad_out, w_lin, w_sc_scalar, w_sc_vector, w_prod, w_skip, w_read)
    gradients = backward((cot_scalars, cot_vectors, cot_energy))
    return (outputs[0], outputs[1], outputs[2], gradients[0], gradients[1], gradients[2][None], gradients[3][None], gradients[4][None], gradients[5][None], gradients[6][None], gradients[7][None], gradients[8][None], gradients[9][None], gradients[10][None], gradients[11][None])
```

```python
import functools
import math

import jax
import jax.numpy as jnp
from jax import lax
from jax.experimental import pallas as pl
from jax.experimental.pallas import tpu as pltpu
from jax.sharding import PartitionSpec as P

CUTOFF = 5.0
SOFTEN = 0.1
NEIGH = 0.17677669529663687
F32 = jnp.float32
BF16 = jnp.bfloat16
LANES = 128
VMEM = pl.BlockSpec(memory_space=pltpu.VMEM)
SMEM = pl.BlockSpec(memory_space=pltpu.SMEM)
LIMIT = 56 * 1024 * 1024

NN = (((1,), (0,)), ((), ()))
NT = (((1,), (1,)), ((), ()))


def split(v):
    high = v.astype(BF16)
    return high, (v - high.astype(F32)).astype(BF16)


def dot(a, b, dims=NN):
    return lax.dot_general(a, b, dims, preferred_element_type=F32)


def dot3(a, b, dims=NN):
    ah, al = a if isinstance(a, tuple) else split(a)
    bh, bl = b if isinstance(b, tuple) else split(b)
    return dot(ah, bh, dims) + (dot(ah, bl, dims) + dot(al, bh, dims))


def cat3(v, axis):
    high, low = split(v)
    return jnp.concatenate([high, high, low], axis=axis)


def wcat3(v, axis):
    high, low = split(v)
    return jnp.concatenate([high, low, high], axis=axis)


def column(row, width):
    return jnp.broadcast_to(row, (width, row.shape[1])).T


ROW_Y = 8
ROW_ENV = 24
GEO_ROWS = 25


def write_geometry(geo, counts, send, recv, shift, tables, own_pos):
    buckets, slots = send.shape
    bucket_of = lax.broadcasted_iota(jnp.int32, (buckets, LANES), 0)
    filled = jnp.zeros((buckets, LANES), jnp.int32)
    for k in range(buckets):
        filled = jnp.where(bucket_of == k, counts[0, k], filled)
    own = [jnp.broadcast_to(own_pos[a : a + 1, :], (buckets, LANES)) for a in range(3)]
    lane = lax.broadcasted_iota(jnp.int32, (buckets, LANES), 1)
    for block in range(slots // LANES):
        cols = slice(block * LANES, (block + 1) * LANES)
        from_idx, to_idx = send[:, cols], recv[:, cols]
        rel = []
        for a in range(3):
            there = jnp.take_along_axis(tables[a], from_idx, axis=1, mode="promise_in_bounds")
            here = jnp.take_along_axis(own[a], to_idx, axis=1, mode="promise_in_bounds")
            rel.append(there - here + shift[:, a, cols].astype(F32))
        dist = jnp.sqrt(rel[0] * rel[0] + rel[1] * rel[1] + rel[2] * rel[2] + SOFTEN)
        inverse = 1.0 / dist
        x, y, z = (r * inverse for r in rel)
        angle = dist * (math.pi / CUTOFF)
        sine, twice = jnp.sin(angle), 2.0 * jnp.cos(angle)
        scale = math.sqrt(2.0 / CUTOFF) * inverse
        before, now = jnp.zeros_like(sine), sine
        for n in range(8):
            geo[n, :, cols] = now * scale
            before, now = now, twice * now - before
        xx, yy, zz = x * x, y * y, z * z
        planar = xx + yy
        rows = [
            jnp.ones_like(x),
            math.sqrt(3.0) * x,
            math.sqrt(3.0) * y,
            math.sqrt(3.0) * z,
            math.sqrt(15.0) * x * y,
            math.sqrt(15.0) * y * z,
            0.5 * math.sqrt(5.0) * (2.0 * zz - planar),
            math.sqrt(15.0) * x * z,
            0.5 * math.sqrt(15.0) * (xx - yy),
            math.sqrt(35.0 / 8.0) * (3.0 * xx - yy) * y,
            math.sqrt(105.0) * x * y * z,
            math.sqrt(21.0 / 8.0) * y * (4.0 * zz - planar),
            0.5 * math.sqrt(7.0) * z * (2.0 * zz - 3.0 * planar),
            math.sqrt(21.0 / 8.0) * x * (4.0 * zz - planar),
            0.5 * math.sqrt(105.0) * z * (xx - yy),
            math.sqrt(35.0 / 8.0) * (xx - 3.0 * yy) * x,
        ]
        for m, row in enumerate(rows):
            geo[ROW_Y + m, :, cols] = row
        q = dist * (1.0 / CUTOFF)
        q6 = q * q * q * q * q * q
        envelope = 1.0 - 28.0 * q6 + 48.0 * q6 * q - 21.0 * q6 * q * q
        geo[ROW_ENV, :, cols] = jnp.where(lane + block * LANES < filled, envelope, 0.0)


def one_hot(index_row, atoms):
    edges = index_row.shape[1]
    atom = lax.broadcasted_iota(jnp.int32, (atoms, edges), 0)
    return jnp.where(atom == index_row, 1.0, 0.0).astype(BF16)


def silu_parts(v):
    gate = 1.0 / (1.0 + jnp.exp(-v))
    return v * gate, gate


def lift(x_ref, w_up_t, out):
    atoms, channels = x_ref.shape[1], x_ref.shape[2]
    for comp in range(4):
        lifted = dot3(w_up_t[min(comp, 1)], x_ref[comp], NT)
        high, low = split(lifted)
        rows = slice(comp * channels, (comp + 1) * channels)
        out[rows, :atoms] = high
        out[rows, atoms:] = low


def forward_messages(feats, radial, geo_rows, out, channels, edges):
    for half in range(edges // LANES):
        cols = slice(half * LANES, (half + 1) * LANES)
        low_cols = slice(edges + half * LANES, edges + (half + 1) * LANES)
        y = [jnp.broadcast_to(row[:, cols], (16, LANES)) for row in geo_rows]
        for c in range(0, channels, 16):
            def feat(k):
                return feats[k * channels + c : k * channels + c + 16, cols]

            def rad(k):
                return radial[k * channels + c : k * channels + c + 16, cols]

            def put(comp, value):
                high, low = split(value)
                rows = slice(comp * channels + c, comp * channels + c + 16)
                out[rows, cols] = high
                out[rows, low_cols] = low

            s, v = feat(0), [feat(1), feat(2), feat(3)]
            inner = y[1] * v[0] + y[2] * v[1] + y[3] * v[2]
            put(0, rad(0) * s + rad(4) * inner)
            first, fifth, sixth = rad(1) * s, rad(5), rad(6)
            put(1, first * y[1] + fifth * v[0] + sixth * (y[2] * v[2] - y[3] * v[1]))
            put(2, first * y[2] + fifth * v[1] + sixth * (y[3] * v[0] - y[1] * v[2]))
            put(3, first * y[3] + fifth * v[2] + sixth * (y[1] * v[1] - y[2] * v[0]))
            second = rad(2) * s
            for m in range(4, 9):
                put(m, second * y[m])
            third = rad(3) * s
            for m in range(9, 16):
                put(m, third * y[m])


def edge_forward(
    n_slabs, slot_of, chunk, counts, send, recv, shift, own_pos, tables,
    x_refs, w_up, w_in, w_mid, w_out, lifted_out, hidden_out, geo, acc, feats, radial, messages,
):
    slots = send.shape[1]
    atoms, channels = x_refs[0].shape[1], x_refs[0].shape[2]
    hid = w_in.shape[1]
    write_geometry(geo, counts, send, recv, shift, tables, own_pos)
    w_up_t = [split(w_up[0].T), split(w_up[1].T)]
    for p in range(n_slabs):
        lift(x_refs[p], w_up_t, lifted_out.at[p])
    w_in_t = wcat3(w_in[...].T, 1)
    w_mid_t = [wcat3(w_mid[0].T, 1), wcat3(w_mid[1].T, 1)]
    w_out_t = wcat3(w_out[...].T, 1)

    def per_bucket(p, carry):
        k = slot_of(p)
        filled = counts[0, k]

        def per_chunk(j, carry):
            at = pl.multiple_of(j * chunk, chunk)
            cols = pl.ds(at, chunk)
            bessel = jnp.concatenate([geo[n, pl.ds(k, 1), cols] for n in range(8)], axis=0)
            b_high = bessel.astype(BF16).astype(F32)
            stacked = jnp.concatenate([b_high, b_high, bessel - b_high], axis=0).astype(BF16)
            h, _ = silu_parts(dot(w_in_t, stacked))
            h, _ = silu_parts(dot(w_mid_t[0], cat3(h, 0)))
            h, _ = silu_parts(dot(w_mid_t[1], cat3(h, 0)))
            h_high, h_low = split(h * geo[ROW_ENV, pl.ds(k, 1), cols])
            hidden_out[p, :hid, cols] = h_high
            hidden_out[p, hid:, cols] = h_low
            radial[...] = dot(w_out_t, jnp.concatenate([h_high, h_high, h_low], axis=0))
            from_hot = one_hot(send[pl.ds(k, 1), cols], atoms)
            feats[...] = dot(lifted_out[p], jnp.concatenate([from_hot, from_hot], axis=0))
            rows = [geo[ROW_Y + m, pl.ds(k, 1), cols] for m in range(16)]
            forward_messages(feats, radial, rows, messages, channels, chunk)
            to_hot = one_hot(recv[pl.ds(k, 1), cols], atoms)
            acc[...] += dot(messages[...], jnp.concatenate([to_hot, to_hot], axis=1), NT)
            return carry

        return lax.fori_loop(0, (filled + chunk - 1) // chunk, per_chunk, carry)

    lax.fori_loop(0, n_slabs, per_bucket, 0)


def own_forward_kernel(
    reach, chunk, counts, send, recv, shift, own_pos, x_own, w_up, w_in, w_mid, w_out,
    acc, lifted_out, hidden_out, geo, feats, radial, messages,
):
    acc[...] = jnp.zeros_like(acc)
    buckets = send.shape[0]
    tables = [jnp.broadcast_to(own_pos[a : a + 1, :], (buckets, LANES)) for a in range(3)]
    edge_forward(
        1, lambda p: reach, chunk, counts, send, recv, shift, own_pos, tables, [x_own],
        w_up, w_in, w_mid, w_out, lifted_out, hidden_out, geo, acc, feats, radial, messages,
    )


def rest_forward_kernel(reach, chunk, *refs):
    n = 2 * reach
    counts, send, recv, shift, own_pos, acc_in = refs[:6]
    pos_refs, x_refs = refs[6 : 6 + n], refs[6 + n : 6 + 2 * n]
    (w_up, w_in, w_mid, w_out, species, w_lin, w_sc_s, w_sc_v, w_prod, w_read, g_total, cot_v,
     skip_s, skip_v) = refs[6 + 2 * n : 20 + 2 * n]
    (new_s, new_v, energy, grad_amp, g_lin, g_sc_s, g_sc_v, g_prod, g_read, lifted_out,
     hidden_out, geo) = refs[20 + 2 * n : 32 + 2 * n]
    acc, feats, radial, messages = refs[32 + 2 * n :]
    tables = []
    for a in range(3):
        rows = [ref[a : a + 1, :] for ref in pos_refs]
        tables.append(jnp.concatenate(rows[:reach] + [own_pos[a : a + 1, :]] + rows[reach:], axis=0))
    acc[...] = acc_in[...]
    edge_forward(
        n, lambda p: jnp.where(p >= reach, p + 1, p), chunk, counts, send, recv, shift, own_pos,
        tables, x_refs, w_up, w_in, w_mid, w_out, lifted_out, hidden_out, geo, acc, feats, radial,
        messages,
    )
    node_stage(
        acc, species, w_lin, w_sc_s, w_sc_v, w_prod, w_read, g_total, cot_v, skip_s, skip_v,
        new_s, new_v, energy, grad_amp, g_lin, g_sc_s, g_sc_v, g_prod, g_read,
    )


DEGREE = (0, 1, 1, 1, 2, 2, 2, 2, 2, 3, 3, 3, 3, 3, 3, 3)


def species_hot(species_row, count):
    atoms = species_row.shape[1]
    which = lax.broadcasted_iota(jnp.int32, (count, atoms), 0)
    return jnp.where(which == species_row, 1.0, 0.0)


def node_stage(
    acc, species, w_lin, w_sc_s, w_sc_v, w_prod, w_read, g_total, cot_v, skip_s, skip_v,
    new_s, new_v, energy, grad_amp, g_lin, g_sc_s, g_sc_v, g_prod, g_read,
):
    channels, atoms = w_lin.shape[1], acc.shape[1]
    n_spec = w_sc_s.shape[0]
    w_lin_parts = [split(w_lin[l]) for l in range(4)]
    amp_t = [acc[m * channels : (m + 1) * channels, :] * NEIGH for m in range(16)]
    amp_t_parts = [split(v) for v in amp_t]
    b = [
        dot3((h.T, l.T), w_lin_parts[DEGREE[m]])
        for m, (h, l) in enumerate(amp_t_parts)
    ]
    b0 = b[0]
    n1 = b[1] * b[1] + b[2] * b[2] + b[3] * b[3]
    n2 = b[4] * b[4] + b[5] * b[5] + b[6] * b[6] + b[7] * b[7] + b[8] * b[8]
    n3 = functools.reduce(jnp.add, [b[m] * b[m] for m in range(9, 16)])
    species_col = column(species[...].astype(F32), channels)
    masks = [species_col == float(s) for s in range(n_spec)]

    def per_atom(w, p):
        value = jnp.broadcast_to(w[0, p : p + 1, :], (atoms, channels))
        for s in range(1, n_spec):
            value = jnp.where(masks[s], w[s, p : p + 1, :], value)
        return value

    ws = [per_atom(w_sc_s, p) for p in range(9)]
    wv = [per_atom(w_sc_v, p) for p in range(5)]
    sq = b0 * b0
    terms = [b0, sq, n1, n2, n3, sq * b0, b0 * n1, b0 * n2, b0 * n3]
    mixed = functools.reduce(jnp.add, [w * t for w, t in zip(ws, terms)])
    factors = [None, b0, sq, n1, n2]
    factor = wv[0]
    for p in range(1, 5):
        factor = factor + wv[p] * factors[p]
    prod_parts = [split(w_prod[0]), split(w_prod[1])]
    out_s = dot3(mixed, prod_parts[0]) + skip_s[...]
    new_s[...] = out_s
    mixed_v = [b[1 + a] * factor for a in range(3)]
    for a in range(3):
        new_v[a] = dot3(mixed_v[a], prod_parts[1]) + skip_v[a]
    read_row = w_read[...]
    energy[...] = dot3(jnp.broadcast_to(read_row, (8, channels)), out_s, NT)[:1]
    cot_e = g_total[1]
    g_read[...] = jnp.sum(out_s * cot_e, axis=0, keepdims=True)

    g_s = split(g_total[0])
    g_v = [split(cot_v[a]) for a in range(3)]
    g_prod[0] = dot3(mixed.T, g_s)
    g_prod[1] = functools.reduce(jnp.add, [dot3(mixed_v[a].T, g_v[a]) for a in range(3)])
    g_mixed = dot3(g_s, prod_parts[0], NT)
    g_mixed_v = [dot3(g_v[a], prod_parts[1], NT) for a in range(3)]
    g_factor = functools.reduce(jnp.add, [g_mixed_v[a] * b[1 + a] for a in range(3)])

    hot = species_hot(species[...], 8).astype(BF16)

    def by_species(value):
        high, low = split(value)
        return dot(hot, high) + dot(hot, low)

    for p in range(9):
        g_sc_s[:, p, :] = by_species(g_mixed * terms[p])[:n_spec]
    g_sc_v[:, 0, :] = by_species(g_factor)[:n_spec]
    for p in range(1, 5):
        g_sc_v[:, p, :] = by_species(g_factor * factors[p])[:n_spec]

    g_b0 = g_mixed * (
        ws[0] + 2.0 * b0 * ws[1] + 3.0 * sq * ws[5] + n1 * ws[6] + n2 * ws[7] + n3 * ws[8]
    ) + g_factor * (wv[1] + 2.0 * b0 * wv[2])
    g_n1 = 2.0 * (g_mixed * (ws[2] + b0 * ws[6]) + g_factor * wv[3])
    g_n2 = 2.0 * (g_mixed * (ws[3] + b0 * ws[7]) + g_factor * wv[4])
    g_n3 = 2.0 * (g_mixed * (ws[4] + b0 * ws[8]))
    g_b = [g_b0]
    for a in range(3):
        g_b.append(g_mixed_v[a] * factor + g_n1 * b[1 + a])
    for m in range(4, 9):
        g_b.append(g_n2 * b[m])
    for m in range(9, 16):
        g_b.append(g_n3 * b[m])
    g_b_parts = [split(v) for v in g_b]
    for l in range(4):
        members = [m for m in range(16) if DEGREE[m] == l]
        g_lin[l] = functools.reduce(
            jnp.add, [dot3(amp_t_parts[m], g_b_parts[m]) for m in members]
        )
    for m in range(16):
        high, low = split(dot3(w_lin_parts[DEGREE[m]], g_b_parts[m], NT) * NEIGH)
        rows = slice(m * channels, (m + 1) * channels)
        grad_amp[rows, :atoms] = high
        grad_amp[rows, atoms:] = low


def skip_kernel(
    x_own, cot_s, cot_v, cot_e, species, w_skip, w_read,
    g_total, skip_s, skip_v, skip_gs, skip_gv, g_skip,
):
    atoms, channels = cot_s.shape
    n_spec = w_skip.shape[1]
    cot_col = column(cot_e[...], channels)
    total = cot_s[...] + cot_col * w_read[...]
    g_total[0] = total
    g_total[1] = cot_col
    species_col = column(species[...].astype(F32), channels)
    masks = [species_col == float(s) for s in range(n_spec)]

    def pick(values):
        result = values[0]
        for s in range(1, n_spec):
            result = jnp.where(masks[s], values[s], result)
        return result

    for kind in range(2):
        weights = [split(w_skip[kind, s]) for s in range(n_spec)]
        if kind == 0:
            xs, gs = [x_own[0]], [total]
            outs, grads = [(skip_s, None)], [(skip_gs, None)]
        else:
            xs, gs = [x_own[1 + a] for a in range(3)], [cot_v[a] for a in range(3)]
            outs, grads = [(skip_v, a) for a in range(3)], [(skip_gv, a) for a in range(3)]
        sums = [None] * n_spec
        for x, g, (out, at), (grad, _) in zip(xs, gs, outs, grads):
            x_parts, g_parts = split(x), split(g)
            forward = pick([dot3(x_parts, w) for w in weights])
            back = pick([dot3(g_parts, w, NT) for w in weights])
            if at is None:
                out[...] = forward
                grad[...] = back
            else:
                out[at] = forward
                grad[at] = back
            x_t = split(x.T)
            for s in range(n_spec):
                part = dot3(x_t, split(jnp.where(masks[s], g, 0.0)))
                sums[s] = part if sums[s] is None else sums[s] + part
        for s in range(n_spec):
            g_skip[kind, s] = sums[s]


def backward_messages(feats, radial, grads, geo_rows, g_radial, g_feats, channels, edges):
    for half in range(edges // LANES):
        cols = slice(half * LANES, (half + 1) * LANES)
        low_cols = slice(edges + half * LANES, edges + (half + 1) * LANES)
        y = [jnp.broadcast_to(row[:, cols], (16, LANES)) for row in geo_rows]
        for c in range(0, channels, 16):
            def load(ref, k):
                return ref[k * channels + c : k * channels + c + 16, cols]

            def put(ref, comp, value):
                high, low = split(value)
                rows = slice(comp * channels + c, comp * channels + c + 16)
                ref[rows, cols] = high
                ref[rows, low_cols] = low

            s = load(feats, 0)
            third = y[9] * load(grads, 9)
            for m in range(10, 16):
                third = third + y[m] * load(grads, m)
            put(g_radial, 3, s * third)
            second = y[4] * load(grads, 4)
            for m in range(5, 9):
                second = second + y[m] * load(grads, m)
            put(g_radial, 2, s * second)
            g = [load(grads, 1 + a) for a in range(3)]
            first = y[1] * g[0] + y[2] * g[1] + y[3] * g[2]
            put(g_radial, 1, s * first)
            zero = load(grads, 0)
            put(g_radial, 0, s * zero)
            put(
                g_feats, 0,
                load(radial, 0) * zero + load(radial, 1) * first
                + load(radial, 2) * second + load(radial, 3) * third,
            )
            v = [load(feats, 1 + a) for a in range(3)]
            put(g_radial, 4, (y[1] * v[0] + y[2] * v[1] + y[3] * v[2]) * zero)
            put(g_radial, 5, v[0] * g[0] + v[1] * g[1] + v[2] * g[2])
            cross = [
                g[1] * y[3] - g[2] * y[2],
                g[2] * y[1] - g[0] * y[3],
                g[0] * y[2] - g[1] * y[1],
            ]
            put(g_radial, 6, v[0] * cross[0] + v[1] * cross[1] + v[2] * cross[2])
            fourth, fifth, sixth = load(radial, 4) * zero, load(radial, 5), load(radial, 6)
            for a in range(3):
                put(g_feats, 1 + a, fourth * y[1 + a] + fifth * g[a] + sixth * cross[a])


def backward_kernel(n_slabs, slot_of, chunk, *refs):
    counts, send, recv, geo, grad_amp, lifted, hidden = refs[:7]
    x_refs = refs[7 : 7 + n_slabs]
    w_up, w_out = refs[7 + n_slabs : 9 + n_slabs]
    g_hidden, g_w_out_t, g_w_up_t = refs[9 + n_slabs : 12 + n_slabs]
    x_grads = refs[12 + n_slabs : 12 + 2 * n_slabs]
    feats, radial, grads, g_radial, g_feats, g_lifted = refs[12 + 2 * n_slabs :]
    atoms, channels = x_refs[0].shape[1], x_refs[0].shape[2]
    hid = w_out.shape[0]
    w_out_t = wcat3(w_out[...].T, 1)
    w_high, w_low = split(w_out[...])
    w_both = jnp.concatenate([w_high, w_low], axis=0)
    g_w_out_t[...] = jnp.zeros_like(g_w_out_t)
    g_lifted[...] = jnp.zeros_like(g_lifted)

    def per_bucket(p, carry):
        k = slot_of(p)
        filled = counts[0, k]

        def per_chunk(j, carry):
            at = pl.multiple_of(j * chunk, chunk)
            cols = pl.ds(at, chunk)
            h_high, h_low = hidden[p, :hid, cols], hidden[p, hid:, cols]
            radial[...] = dot(w_out_t, jnp.concatenate([h_high, h_high, h_low], axis=0))
            from_hot = one_hot(send[pl.ds(k, 1), cols], atoms)
            feats[...] = dot(lifted[p], jnp.concatenate([from_hot, from_hot], axis=0))
            to_hot = one_hot(recv[pl.ds(k, 1), cols], atoms)
            grads[...] = dot(grad_amp[...], jnp.concatenate([to_hot, to_hot], axis=0))
            rows = [geo[ROW_Y + m, pl.ds(k, 1), cols] for m in range(16)]
            backward_messages(feats, radial, grads, rows, g_radial, g_feats, channels, chunk)
            both = dot(w_both, g_radial[:, :chunk])
            g_hidden[p, :, cols] = (
                both[:hid] + both[hid:] + dot(w_high, g_radial[:, chunk:])
            ) * geo[ROW_ENV, pl.ds(k, 1), cols]
            stacked = jnp.concatenate(
                [
                    jnp.concatenate([h_high, h_high], axis=1),
                    jnp.concatenate([h_low, jnp.zeros_like(h_low)], axis=1),
                ],
                axis=0,
            )
            g_w_out_t[...] += dot(g_radial[...], stacked, NT)
            g_lifted[p] += dot(g_feats[...], jnp.concatenate([from_hot, from_hot], axis=1), NT)
            return carry

        return lax.fori_loop(0, (filled + chunk - 1) // chunk, per_chunk, carry)

    lax.fori_loop(0, n_slabs, per_bucket, 0)
    w_up_parts = [split(w_up[0]), split(w_up[1])]
    sums = [None, None]
    for p in range(n_slabs):
        for comp in range(4):
            kind = min(comp, 1)
            value = g_lifted[p, comp * channels : (comp + 1) * channels, :]
            high, low = split(value)
            x_grads[p][comp] = dot3((high.T, low.T), w_up_parts[kind], NT)
            part = dot3((high, low), x_refs[p][comp])
            sums[kind] = part if sums[kind] is None else sums[kind] + part
    g_w_up_t[0] = sums[0]
    g_w_up_t[1] = sums[1]


def mlp_backward_kernel(reach, chunk, counts, geo, gh_own, gh_rest, w_in, w_mid, g_in, g_mid,
                        acc_in, acc_mid):
    hid = w_in.shape[1]
    n_basis = w_in.shape[0]
    w_in_t = wcat3(w_in[...].T, 1)
    w_mid_t = [wcat3(w_mid[0].T, 1), wcat3(w_mid[1].T, 1)]
    w_mid_n = [wcat3(w_mid[0], 1), wcat3(w_mid[1], 1)]
    acc_in[...] = jnp.zeros_like(acc_in)
    acc_mid[...] = jnp.zeros_like(acc_mid)

    def stack(v):
        high, low = split(v)
        return jnp.concatenate([high, low], axis=0)

    def bucket(k, grad_of):
        def per_chunk(j, carry):
            at = pl.multiple_of(j * chunk, chunk)
            cols = pl.ds(at, chunk)
            bessel = jnp.concatenate([geo[n, pl.ds(k, 1), cols] for n in range(8)], axis=0)
            b_high = bessel.astype(BF16).astype(F32)
            b_low = bessel - b_high
            stacked = jnp.concatenate([b_high, b_high, b_low], axis=0).astype(BF16)
            z1 = dot(w_in_t, stacked)
            h1, s1 = silu_parts(z1)
            h2, s2 = silu_parts(dot(w_mid_t[0], cat3(h1, 0)))
            h3, s3 = silu_parts(dot(w_mid_t[1], cat3(h2, 0)))
            d3 = grad_of(cols) * (s3 + h3 * (1.0 - s3))
            acc_mid[1] += dot(stack(h2), stack(d3), NT)
            d2 = dot(w_mid_n[1], cat3(d3, 0)) * (s2 + h2 * (1.0 - s2))
            acc_mid[0] += dot(stack(h1), stack(d2), NT)
            d1 = dot(w_mid_n[0], cat3(d2, 0)) * (s1 + h1 * (1.0 - s1))
            basis = jnp.concatenate([b_high, b_low], axis=0).astype(BF16)
            acc_in[...] += dot(basis, stack(d1), NT)
            return carry

        lax.fori_loop(0, (counts[0, k] + chunk - 1) // chunk, per_chunk, 0)

    bucket(reach, lambda cols: gh_own[0, :, cols])

    def per_bucket(p, carry):
        bucket(jnp.where(p >= reach, p + 1, p), lambda cols: gh_rest[p, :, cols])
        return carry

    lax.fori_loop(0, 2 * reach, per_bucket, 0)

    def quadrants(v, rows):
        return v[:rows, :hid] + v[:rows, hid:] + v[rows:, :hid]

    g_in[...] = quadrants(acc_in[...], n_basis)
    for layer in range(2):
        g_mid[layer] = quadrants(acc_mid[layer], hid)


def call(kernel, out_shape, in_specs, scratch, args, name):
    return pl.pallas_call(
        kernel,
        out_shape=out_shape,
        in_specs=in_specs,
        out_specs=jax.tree.map(lambda _: VMEM, out_shape),
        scratch_shapes=scratch,
        compiler_params=pltpu.CompilerParams(vmem_limit_bytes=LIMIT),
        name=name,
    )(*args)


def shape(*dims, dtype=F32):
    return jax.ShapeDtypeStruct(dims, dtype)


def shifted(value, steps):
    count = lax.axis_size("blk")
    return lax.ppermute(value, "blk", [(i, (i + steps) % count) for i in range(count)])


def total_over_blocks(flat):
    count = lax.axis_size("blk")
    me = lax.axis_index("blk")
    steps, stride = [], 1
    while stride < count:
        radix = 4 if (count // stride) % 4 == 0 else 2
        steps.append((radix, stride))
        stride *= radix

    def partner(k, stride):
        return [(i, i ^ (k * stride)) for i in range(count)]

    value = flat
    for radix, stride in steps:
        digit = (me // stride) % radix
        parts = value.reshape(radix, -1, LANES)
        kept = lax.dynamic_index_in_dim(parts, digit, 0, keepdims=False)
        for k in range(1, radix):
            sent = lax.dynamic_index_in_dim(parts, digit ^ k, 0, keepdims=False)
            kept = kept + lax.ppermute(sent, "blk", partner(k, stride))
        value = kept
    for radix, stride in reversed(steps):
        digit = (me // stride) % radix
        whole = jnp.zeros((radix,) + value.shape, F32)
        whole = lax.dynamic_update_index_in_dim(whole, value, digit, 0)
        for k in range(1, radix):
            got = lax.ppermute(value, "blk", partner(k, stride))
            whole = lax.dynamic_update_index_in_dim(whole, got, digit ^ k, 0)
        value = whole.reshape(-1, LANES)
    return value


def per_device(
    node_scalars, node_vectors, positions, species, edge_senders, edge_receivers, edge_shifts,
    bucket_counts, w_up, w_rad_in, w_rad_mid, w_rad_out, w_lin, w_sc_scalar, w_sc_vector, w_prod,
    w_skip, w_read, cot_scalars, cot_vectors, cot_energy,
):
    send, recv, shift = edge_senders[0], edge_receivers[0], edge_shifts[0]
    buckets, slots = send.shape
    reach = (buckets - 1) // 2
    atoms, channels = node_scalars.shape
    hid, outs = w_rad_out.shape
    n_basis = w_rad_in.shape[0]
    n_spec = w_skip.shape[1]
    chunk = min(256, slots)
    n = 2 * reach
    x_own = jnp.concatenate([node_scalars[None], node_vectors], axis=0)
    packed = jnp.concatenate(
        [x_own.reshape(4 * atoms, channels), positions, jnp.zeros((5, atoms), F32)], axis=0
    )
    offsets = [d for d in range(-reach, reach + 1) if d]
    order = sorted(offsets, key=abs)
    arrived = {d: shifted(packed, -d) for d in order}
    x_rest = [arrived[d][: 4 * atoms].reshape(4, atoms, channels) for d in offsets]
    pos_rest = [arrived[d][4 * atoms : 4 * atoms + 3] for d in offsets]
    species_row = species.reshape(1, atoms)
    read_row = w_read.reshape(1, channels)

    g_total, skip_s, skip_v, skip_gs, skip_gv, g_skip = call(
        skip_kernel,
        (shape(2, atoms, channels), shape(atoms, channels), shape(3, atoms, channels),
         shape(atoms, channels), shape(3, atoms, channels), shape(2, n_spec, channels, channels)),
        [VMEM] * 7, [],
        (x_own, cot_scalars, cot_vectors, cot_energy.reshape(1, atoms), species_row, w_skip,
         read_row),
        "self_connection",
    )

    geo_shape = (GEO_ROWS, buckets, slots)
    work = [
        pltpu.VMEM((4 * channels, chunk), F32),
        pltpu.VMEM((outs, chunk), F32),
        pltpu.VMEM((16 * channels, 2 * chunk), BF16),
    ]
    acc_own, lifted_own, hidden_own = call(
        functools.partial(own_forward_kernel, reach, chunk),
        (shape(16 * channels, atoms), shape(1, 4 * channels, 2 * atoms, dtype=BF16),
         shape(1, 2 * hid, slots, dtype=BF16)),
        [SMEM] + [VMEM] * 9,
        [pltpu.VMEM(geo_shape, F32)] + work,
        (bucket_counts, send, recv, shift, positions, x_own, w_up, w_rad_in, w_rad_mid, w_rad_out),
        "edges_own",
    )
    (new_s, new_v, energy, grad_amp, g_lin, g_sc_s, g_sc_v, g_prod, g_read, lifted_rest,
     hidden_rest, geo) = call(
        functools.partial(rest_forward_kernel, reach, chunk),
        (shape(atoms, channels), shape(3, atoms, channels), shape(1, atoms),
         shape(16 * channels, 2 * atoms, dtype=BF16), shape(4, channels, channels),
         shape(*w_sc_scalar.shape), shape(*w_sc_vector.shape), shape(2, channels, channels),
         shape(1, channels), shape(n, 4 * channels, 2 * atoms, dtype=BF16),
         shape(n, 2 * hid, slots, dtype=BF16), shape(*geo_shape)),
        [SMEM] + [VMEM] * (19 + 2 * n),
        [pltpu.VMEM((16 * channels, atoms), F32)] + work,
        (bucket_counts, send, recv, shift, positions, acc_own, *pos_rest, *x_rest, w_up, w_rad_in,
         w_rad_mid, w_rad_out, species_row, w_lin, w_sc_scalar, w_sc_vector, w_prod, read_row,
         g_total, cot_vectors, skip_s, skip_v),
        "edges_rest_and_nodes",
    )

    back_work = [
        pltpu.VMEM((4 * channels, chunk), F32),
        pltpu.VMEM((outs, chunk), F32),
        pltpu.VMEM((16 * channels, chunk), F32),
        pltpu.VMEM((outs, 2 * chunk), BF16),
        pltpu.VMEM((4 * channels, 2 * chunk), BF16),
    ]

    def backward(count, slot_of, lifted, hidden, xs, name):
        result = call(
            functools.partial(backward_kernel, count, slot_of, chunk),
            (shape(count, hid, slots), shape(outs, 2 * hid), shape(2, channels, channels))
            + tuple(shape(4, atoms, channels) for _ in range(count)),
            [SMEM] + [VMEM] * (8 + count),
            back_work + [pltpu.VMEM((count, 4 * channels, atoms), F32)],
            (bucket_counts, send, recv, geo, grad_amp, lifted, hidden, *xs, w_up, w_rad_out),
            name,
        )
        return result[0], result[1], result[2], result[3:]

    gh_rest, gwo_rest, gwu_rest, gx_rest = backward(
        n, lambda p: jnp.where(p >= reach, p + 1, p), lifted_rest, hidden_rest, x_rest,
        "edges_rest_back",
    )
    home = [shifted(gx_rest[offsets.index(d)], d) for d in order]
    gh_own, gwo_own, gwu_own, gx_own = backward(
        1, lambda p: reach, lifted_own, hidden_own, [x_own], "edges_own_back"
    )
    g_in, g_mid = call(
        functools.partial(mlp_backward_kernel, reach, chunk),
        (shape(n_basis, hid), shape(2, hid, hid)),
        [SMEM] + [VMEM] * 5,
        [pltpu.VMEM((2 * n_basis, 2 * hid), F32), pltpu.VMEM((2, 2 * hid, 2 * hid), F32)],
        (bucket_counts, geo, gh_own, gh_rest, w_rad_in, w_rad_mid),
        "radial_back",
    )
    gx = gx_own[0]
    for part in home:
        gx = gx + part
    grad_scalars = gx[0] + skip_gs
    grad_vectors = gx[1:] + skip_gv

    gwo = gwo_rest + gwo_own
    g_out = (gwo[:, :hid] + gwo[:, hid:]).T
    g_up = jnp.swapaxes(gwu_rest + gwu_own, 1, 2)
    pieces = [g_up, g_in, g_mid, g_out, g_lin, g_sc_s, g_sc_v, g_prod, g_skip, g_read.reshape(-1)]
    flat = jnp.concatenate([p.reshape(-1, LANES) for p in pieces], axis=0)
    unit = 8 * lax.axis_size("blk")
    extra = -flat.shape[0] % unit
    flat = total_over_blocks(jnp.pad(flat, ((0, extra), (0, 0))))
    totals, at = [], 0
    for p in pieces:
        rows = p.size // LANES
        totals.append(flat[at : at + rows].reshape((1,) + p.shape))
        at += rows
    return (new_s, new_v, energy.reshape(-1), grad_scalars, grad_vectors, *totals)


def solution(mesh):
    atoms = ("cell", "blk")
    in_specs = (
        P(atoms, None), P(None, atoms, None), P(None, atoms), P(atoms), P(atoms, None, None),
        P(atoms, None, None), P(atoms, None, None, None), P(atoms, None),
        P(), P(), P(), P(), P(), P(), P(), P(), P(), P(),
        P(atoms, None), P(None, atoms, None), P(atoms),
    )
    out_specs = (
        P(atoms, None), P(None, atoms, None), P(atoms), P(atoms, None), P(None, atoms, None),
        P("cell", None, None, None), P("cell", None, None), P("cell", None, None, None),
        P("cell", None, None), P("cell", None, None, None), P("cell", None, None, None),
        P("cell", None, None, None), P("cell", None, None, None),
        P("cell", None, None, None, None), P("cell", None),
    )
    return jax.shard_map(
        per_device, mesh=mesh, in_specs=in_specs, out_specs=out_specs, check_vma=False
    )
```

```python
import functools
import math

import jax
import jax.numpy as jnp
from jax import lax
from jax.experimental import pallas as pl
from jax.experimental.pallas import tpu as pltpu
from jax.sharding import PartitionSpec as P

CUTOFF = 5.0
SOFTEN = 0.1
NEIGH = 0.17677669529663687
F32 = jnp.float32
BF16 = jnp.bfloat16
LANES = 128
VMEM = pl.BlockSpec(memory_space=pltpu.VMEM)
SMEM = pl.BlockSpec(memory_space=pltpu.SMEM)
LIMIT = 20 * 1024 * 1024

NN = (((1,), (0,)), ((), ()))
NT = (((1,), (1,)), ((), ()))


BLOCK = 16


def row_of(comp, count, channel):
    return (channel // BLOCK * count + comp) * BLOCK


def by_block(parts):
    channels = parts[0].shape[0]
    return jnp.concatenate(
        [part[c : c + BLOCK] for c in range(0, channels, BLOCK) for part in parts], axis=0
    )


def component(value, comp, count):
    step = count * BLOCK
    at = comp * BLOCK
    return jnp.concatenate(
        [value[r + at : r + at + BLOCK] for r in range(0, value.shape[0], step)], axis=0
    )


def split(v):
    high = v.astype(BF16)
    return high, (v - high.astype(F32)).astype(BF16)


def dot(a, b, dims=NN):
    return lax.dot_general(a, b, dims, preferred_element_type=F32)


def dot3(a, b, dims=NN):
    ah, al = a if isinstance(a, tuple) else split(a)
    bh, bl = b if isinstance(b, tuple) else split(b)
    return dot(ah, bh, dims) + (dot(ah, bl, dims) + dot(al, bh, dims))


def cat3(v, axis):
    high, low = split(v)
    return jnp.concatenate([high, high, low], axis=axis)


def wcat3(v, axis):
    high, low = split(v)
    return jnp.concatenate([high, low, high], axis=axis)


def column(row, width):
    return jnp.broadcast_to(row, (width, row.shape[1])).T


ROW_Y = 8
ROW_ENV = 24
GEO_ROWS = 32


def write_geometry(geo, base, slots, counts, send, recv, shift, tables, own_pos):
    buckets, _, edges = send.shape
    bucket_of = lax.broadcasted_iota(jnp.int32, (buckets, LANES), 0)
    filled = jnp.zeros((buckets, LANES), jnp.int32)
    for k in slots:
        filled = jnp.where(bucket_of == k, counts[0, k], filled)
    own = [jnp.broadcast_to(own_pos[a : a + 1, :], (buckets, LANES)) for a in range(3)]
    lane = lax.broadcasted_iota(jnp.int32, (buckets, LANES), 1)
    for block in range(edges // LANES):
        cols = slice(block * LANES, (block + 1) * LANES)

        def put(row, value):
            for p, k in enumerate(slots, base):
                geo[p, row : row + 1, cols] = value[k : k + 1]

        from_idx = jnp.concatenate([send[k, :, cols] for k in range(buckets)], axis=0)
        to_idx = jnp.concatenate([recv[k, :, cols] for k in range(buckets)], axis=0)
        rel = []
        for a in range(3):
            there = jnp.take_along_axis(tables[a], from_idx, axis=1, mode="promise_in_bounds")
            here = jnp.take_along_axis(own[a], to_idx, axis=1, mode="promise_in_bounds")
            moved = jnp.concatenate([shift[3 * k + a, :, cols] for k in range(buckets)], axis=0)
            rel.append(there - here + moved.astype(F32))
        dist = jnp.sqrt(rel[0] * rel[0] + rel[1] * rel[1] + rel[2] * rel[2] + SOFTEN)
        inverse = 1.0 / dist
        x, y, z = (r * inverse for r in rel)
        angle = dist * (math.pi / CUTOFF)
        sine, twice = jnp.sin(angle), 2.0 * jnp.cos(angle)
        scale = math.sqrt(2.0 / CUTOFF) * inverse
        before, now = jnp.zeros_like(sine), sine
        for n in range(8):
            put(n, now * scale)
            before, now = now, twice * now - before
        xx, yy, zz = x * x, y * y, z * z
        planar = xx + yy
        rows = [
            jnp.ones_like(x),
            math.sqrt(3.0) * x,
            math.sqrt(3.0) * y,
            math.sqrt(3.0) * z,
            math.sqrt(15.0) * x * y,
            math.sqrt(15.0) * y * z,
            0.5 * math.sqrt(5.0) * (2.0 * zz - planar),
            math.sqrt(15.0) * x * z,
            0.5 * math.sqrt(15.0) * (xx - yy),
            math.sqrt(35.0 / 8.0) * (3.0 * xx - yy) * y,
            math.sqrt(105.0) * x * y * z,
            math.sqrt(21.0 / 8.0) * y * (4.0 * zz - planar),
            0.5 * math.sqrt(7.0) * z * (2.0 * zz - 3.0 * planar),
            math.sqrt(21.0 / 8.0) * x * (4.0 * zz - planar),
            0.5 * math.sqrt(105.0) * z * (xx - yy),
            math.sqrt(35.0 / 8.0) * (xx - 3.0 * yy) * x,
        ]
        for m, row in enumerate(rows):
            put(ROW_Y + m, row)
        q = dist * (1.0 / CUTOFF)
        q6 = q * q * q * q * q * q
        envelope = 1.0 - 28.0 * q6 + 48.0 * q6 * q - 21.0 * q6 * q * q
        put(ROW_ENV, jnp.where(lane + block * LANES < filled, envelope, 0.0))


def one_hot(index_row, atoms):
    edges = index_row.shape[1]
    atom = lax.broadcasted_iota(jnp.int32, (atoms, edges), 0)
    return jnp.where(atom == index_row, 1.0, 0.0).astype(BF16)


def twice(v, axis):
    return jnp.concatenate([v, v], axis=axis)


def silu_parts(v):
    gate = 1.0 / (1.0 + jnp.exp(-v))
    return v * gate, gate


def basis_stack(bessel):
    high = bessel.astype(BF16).astype(F32)
    return jnp.concatenate([high, high, bessel - high], axis=0).astype(BF16)


def lift(x_ref, w_up_t, out):
    atoms = out.shape[1] // 2
    parts = [
        split(dot3(w_up_t[min(comp, 1)], x_ref[comp * atoms : (comp + 1) * atoms, :], NT))
        for comp in range(4)
    ]
    out[:, :atoms] = by_block([high for high, _ in parts])
    out[:, atoms:] = by_block([low for _, low in parts])


def radial_weights(w_out, channels):
    w_t = w_out[...].T
    return by_block([w_t[at : at + channels] for at in range(0, w_t.shape[0], channels)])


def list_chunks(table, slots, counts, chunk, base=0):
    table[0, 0], table[1, 0], table[2, 0] = base, slots[0], 0
    total = 0
    for p, k in enumerate(slots, base):
        number = (counts[0, k] + chunk - 1) // chunk

        def note(j, at, p=p, k=k):
            table[0, at] = p
            table[1, at] = k
            table[2, at] = j * chunk
            return at + 1

        total = lax.fori_loop(0, number, note, total)
    return total


def chunk_at(table, t, chunk):
    return table[0, t], table[1, t], pl.ds(pl.multiple_of(table[2, t], chunk), chunk)


def forward_messages(feats, radial, geo_rows, out, channels, edges):
    ys = []
    for half in range(edges // LANES):
        cols = slice(half * LANES, (half + 1) * LANES)
        ys.append([jnp.broadcast_to(row[:, cols], (BLOCK, LANES)) for row in geo_rows])
    for c in range(0, channels, BLOCK):
        for half in range(edges // LANES):
            cols = slice(half * LANES, (half + 1) * LANES)
            low_cols = slice(edges + half * LANES, edges + (half + 1) * LANES)
            y = ys[half]

            def feat(k):
                at = row_of(k, 4, c)
                return feats[at : at + BLOCK, cols]

            def rad(k):
                at = row_of(k, 7, c)
                return radial[at : at + BLOCK, cols]

            def put(comp, value):
                high, low = split(value)
                at = row_of(comp, 16, c)
                out[at : at + BLOCK, cols] = high
                out[at : at + BLOCK, low_cols] = low

            s, v = feat(0), [feat(1), feat(2), feat(3)]
            inner = y[1] * v[0] + y[2] * v[1] + y[3] * v[2]
            put(0, rad(0) * s + rad(4) * inner)
            first, fifth, sixth = rad(1) * s, rad(5), rad(6)
            put(1, first * y[1] + fifth * v[0] + sixth * (y[2] * v[2] - y[3] * v[1]))
            put(2, first * y[2] + fifth * v[1] + sixth * (y[3] * v[0] - y[1] * v[2]))
            put(3, first * y[3] + fifth * v[2] + sixth * (y[1] * v[1] - y[2] * v[0]))
            second = rad(2) * s
            for m in range(4, 9):
                put(m, second * y[m])
            third = rad(3) * s
            for m in range(9, 16):
                put(m, third * y[m])


def in_pairs(count, one):
    if count > 1:
        def pair(i, carry):
            one(2 * i)
            one(2 * i + 1)
            return carry

        if count < 4:
            pair(0, 0)
        else:
            lax.fori_loop(0, count // 2, pair, 0)
    if count % 2:
        one(count - 1)


def radial_hidden(base, count, w_in, w_mid, geo, hidden_out):
    hid = w_in.shape[1]
    w_in_t = wcat3(w_in[...].T, 1)
    w_mid_t = [wcat3(w_mid[0].T, 1), wcat3(w_mid[1].T, 1)]

    def one(at):
        p = base + at
        h, _ = silu_parts(dot(w_in_t, basis_stack(geo[p, :8, :])))
        h, _ = silu_parts(dot(w_mid_t[0], cat3(h, 0)))
        h, _ = silu_parts(dot(w_mid_t[1], cat3(h, 0)))
        high, low = split(h * geo[p, ROW_ENV : ROW_ENV + 1, :])
        hidden_out[p, :hid, :] = high
        hidden_out[p, hid:, :] = low

    in_pairs(count, one)


def edge_forward(
    base, slots, chunk, counts, send, recv, shift, own_pos, tables, x_refs, w_up, w_in, w_mid, w_out,
    lifted_out, hidden_out, geo, acc, table, feats, radial, messages,
):
    channels, atoms = w_up.shape[1], acc.shape[1]
    hid = w_in.shape[1]
    total = list_chunks(table, slots, counts, chunk, base)
    write_geometry(geo, base, slots, counts, send, recv, shift, tables, own_pos)
    w_up_t = [split(w_up[0].T), split(w_up[1].T)]
    for p in range(len(slots)):
        lift(x_refs[p], w_up_t, lifted_out.at[base + p])
    radial_hidden(base, len(slots), w_in, w_mid, geo, hidden_out)
    w_out_t = wcat3(radial_weights(w_out, channels), 1)
    messages[1] = jnp.zeros_like(messages[1])

    def prepare(t, slot):
        p, k, cols = chunk_at(table, jnp.minimum(t, total - 1), chunk)
        high, low = hidden_out[p, :hid, cols], hidden_out[p, hid:, cols]
        radial[slot] = dot(w_out_t, jnp.concatenate([high, high, low], axis=0))
        from_hot = one_hot(send[k, :, cols], atoms)
        feats[slot] = dot(lifted_out[p], twice(from_hot, 0))

    def collect(t, slot):
        _, k, cols = chunk_at(table, jnp.maximum(t, 0), chunk)
        to_hot = one_hot(recv[k, :, cols], atoms)
        acc[...] += dot(messages[slot], twice(to_hot, 1), NT)

    def combine(t, slot):
        p, _, cols = chunk_at(table, t, chunk)
        rows = [geo[p, ROW_Y + m : ROW_Y + m + 1, cols] for m in range(16)]
        forward_messages(
            feats.at[slot], radial.at[slot], rows, messages.at[slot], channels, chunk
        )

    def step(i, carry):
        t = 2 * i
        combine(t, 0)
        prepare(t + 1, 1)
        collect(t - 1, 1)
        combine(t + 1, 1)
        prepare(t + 2, 0)
        collect(t, 0)
        return carry

    prepare(0, 0)
    lax.fori_loop(0, total // 2, step, 0)
    collect(total // 2 * 2 - 1, 1)

    @pl.when(total % 2 == 1)
    def _():
        combine(total - 1, 0)
        collect(total - 1, 0)


def forward_kernel(base, slots, chunk, first, node_counts, *refs):
    n = len(slots)
    counts, send, recv, shift, refs = *refs[:4], refs[4:]
    x_own, x_refs, refs = refs[0], refs[1 : 1 + n], refs[1 + n :]
    w_up, w_in, w_mid, w_out, refs = *refs[:4], refs[4:]
    atoms = w_up.shape[1]
    at = 4 * atoms
    if not first:
        acc_in, refs = refs[0], refs[1:]
    before, refs = refs[: 3 if base else 0], refs[3 if base else 0 :]
    if node_counts:
        n_in, n_out = node_counts
        node_in, node_out, refs = refs[:n_in], refs[n_in : n_in + n_out], refs[n_in + n_out :]
        lifted_out, hidden_out, geo, acc, flat, table, feats, radial, messages = refs
    else:
        acc, lifted_out, hidden_out, geo, table, feats, radial, messages = refs
    if first:
        acc[...] = jnp.zeros_like(acc)
    else:
        acc[...] = acc_in[...]
    for ref, out in zip(before, (lifted_out, hidden_out, geo)):
        out[:base] = ref[...]
    tables = []
    for a in range(3):
        rows = [x_own[at + a : at + a + 1, :]] * send.shape[0]
        for k, ref in zip(slots, x_refs):
            rows[k] = ref[at + a : at + a + 1, :]
        tables.append(jnp.concatenate(rows, axis=0))
    edge_forward(
        base, slots, chunk, counts, send, recv, shift, x_own.at[at : at + 8], tables, x_refs, w_up, w_in,
        w_mid, w_out, lifted_out, hidden_out, geo, acc, table, feats, radial, messages,
    )
    if node_counts:
        rows = [x_own[at + 3 : at + 4, :], x_own[at + 5 : at + 6, :]]
        node_stage(acc, flat, *rows, *node_in, *node_out)


def deal(flat, digit, parts):
    rows = parts[0].shape[0]
    for k, part in enumerate(parts):
        at = pl.multiple_of((digit ^ k) * rows, 8)
        part[...] = flat[pl.ds(at, rows), :]


def add_kernel(stage, groups, n_out, *refs):
    digits, refs = refs[0], refs[1:]
    totals = []
    for count, sizes in groups:
        total = functools.reduce(jnp.add, [part[...] for part in refs[:count]])
        refs = refs[count:]
        at = 0
        for size in sizes:
            totals.append(total[at : at + size])
            at += size
    if n_out == 1:
        at = 0
        for total in totals:
            refs[0][at : at + total.shape[0], :] = total
            at += total.shape[0]
        return
    outs, scratch = refs[:n_out], refs[n_out]
    at, out_at = 0, 0
    for total in totals:
        size = total.shape[0]
        scratch[at : at + size, :] = total
        rows = size // n_out
        for k, out in enumerate(outs):
            first = pl.multiple_of(at + (digits[0, stage] ^ k) * rows, 8)
            out[out_at : out_at + rows, :] = scratch[pl.ds(first, rows), :]
        at += size
        out_at += rows


def join_into(out, digit, inputs, sizes):
    at, out_at = 0, 0
    for size in sizes:
        for k, part in enumerate(inputs):
            first = pl.multiple_of(out_at + (digit ^ k) * size, 8)
            out[pl.ds(first, size), :] = part[at : at + size, :]
        at += size
        out_at += size * len(inputs)


def join_kernel(stage, radix, sizes, *refs):
    digits, inputs, out = refs[0], refs[1 : 1 + radix], refs[1 + radix]
    join_into(out, digits[0, stage], inputs, sizes)


def finish_kernel(radix, sizes, n_spec, *refs):
    digits, inputs, refs = refs[0], refs[1 : 1 + radix], refs[1 + radix :]
    node_outs, (g_out, g_up, g_mid, g_in, flat, store) = refs[:6], refs[6:]
    digit = digits[0, 0]
    join_into(flat, digit, inputs, sizes)
    at = 0
    for out in node_outs:
        if len(out.shape) == 3:
            for p in range(out.shape[0]):
                out[p] = flat[at + p * n_spec : at + (p + 1) * n_spec, :]
            at += up8(out.shape[0] * n_spec)
        else:
            out[...] = flat[at : at + out.shape[0], :]
            at += up8(out.shape[0])
    at = sizes[0] * radix
    hid, n_basis = g_out.shape[0], g_in.shape[0]
    for path in range(g_out.shape[1] // LANES):
        g_out[:, path * LANES : (path + 1) * LANES] = flat[at : at + hid, :]
        at += hid
    g_up[...] = flat[at : at + g_up.shape[0], :]
    for k, part in enumerate(inputs):
        store[digit ^ k] = part[sum(sizes) :, :]
    small = store[0]
    for member in range(1, radix):
        small = small + store[member]
    g_mid[0] = small[:hid, :hid]
    g_mid[1] = small[:hid, hid:]
    g_in[...] = small[hid : hid + n_basis, :hid]


DEGREE = (0, 1, 1, 1, 2, 2, 2, 2, 2, 3, 3, 3, 3, 3, 3, 3)


def species_hot(species_row, count):
    atoms = species_row.shape[1]
    which = lax.broadcasted_iota(jnp.int32, (count, atoms), 0)
    return jnp.where(which == species_row, 1.0, 0.0)


def up8(rows):
    return (rows + 7) // 8 * 8


def node_stage(
    acc, flat, species, w_read, digits, w_lin, w_sc_s, w_sc_v, w_prod, g_total, cot_v, skip_s,
    skip_v, g_skip, new_s, new_v, energy, grad_amp, *parts,
):
    channels, atoms = w_lin.shape[1], acc.shape[1]
    n_spec = w_sc_s.shape[1]
    flat[g_skip.shape[0] :, :] = jnp.zeros_like(flat[g_skip.shape[0] :, :])
    flat[: g_skip.shape[0], :] = g_skip[...]
    lin_at = g_skip.shape[0]
    prod_at = lin_at + 4 * channels
    sc_s_at = prod_at + 2 * channels
    sc_v_at = sc_s_at + up8(9 * n_spec)
    read_at = sc_v_at + up8(5 * n_spec)
    members = [[m for m in range(16) if DEGREE[m] == l] for l in range(4)]
    amp_t = [component(acc, m, 16) * NEIGH for m in range(16)]
    amp_t_parts = [split(v) for v in amp_t]
    b = []
    for l in range(4):
        high = jnp.concatenate([amp_t_parts[m][0].T for m in members[l]], axis=0)
        low = jnp.concatenate([amp_t_parts[m][1].T for m in members[l]], axis=0)
        stacked = dot(jnp.concatenate([high, high, low], axis=1), wcat3(w_lin[l], 0))
        b.extend(stacked[j * atoms : (j + 1) * atoms] for j in range(len(members[l])))
    b0 = b[0]
    n1 = b[1] * b[1] + b[2] * b[2] + b[3] * b[3]
    n2 = b[4] * b[4] + b[5] * b[5] + b[6] * b[6] + b[7] * b[7] + b[8] * b[8]
    n3 = functools.reduce(jnp.add, [b[m] * b[m] for m in range(9, 16)])
    species_col = column(species, channels)
    masks = [species_col == float(s) for s in range(n_spec)]

    def per_atom(w, p):
        value = jnp.broadcast_to(w[p, :1, :], (atoms, channels))
        for s in range(1, n_spec):
            value = jnp.where(masks[s], w[p, s : s + 1, :], value)
        return value

    ws = [per_atom(w_sc_s, p) for p in range(9)]
    wv = [per_atom(w_sc_v, p) for p in range(5)]
    sq = b0 * b0
    terms = [b0, sq, n1, n2, n3, sq * b0, b0 * n1, b0 * n2, b0 * n3]
    mixed = functools.reduce(jnp.add, [w * t for w, t in zip(ws, terms)])
    factors = [None, b0, sq, n1, n2]
    factor = wv[0]
    for p in range(1, 5):
        factor = factor + wv[p] * factors[p]
    prod_parts = [split(w_prod[0]), split(w_prod[1])]
    out_s = dot3(mixed, prod_parts[0]) + skip_s[...]
    new_s[...] = out_s
    mixed_v = [b[1 + a] * factor for a in range(3)]
    for a in range(3):
        new_v[a] = dot3(mixed_v[a], prod_parts[1]) + skip_v[a]
    energy[...] = dot3(jnp.broadcast_to(w_read, (8, channels)), out_s, NT)[:1]
    cot_e = g_total[1]
    flat[read_at : read_at + 1, :] = jnp.sum(out_s * cot_e, axis=0, keepdims=True)

    g_s = split(g_total[0])
    g_v = [split(cot_v[a]) for a in range(3)]
    flat[prod_at : prod_at + channels, :] = dot3(mixed.T, g_s)
    flat[prod_at + channels : sc_s_at, :] = functools.reduce(
        jnp.add, [dot3(mixed_v[a].T, g_v[a]) for a in range(3)]
    )
    g_mixed = dot3(g_s, prod_parts[0], NT)
    g_mixed_v = [dot3(g_v[a], prod_parts[1], NT) for a in range(3)]
    g_factor = functools.reduce(jnp.add, [g_mixed_v[a] * b[1 + a] for a in range(3)])

    hot = species_hot(species.astype(jnp.int32), 8).astype(BF16)

    def by_species(value):
        high, low = split(value)
        return dot(hot, high) + dot(hot, low)

    for p in range(9):
        row = sc_s_at + p * n_spec
        flat[row : row + n_spec, :] = by_species(g_mixed * terms[p])[:n_spec]
    for p in range(5):
        row = sc_v_at + p * n_spec
        value = g_factor * factors[p] if p else g_factor
        flat[row : row + n_spec, :] = by_species(value)[:n_spec]

    g_b0 = g_mixed * (
        ws[0] + 2.0 * b0 * ws[1] + 3.0 * sq * ws[5] + n1 * ws[6] + n2 * ws[7] + n3 * ws[8]
    ) + g_factor * (wv[1] + 2.0 * b0 * wv[2])
    g_n1 = 2.0 * (g_mixed * (ws[2] + b0 * ws[6]) + g_factor * wv[3])
    g_n2 = 2.0 * (g_mixed * (ws[3] + b0 * ws[7]) + g_factor * wv[4])
    g_n3 = 2.0 * (g_mixed * (ws[4] + b0 * ws[8]))
    g_b = [g_b0]
    for a in range(3):
        g_b.append(g_mixed_v[a] * factor + g_n1 * b[1 + a])
    for m in range(4, 9):
        g_b.append(g_n2 * b[m])
    for m in range(9, 16):
        g_b.append(g_n3 * b[m])
    g_b_parts = [split(v) for v in g_b]
    grads = []
    for l in range(4):
        row = lin_at + l * channels
        high = jnp.concatenate([g_b_parts[m][0] for m in members[l]], axis=0)
        low = jnp.concatenate([g_b_parts[m][1] for m in members[l]], axis=0)
        amp_high = jnp.concatenate([amp_t_parts[m][0] for m in members[l]], axis=1)
        amp_low = jnp.concatenate([amp_t_parts[m][1] for m in members[l]], axis=1)
        flat[row : row + channels, :] = dot(
            jnp.concatenate([amp_high, amp_high, amp_low], axis=1),
            jnp.concatenate([high, low, high], axis=0),
        )
        back = dot(wcat3(w_lin[l], 1), jnp.concatenate([high, high, low], axis=1), NT) * NEIGH
        grads.extend(
            split(back[:, j * atoms : (j + 1) * atoms]) for j in range(len(members[l]))
        )
    grad_amp[:, :atoms] = by_block([high for high, _ in grads])
    grad_amp[:, atoms:] = by_block([low for _, low in grads])
    deal(flat, digits[0, 0], parts)


def skip_kernel(
    x_own, cot_s, cot_v, w_skip,
    g_total, skip_s, skip_v, skip_gs, skip_gv, g_skip,
):
    atoms, channels = cot_s.shape
    n_spec = w_skip.shape[1]

    def own(comp):
        return x_own[comp * atoms : (comp + 1) * atoms, :]

    at = 4 * atoms + 3
    species, cot_e, w_read = x_own[at : at + 1, :], x_own[at + 1 : at + 2, :], x_own[at + 2 : at + 3, :]
    cot_col = column(cot_e, channels)
    total = cot_s[...] + cot_col * w_read
    g_total[0] = total
    g_total[1] = cot_col
    species_col = column(species, channels)
    masks = [species_col == float(s) for s in range(n_spec)]

    def pick(values):
        result = values[0]
        for s in range(1, n_spec):
            result = jnp.where(masks[s], values[s], result)
        return result

    for kind in range(2):
        weights = [split(w_skip[kind, s]) for s in range(n_spec)]
        if kind == 0:
            xs, gs = [own(0)], [total]
            outs, grads = [(skip_s, None)], [(skip_gs, None)]
        else:
            xs, gs = [own(1 + a) for a in range(3)], [cot_v[a] for a in range(3)]
            outs, grads = [(skip_v, a) for a in range(3)], [(skip_gv, a) for a in range(3)]
        sums = [None] * n_spec
        for x, g, (out, at), (grad, _) in zip(xs, gs, outs, grads):
            x_parts, g_parts = split(x), split(g)
            forward = pick([dot3(x_parts, w) for w in weights])
            back = pick([dot3(g_parts, w, NT) for w in weights])
            if at is None:
                out[...] = forward
                grad[...] = back
            else:
                out[at] = forward
                grad[at] = back
            x_t = split(x.T)
            for s in range(n_spec):
                part = dot3(x_t, split(jnp.where(masks[s], g, 0.0)))
                sums[s] = part if sums[s] is None else sums[s] + part
        for s in range(n_spec):
            row = (kind * n_spec + s) * channels
            g_skip[row : row + channels, :] = sums[s]


def backward_messages(feats, radial, grads, geo_rows, g_radial, g_feats, channels, edges):
    ys = []
    for half in range(edges // LANES):
        cols = slice(half * LANES, (half + 1) * LANES)
        ys.append([jnp.broadcast_to(row[:, cols], (BLOCK, LANES)) for row in geo_rows])
    for c in range(0, channels, BLOCK):
        for half in range(edges // LANES):
            cols = slice(half * LANES, (half + 1) * LANES)
            low_cols = slice(edges + half * LANES, edges + (half + 1) * LANES)
            y = ys[half]

            def load(ref, k, count):
                at = row_of(k, count, c)
                return ref[at : at + BLOCK, cols]

            def grad(m):
                return load(grads, m, 16)

            def rad(k):
                return load(radial, k, 7)

            def put(ref, comp, count, value):
                high, low = split(value)
                at = row_of(comp, count, c)
                ref[at : at + BLOCK, cols] = high
                ref[at : at + BLOCK, low_cols] = low

            s = load(feats, 0, 4)
            third = y[9] * grad(9)
            for m in range(10, 16):
                third = third + y[m] * grad(m)
            put(g_radial, 3, 7, s * third)
            second = y[4] * grad(4)
            for m in range(5, 9):
                second = second + y[m] * grad(m)
            put(g_radial, 2, 7, s * second)
            g = [grad(1 + a) for a in range(3)]
            first = y[1] * g[0] + y[2] * g[1] + y[3] * g[2]
            put(g_radial, 1, 7, s * first)
            zero = grad(0)
            put(g_radial, 0, 7, s * zero)
            put(
                g_feats, 0, 4,
                rad(0) * zero + rad(1) * first + rad(2) * second + rad(3) * third,
            )
            v = [load(feats, 1 + a, 4) for a in range(3)]
            put(g_radial, 4, 7, (y[1] * v[0] + y[2] * v[1] + y[3] * v[2]) * zero)
            put(g_radial, 5, 7, v[0] * g[0] + v[1] * g[1] + v[2] * g[2])
            cross = [
                g[1] * y[3] - g[2] * y[2],
                g[2] * y[1] - g[0] * y[3],
                g[0] * y[2] - g[1] * y[1],
            ]
            put(g_radial, 6, 7, v[0] * cross[0] + v[1] * cross[1] + v[2] * cross[2])
            fourth, fifth, sixth = rad(4) * zero, rad(5), rad(6)
            for a in range(3):
                put(g_feats, 1 + a, 4, fourth * y[1 + a] + fifth * g[a] + sixth * cross[a])


def backward_kernel(slots, chunk, first, last, n_parts, *refs):
    n = len(slots)
    counts, digits, send, recv, grad_amp = refs[:5]
    geo, lifted, hidden = refs[5:8]
    x_refs, refs = refs[8 : 8 + n], refs[8 + n :]
    w_up, w_out, refs = refs[0], refs[1], refs[2:]
    if not first:
        acc_out_in, acc_up_in, refs = refs[0], refs[1], refs[2:]
    x_grads, g_hidden, refs = refs[:n], refs[n], refs[n + 1 :]
    if last:
        parts, refs = refs[:n_parts], refs[n_parts:]
        flat, refs = refs[0], refs[1:]
    else:
        g_out, g_up, refs = refs[0], refs[1], refs[2:]
    table, feats, radial, grads, g_radial, g_feats, g_lifted, acc_out = refs
    channels = w_up.shape[1]
    atoms = g_lifted.shape[2]
    hid = w_out.shape[0]
    total = list_chunks(table, slots, counts, chunk)
    w_blocked = radial_weights(w_out, channels)
    w_out_t = wcat3(w_blocked, 1)
    w_high, w_low = split(w_blocked.T)
    w_both = jnp.concatenate([w_high, w_low], axis=0)
    if first:
        acc_out[...] = jnp.zeros_like(acc_out)
    else:
        acc_out[...] = acc_out_in[...]
    g_lifted[...] = jnp.zeros_like(g_lifted)
    g_radial[1] = jnp.zeros_like(g_radial[1])
    g_feats[1] = jnp.zeros_like(g_feats[1])

    def prepare(t, slot):
        p, k, cols = chunk_at(table, jnp.minimum(t, total - 1), chunk)
        high, low = hidden[p, :hid, cols], hidden[p, hid:, cols]
        to_hot = one_hot(recv[k, :, cols], atoms)
        grads[slot] = dot(grad_amp[...], twice(to_hot, 0))
        radial[slot] = dot(w_out_t, jnp.concatenate([high, high, low], axis=0))
        from_hot = one_hot(send[k, :, cols], atoms)
        feats[slot] = dot(lifted[p], twice(from_hot, 0))

    def collect(t, slot):
        p, k, cols = chunk_at(table, jnp.maximum(t, 0), chunk)
        both = dot(w_both, g_radial[slot, :, :chunk])
        g_hidden[p, :, cols] = both[:hid] + both[hid:] + dot(w_high, g_radial[slot, :, chunk:])
        high, low = hidden[p, :hid, cols], hidden[p, hid:, cols]
        stacked = jnp.concatenate(
            [twice(high, 1), jnp.concatenate([low, jnp.zeros_like(low)], axis=1)], axis=0
        )
        acc_out[...] += dot(g_radial[slot], stacked, NT)
        from_hot = one_hot(send[k, :, cols], atoms)
        g_lifted[p] += dot(g_feats[slot], twice(from_hot, 1), NT)

    def combine(t, slot):
        p, _, cols = chunk_at(table, t, chunk)
        rows = [geo[p, ROW_Y + m : ROW_Y + m + 1, cols] for m in range(16)]
        backward_messages(
            feats.at[slot], radial.at[slot], grads.at[slot], rows, g_radial.at[slot],
            g_feats.at[slot], channels, chunk,
        )

    def step(i, carry):
        t = 2 * i
        combine(t, 0)
        prepare(t + 1, 1)
        collect(t - 1, 1)
        combine(t + 1, 1)
        prepare(t + 2, 0)
        collect(t, 0)
        return carry

    prepare(0, 0)
    lax.fori_loop(0, total // 2, step, 0)
    collect(total // 2 * 2 - 1, 1)

    @pl.when(total % 2 == 1)
    def _():
        combine(total - 1, 0)
        collect(total - 1, 0)

    w_up_parts = [split(w_up[0]), split(w_up[1])]
    sums = [None, None] if first else [acc_up_in[0], acc_up_in[1]]
    for p in range(n):
        for comp in range(4):
            kind = min(comp, 1)
            high, low = split(component(g_lifted[p], comp, 4))
            x_grads[p][comp] = dot3((high.T, low.T), w_up_parts[kind], NT)
            part = dot3((high, low), x_refs[p][comp * atoms : (comp + 1) * atoms, :])
            sums[kind] = part if sums[kind] is None else sums[kind] + part
    if last:
        both = acc_out[...]
        both = both[:, :hid] + both[:, hid:]
        paths = both.shape[0] // channels
        up_at = paths * hid
        end = up_at + 2 * channels
        flat[end:, :] = jnp.zeros_like(flat[end:, :])
        for path in range(paths):
            flat[path * hid : (path + 1) * hid, :] = component(both, path, paths).T
        for kind in range(2):
            row = up_at + kind * channels
            flat[row : row + channels, :] = sums[kind].T
        deal(flat, digits[0, 0], parts)
    else:
        for kind in range(2):
            g_up[kind] = sums[kind]
        g_out[...] = acc_out[...]


def mlp_backward_kernel(groups, *refs):
    counts, refs = refs[0], refs[1:]
    number = len(groups)
    geos, grads, refs = refs[:number], refs[number : 2 * number], refs[2 * number :]
    w_in, w_mid, small, acc_in, acc_mid = refs
    n_basis, hid = w_in.shape
    w_in_t = wcat3(w_in[...].T, 1)
    w_mid_t = [wcat3(w_mid[0].T, 1), wcat3(w_mid[1].T, 1)]
    w_mid_n = [wcat3(w_mid[0], 1), wcat3(w_mid[1], 1)]
    acc_in[...] = jnp.zeros_like(acc_in)
    acc_mid[...] = jnp.zeros_like(acc_mid)
    edges = geos[0].shape[2]
    lane = lax.broadcasted_iota(jnp.int32, (hid, edges), 1)

    def stack(v):
        high, low = split(v)
        return jnp.concatenate([high, low], axis=0)

    for slots, geo, grad in zip(groups, geos, grads):
        def one(p, slots=slots, geo=geo, grad=grad):
            k = slots[0]
            for at, slot in enumerate(slots):
                k = jnp.where(p == at, slot, k)
            bessel = geo[p, :8, :]
            h1, s1 = silu_parts(dot(w_in_t, basis_stack(bessel)))
            h2, s2 = silu_parts(dot(w_mid_t[0], cat3(h1, 0)))
            h3, s3 = silu_parts(dot(w_mid_t[1], cat3(h2, 0)))
            g3 = grad[p] * geo[p, ROW_ENV : ROW_ENV + 1, :]
            g3 = jnp.where(lane < counts[0, k], g3, 0.0)
            d3 = g3 * (s3 + h3 * (1.0 - s3))
            acc_mid[1] += dot(stack(h2), stack(d3), NT)
            d2 = dot(w_mid_n[1], cat3(d3, 0)) * (s2 + h2 * (1.0 - s2))
            acc_mid[0] += dot(stack(h1), stack(d2), NT)
            d1 = dot(w_mid_n[0], cat3(d2, 0)) * (s1 + h1 * (1.0 - s1))
            high = bessel.astype(BF16).astype(F32)
            basis = jnp.concatenate([high, bessel - high], axis=0).astype(BF16)
            acc_in[...] += dot(basis, stack(d1), NT)

        in_pairs(len(slots), one)

    def quadrants(v, rows):
        return v[:rows, :hid] + v[:rows, hid:] + v[rows:, :hid]

    small[hid + n_basis :, :] = jnp.zeros_like(small[hid + n_basis :, :])
    small[:hid, :] = jnp.concatenate([quadrants(acc_mid[layer], hid) for layer in range(2)], axis=1)
    basis_grad = quadrants(acc_in[...], n_basis)
    small[hid : hid + n_basis, :] = jnp.concatenate([basis_grad, jnp.zeros_like(basis_grad)], axis=1)


def call(kernel, out_shape, smem, scratch, args, name, us):
    specs = [SMEM] * smem + [VMEM] * (len(args) - smem)
    return call_with(kernel, out_shape, specs, scratch, args, name, us)


def call_with(kernel, out_shape, specs, scratch, args, name, us):
    return pl.pallas_call(
        kernel,
        out_shape=out_shape,
        in_specs=specs,
        out_specs=jax.tree.map(lambda _: VMEM, out_shape),
        scratch_shapes=scratch,
        compiler_params=pltpu.CompilerParams(vmem_limit_bytes=LIMIT),
        cost_estimate=pl.CostEstimate(
            flops=int(us * 5e8), bytes_accessed=int(us * 2e6), transcendentals=0
        ),
        name=name,
    )(*args)


def shape(*dims, dtype=F32):
    return jax.ShapeDtypeStruct(dims, dtype)


def shifted(value, steps):
    count = lax.axis_size("blk")
    return lax.ppermute(value, "blk", [(i, (i + steps) % count) for i in range(count)])


def stages_of(count):
    stages, stride = [], 1
    while stride < count:
        members = 4 if (count // stride) % 4 == 0 else 2
        stages.append((members, stride))
        stride *= members
    return stages


def exchange(values, stage):
    members, stride = stage
    count = lax.axis_size("blk")
    moved = [
        lax.ppermute(values[k], "blk", [(i, i ^ (k * stride)) for i in range(count)])
        for k in range(1, members)
    ]
    return [values[0]] + moved


def add_parts(groups, stages, at, digits):
    arrays = [part for parts, _ in groups for part in parts]
    counts = tuple((len(parts), tuple(sizes)) for parts, sizes in groups)
    total = sum(size for _, sizes in groups for size in sizes)
    out = stages[at + 1][0] if at + 1 < len(stages) else 1
    shapes = shape(total, LANES)
    if out > 1:
        shapes = tuple(shape(total // out, LANES) for _ in range(out))
    return call(
        functools.partial(add_kernel, at + 1, counts, out), shapes, 1,
        [pltpu.VMEM((total, LANES), F32)] if out > 1 else [], (digits, *arrays), f"add_{at}", 1,
    )


def join_parts(parts, sizes, stages, at, digits):
    members = stages[at][0]
    return call(
        functools.partial(join_kernel, at, members, sizes), shape(members * sum(sizes), LANES), 1,
        [], (digits, *parts), f"join_{at}", 1,
    )


def per_device(
    node_scalars, node_vectors, positions, species, edge_senders, edge_receivers, edge_shifts,
    bucket_counts, w_up, w_rad_in, w_rad_mid, w_rad_out, w_lin, w_sc_scalar, w_sc_vector, w_prod,
    w_skip, w_read, cot_scalars, cot_vectors, cot_energy,
):
    _, buckets, slots = edge_senders.shape
    send = edge_senders.reshape(buckets, 1, slots)
    recv = edge_receivers.reshape(buckets, 1, slots)
    shift = edge_shifts.reshape(3 * buckets, 1, slots)
    reach = (buckets - 1) // 2
    atoms, channels = node_scalars.shape
    hid, outs = w_rad_out.shape
    n_basis = w_rad_in.shape[0]
    n_spec = w_skip.shape[1]
    chunk = min(256, slots)
    blocks = lax.axis_size("blk")
    stages = stages_of(blocks)
    me = lax.axis_index("blk")
    digits = jnp.stack([(me // stride) % members for members, stride in stages]).reshape(1, -1)
    rows, at = [], 0
    height = up8(4 * atoms + 6)
    for piece in (node_scalars, node_vectors.reshape(3 * atoms, channels), positions,
                  species.reshape(1, atoms), cot_energy.reshape(1, atoms),
                  w_read.reshape(1, channels)):
        end = at + piece.shape[0]
        rows.append(jnp.pad(piece, ((at, height - end), (0, 0))).astype(F32))
        at = end
    packed = functools.reduce(jnp.add, rows)
    offsets = sorted([d for d in range(-reach, reach + 1) if d], key=abs)
    x_of = {reach: packed, **{reach + d: shifted(packed, -d) for d in offsets}}
    sc_s_t, sc_v_t = jnp.swapaxes(w_sc_scalar, 0, 1), jnp.swapaxes(w_sc_vector, 0, 1)

    skip_rows = 2 * n_spec * channels
    g_total, skip_s, skip_v, skip_gs, skip_gv, g_skip = call(
        skip_kernel,
        (shape(2, atoms, channels), shape(atoms, channels), shape(3, atoms, channels),
         shape(atoms, channels), shape(3, atoms, channels), shape(skip_rows, channels)),
        0, [],
        (packed, cot_scalars, cot_vectors, w_skip),
        "self_connection", 4,
    )

    def padded(rows):
        unit = 8 * blocks
        return -(-rows // unit) * unit

    node_rows = padded(skip_rows + 6 * channels + up8(9 * n_spec) + up8(5 * n_spec) + 8)
    edge_rows = padded(outs // channels * hid + 2 * channels)
    tail_unit = 8 * (blocks // stages[0][0])
    small_rows = -(-(hid + n_basis) // tail_unit) * tail_unit

    near = (reach - 1, reach + 1)
    far = tuple(k for k in range(buckets) if abs(k - reach) > 1)
    groups = [(reach,), near] + ([far] if far else [])
    most = [len(g) * (slots // chunk) for g in groups]
    first_parts = stages[0][0]
    acc = ()
    kept = []
    for at, group in enumerate(groups):
        n = len(group)
        last = at == len(groups) - 1
        base = len(groups[1]) if at == 2 else 0
        out_shapes = (
            shape(base + n, 4 * channels, 2 * atoms, dtype=BF16), shape(base + n, 2 * hid, slots, dtype=BF16),
            shape(base + n, GEO_ROWS, slots),
        )
        scratch = [
            pltpu.SMEM((3, most[at]), jnp.int32),
            pltpu.VMEM((2, 4 * channels, chunk), F32),
            pltpu.VMEM((2, outs, chunk), F32),
            pltpu.VMEM((2, 16 * channels, 2 * chunk), BF16),
        ]
        node_args, node_counts = (), None
        if last:
            node_args = (digits, w_lin, sc_s_t, sc_v_t, w_prod, g_total,
                         cot_vectors, skip_s, skip_v, g_skip)
            node_outs = (
                shape(atoms, channels), shape(3, atoms, channels), shape(1, atoms),
                shape(16 * channels, 2 * atoms, dtype=BF16),
                *[shape(node_rows // first_parts, LANES)] * first_parts,
            )
            node_counts = len(node_args), len(node_outs)
            scratch = [
                pltpu.VMEM((16 * channels, atoms), F32), pltpu.VMEM((node_rows, LANES), F32)
            ] + scratch
            out_shapes = node_outs + out_shapes
        else:
            out_shapes = (shape(16 * channels, atoms),) + out_shapes
        args = (
            bucket_counts, send, recv, shift, packed, *[x_of[k] for k in group], w_up, w_rad_in,
            w_rad_mid, w_rad_out, *acc, *(kept[-1] if base else ()), *node_args,
        )
        specs = [SMEM] + [VMEM] * (len(args) - 1)
        if last:
            specs[len(args) - len(node_args)] = SMEM
        result = call_with(
            functools.partial(forward_kernel, base, group, chunk, at == 0, node_counts), out_shapes,
            specs, scratch, args, f"edges_{at}", 5 * n + (6 if last else 0),
        )
        kept.append(result[-3:])
        if last:
            new_s, new_v, energy, grad_amp = result[:4]
            node_parts = result[4 : 4 + first_parts]
        else:
            acc = result[:1]

    tie = lax.optimization_barrier
    node_parts = exchange(node_parts, stages[0])
    others = tuple(k for group in groups[1:] for k in group)
    sums = ()
    grads_hidden = []
    home = []
    for group, (lifted, hidden, geo) in ((others, kept[-1]), (groups[0], kept[0])):
        n = len(group)
        first, last = not sums, bool(sums)
        if last:
            final = (shape(edge_rows // first_parts, LANES),) * first_parts
        else:
            final = (shape(outs, 2 * hid), shape(2, channels, channels))
        args = (
            bucket_counts, digits, send, recv, grad_amp, geo, lifted, hidden,
            *[x_of[k] for k in group], w_up, w_rad_out, *sums,
        )
        result = call(
            functools.partial(backward_kernel, group, chunk, first, last, first_parts),
            (*[shape(4, atoms, channels) for _ in group], shape(n, hid, slots), *final), 2,
            ([pltpu.VMEM((edge_rows, LANES), F32)] if last else [])
            + [
                pltpu.SMEM((3, n * (slots // chunk)), jnp.int32),
                pltpu.VMEM((2, 4 * channels, chunk), F32),
                pltpu.VMEM((2, outs, chunk), F32),
                pltpu.VMEM((2, 16 * channels, chunk), F32),
                pltpu.VMEM((2, outs, 2 * chunk), BF16),
                pltpu.VMEM((2, 4 * channels, 2 * chunk), BF16),
                pltpu.VMEM((n, 4 * channels, atoms), F32),
                pltpu.VMEM((outs, 2 * hid), F32),
            ],
            args, "edges_back_own" if last else "edges_back", 6 * n,
        )
        if first:
            result, node_parts = tie((result, node_parts))
            node_sizes = [node_rows // first_parts]
            node_parts = exchange(
                add_parts([(node_parts, node_sizes)], stages, 0, digits), stages[1]
            )
            away = dict(zip(group, result[:n]))
            early = [k for k in group if k > reach]
            late = [k for k in group if k < reach]
            home = [shifted(away[k], k - reach) for k in early]
        else:
            result, node_parts, home, away = tie((result, node_parts, home, away))
            edge_parts = exchange(result[n + 1 :], stages[0])
            home = home + [result[0]] + [shifted(away[k], k - reach) for k in late]
        grads_hidden.append(result[n])
        sums = result[n + 1 :]
    small = call(
        functools.partial(mlp_backward_kernel, (others, groups[0])), shape(small_rows, LANES), 1,
        [pltpu.VMEM((2 * n_basis, 2 * hid), F32), pltpu.VMEM((2, 2 * hid, 2 * hid), F32)],
        (bucket_counts, kept[-1][2], kept[0][2], *grads_hidden, w_rad_in, w_rad_mid),
        "radial_back", 7,
    )
    small, edge_parts = tie((small, edge_parts))
    edge_sizes = [edge_rows // first_parts]
    groups = [(edge_parts, edge_sizes), ([small], [small_rows])]
    edge_parts = exchange(add_parts(groups, stages, 0, digits), stages[1])
    edge_parts, home = tie((edge_parts, home))
    second = stages[1][0]
    sizes = [node_sizes[0] // second, edge_sizes[0] // second, small_rows // second]
    groups = [(node_parts, sizes[:1]), (edge_parts, sizes[1:])]
    whole = add_parts(groups, stages, 1, digits)
    for at in range(2, len(stages)):
        sizes = [size // stages[at][0] for size in sizes]
        whole = add_parts([(exchange(whole, stages[at]), sizes)], stages, at, digits)
    for at in reversed(range(1, len(stages))):
        parts = exchange([whole] * stages[at][0], stages[at])
        whole = join_parts(parts, sizes, stages, at, digits)
        sizes = [size * stages[at][0] for size in sizes]
    parts = exchange([whole] * first_parts, stages[0])
    g_skip, g_lin, g_prod, g_sc_s, g_sc_v, g_read, g_out, g_up, g_mid, g_in = call(
        functools.partial(finish_kernel, first_parts, sizes[:2], n_spec),
        (shape(skip_rows, channels), shape(4 * channels, channels), shape(2 * channels, channels),
         shape(9, n_spec, channels), shape(5, n_spec, channels), shape(1, channels),
         shape(hid, outs), shape(2 * channels, channels), shape(2, hid, hid), shape(n_basis, hid)),
        1,
        [pltpu.VMEM((node_rows + edge_rows, LANES), F32),
         pltpu.VMEM((first_parts, small_rows, LANES), F32)],
        (digits, *parts), "finish", 2,
    )
    gx = home[0]
    for part in home[1:]:
        gx = gx + part
    return (
        new_s, new_v, energy.reshape(-1), gx[0] + skip_gs, gx[1:] + skip_gv,
        g_up.reshape(1, 2, channels, channels), g_in[None], g_mid[None], g_out[None],
        g_lin.reshape(1, 4, channels, channels), jnp.swapaxes(g_sc_s, 0, 1)[None],
        jnp.swapaxes(g_sc_v, 0, 1)[None], g_prod.reshape(1, 2, channels, channels),
        g_skip.reshape(1, 2, n_spec, channels, channels), g_read,
    )


def solution(mesh):
    atoms = ("cell", "blk")
    in_specs = (
        P(atoms, None), P(None, atoms, None), P(None, atoms), P(atoms), P(atoms, None, None),
        P(atoms, None, None), P(atoms, None, None, None), P(atoms, None),
        P(), P(), P(), P(), P(), P(), P(), P(), P(), P(),
        P(atoms, None), P(None, atoms, None), P(atoms),
    )
    out_specs = (
        P(atoms, None), P(None, atoms, None), P(atoms), P(atoms, None), P(None, atoms, None),
        P("cell", None, None, None), P("cell", None, None), P("cell", None, None, None),
        P("cell", None, None), P("cell", None, None, None), P("cell", None, None, None),
        P("cell", None, None, None), P("cell", None, None, None),
        P("cell", None, None, None, None), P("cell", None),
    )
    return jax.shard_map(
        per_device, mesh=mesh, in_specs=in_specs, out_specs=out_specs, check_vma=False
    )
```

```python
import functools
import math

import jax
import jax.numpy as jnp
from jax import lax
from jax.experimental import pallas as pl
from jax.experimental.pallas import tpu as pltpu
from jax.sharding import PartitionSpec as P

CUTOFF = 5.0
SOFTEN = 0.1
NEIGH = 0.17677669529663687
F32 = jnp.float32
BF16 = jnp.bfloat16
LANES = 128
VMEM = pl.BlockSpec(memory_space=pltpu.VMEM)
SMEM = pl.BlockSpec(memory_space=pltpu.SMEM)
LIMIT = 20 * 1024 * 1024

NN = (((1,), (0,)), ((), ()))
NT = (((1,), (1,)), ((), ()))


BLOCK = 16


def row_of(comp, count, channel):
    return (channel // BLOCK * count + comp) * BLOCK


def by_block(parts):
    channels = parts[0].shape[0]
    return jnp.concatenate(
        [part[c : c + BLOCK] for c in range(0, channels, BLOCK) for part in parts], axis=0
    )


def component(value, comp, count):
    step = count * BLOCK
    at = comp * BLOCK
    return jnp.concatenate(
        [value[r + at : r + at + BLOCK] for r in range(0, value.shape[0], step)], axis=0
    )


def split(v):
    high = v.astype(BF16)
    return high, (v - high.astype(F32)).astype(BF16)


def dot(a, b, dims=NN):
    return lax.dot_general(a, b, dims, preferred_element_type=F32)


def dot3(a, b, dims=NN):
    ah, al = a if isinstance(a, tuple) else split(a)
    bh, bl = b if isinstance(b, tuple) else split(b)
    return dot(ah, bh, dims) + (dot(ah, bl, dims) + dot(al, bh, dims))


def dot1(a, b, dims=NN):
    ah, al = a if isinstance(a, tuple) else split(a)
    bh, bl = b if isinstance(b, tuple) else split(b)
    left = jnp.concatenate([ah, ah, al], axis=1)
    right = jnp.concatenate([bh, bl, bh], axis=dims[0][1][0])
    return dot(left, right, dims)


def rows_of(v, count):
    step = v.shape[0] // count
    return [v[at * step : (at + 1) * step] for at in range(count)]


def columns_of(v, count):
    step = v.shape[1] // count
    return [v[:, at * step : (at + 1) * step] for at in range(count)]


def cat3(v, axis):
    high, low = split(v)
    return jnp.concatenate([high, high, low], axis=axis)


def wcat3(v, axis):
    high, low = split(v)
    return jnp.concatenate([high, low, high], axis=axis)


def column(row, width):
    return jnp.broadcast_to(row, (width, row.shape[1])).T


ROW_Y = 8
ROW_ENV = 24
GEO_ROWS = 32


def write_geometry(geo, base, slots, counts, send, recv, shift, tables, own_pos):
    buckets, _, edges = send.shape
    bucket_of = lax.broadcasted_iota(jnp.int32, (buckets, LANES), 0)
    filled = jnp.zeros((buckets, LANES), jnp.int32)
    for k in slots:
        filled = jnp.where(bucket_of == k, counts[0, k], filled)
    own = [jnp.broadcast_to(own_pos[a : a + 1, :], (buckets, LANES)) for a in range(3)]
    lane = lax.broadcasted_iota(jnp.int32, (buckets, LANES), 1)
    for block in range(edges // LANES):
        cols = slice(block * LANES, (block + 1) * LANES)

        def put(row, value):
            for p, k in enumerate(slots, base):
                geo[p, row : row + 1, cols] = value[k : k + 1]

        from_idx = jnp.concatenate([send[k, :, cols] for k in range(buckets)], axis=0)
        to_idx = jnp.concatenate([recv[k, :, cols] for k in range(buckets)], axis=0)
        rel = []
        for a in range(3):
            there = jnp.take_along_axis(tables[a], from_idx, axis=1, mode="promise_in_bounds")
            here = jnp.take_along_axis(own[a], to_idx, axis=1, mode="promise_in_bounds")
            moved = jnp.concatenate([shift[3 * k + a, :, cols] for k in range(buckets)], axis=0)
            rel.append(there - here + moved.astype(F32))
        dist = jnp.sqrt(rel[0] * rel[0] + rel[1] * rel[1] + rel[2] * rel[2] + SOFTEN)
        inverse = 1.0 / dist
        x, y, z = (r * inverse for r in rel)
        angle = dist * (math.pi / CUTOFF)
        sine, twice = jnp.sin(angle), 2.0 * jnp.cos(angle)
        scale = math.sqrt(2.0 / CUTOFF) * inverse
        before, now = jnp.zeros_like(sine), sine
        for n in range(8):
            put(n, now * scale)
            before, now = now, twice * now - before
        xx, yy, zz = x * x, y * y, z * z
        planar = xx + yy
        rows = [
            jnp.ones_like(x),
            math.sqrt(3.0) * x,
            math.sqrt(3.0) * y,
            math.sqrt(3.0) * z,
            math.sqrt(15.0) * x * y,
            math.sqrt(15.0) * y * z,
            0.5 * math.sqrt(5.0) * (2.0 * zz - planar),
            math.sqrt(15.0) * x * z,
            0.5 * math.sqrt(15.0) * (xx - yy),
            math.sqrt(35.0 / 8.0) * (3.0 * xx - yy) * y,
            math.sqrt(105.0) * x * y * z,
            math.sqrt(21.0 / 8.0) * y * (4.0 * zz - planar),
            0.5 * math.sqrt(7.0) * z * (2.0 * zz - 3.0 * planar),
            math.sqrt(21.0 / 8.0) * x * (4.0 * zz - planar),
            0.5 * math.sqrt(105.0) * z * (xx - yy),
            math.sqrt(35.0 / 8.0) * (xx - 3.0 * yy) * x,
        ]
        for m, row in enumerate(rows):
            put(ROW_Y + m, row)
        q = dist * (1.0 / CUTOFF)
        q6 = q * q * q * q * q * q
        envelope = 1.0 - 28.0 * q6 + 48.0 * q6 * q - 21.0 * q6 * q * q
        put(ROW_ENV, jnp.where(lane + block * LANES < filled, envelope, 0.0))


def one_hot(index_row, atoms):
    edges = index_row.shape[1]
    atom = lax.broadcasted_iota(jnp.int32, (atoms, edges), 0)
    return jnp.where(atom == index_row, 1.0, 0.0).astype(BF16)


def twice(v, axis):
    return jnp.concatenate([v, v], axis=axis)


def silu_parts(v):
    gate = 1.0 / (1.0 + jnp.exp(-v))
    return v * gate, gate


def basis_stack(bessel):
    high = bessel.astype(BF16).astype(F32)
    return jnp.concatenate([high, high, bessel - high], axis=0).astype(BF16)


def lift(x_ref, w_up_t, out):
    atoms = out.shape[1] // 2
    scalars = dot1(w_up_t[0], x_ref[:atoms, :], NT)
    vectors = dot1(w_up_t[1], x_ref[atoms : 4 * atoms, :], NT)
    parts = [split(value) for value in [scalars] + columns_of(vectors, 3)]
    out[:, :atoms] = by_block([high for high, _ in parts])
    out[:, atoms:] = by_block([low for _, low in parts])


def radial_weights(w_out, channels):
    w_t = w_out[...].T
    return by_block([w_t[at : at + channels] for at in range(0, w_t.shape[0], channels)])


def list_chunks(table, slots, counts, chunk, base=0):
    table[0, 0], table[1, 0], table[2, 0] = base, slots[0], 0
    total = 0
    for p, k in enumerate(slots, base):
        number = (counts[0, k] + chunk - 1) // chunk

        def note(j, at, p=p, k=k):
            table[0, at] = p
            table[1, at] = k
            table[2, at] = j * chunk
            return at + 1

        total = lax.fori_loop(0, number, note, total)
    return total


def chunk_at(table, t, chunk):
    return table[0, t], table[1, t], pl.ds(pl.multiple_of(table[2, t], chunk), chunk)


def forward_messages(feats, radial, geo_rows, out, channels, edges):
    ys = []
    for half in range(edges // LANES):
        cols = slice(half * LANES, (half + 1) * LANES)
        ys.append([jnp.broadcast_to(row[:, cols], (BLOCK, LANES)) for row in geo_rows])
    for c in range(0, channels, BLOCK):
        for half in range(edges // LANES):
            cols = slice(half * LANES, (half + 1) * LANES)
            low_cols = slice(edges + half * LANES, edges + (half + 1) * LANES)
            y = ys[half]

            def feat(k):
                at = row_of(k, 4, c)
                return feats[at : at + BLOCK, cols]

            def rad(k):
                at = row_of(k, 7, c)
                return radial[at : at + BLOCK, cols]

            def put(comp, value):
                high, low = split(value)
                at = row_of(comp, 16, c)
                out[at : at + BLOCK, cols] = high
                out[at : at + BLOCK, low_cols] = low

            s, v = feat(0), [feat(1), feat(2), feat(3)]
            inner = y[1] * v[0] + y[2] * v[1] + y[3] * v[2]
            put(0, rad(0) * s + rad(4) * inner)
            first, fifth, sixth = rad(1) * s, rad(5), rad(6)
            put(1, first * y[1] + fifth * v[0] + sixth * (y[2] * v[2] - y[3] * v[1]))
            put(2, first * y[2] + fifth * v[1] + sixth * (y[3] * v[0] - y[1] * v[2]))
            put(3, first * y[3] + fifth * v[2] + sixth * (y[1] * v[1] - y[2] * v[0]))
            second = rad(2) * s
            for m in range(4, 9):
                put(m, second * y[m])
            third = rad(3) * s
            for m in range(9, 16):
                put(m, third * y[m])


def in_pairs(count, one):
    if count > 1:
        def pair(i, carry):
            one(2 * i)
            one(2 * i + 1)
            return carry

        if count < 4:
            pair(0, 0)
        else:
            lax.fori_loop(0, count // 2, pair, 0)
    if count % 2:
        one(count - 1)


def radial_hidden(base, count, w_in, w_mid, geo, hidden_out):
    hid = w_in.shape[1]
    w_in_t = wcat3(w_in[...].T, 1)
    w_mid_t = [wcat3(w_mid[0].T, 1), wcat3(w_mid[1].T, 1)]

    def one(at):
        p = base + at
        h, _ = silu_parts(dot(w_in_t, basis_stack(geo[p, :8, :])))
        h, _ = silu_parts(dot(w_mid_t[0], cat3(h, 0)))
        h, _ = silu_parts(dot(w_mid_t[1], cat3(h, 0)))
        high, low = split(h * geo[p, ROW_ENV : ROW_ENV + 1, :])
        hidden_out[p, :hid, :] = high
        hidden_out[p, hid:, :] = low

    in_pairs(count, one)


def edge_forward(
    base, slots, chunk, counts, send, recv, shift, own_pos, tables, x_refs, w_up, w_in, w_mid, w_out,
    lifted_out, hidden_out, geo, acc, table, feats, radial, messages,
):
    channels, atoms = w_up.shape[1], acc.shape[1]
    hid = w_in.shape[1]
    total = list_chunks(table, slots, counts, chunk, base)
    write_geometry(geo, base, slots, counts, send, recv, shift, tables, own_pos)
    w_up_t = [split(w_up[0].T), split(w_up[1].T)]
    for p in range(len(slots)):
        lift(x_refs[p], w_up_t, lifted_out.at[base + p])
    radial_hidden(base, len(slots), w_in, w_mid, geo, hidden_out)
    w_out_t = wcat3(radial_weights(w_out, channels), 1)
    messages[1] = jnp.zeros_like(messages[1])

    def prepare(t, slot):
        p, k, cols = chunk_at(table, jnp.minimum(t, total - 1), chunk)
        high, low = hidden_out[p, :hid, cols], hidden_out[p, hid:, cols]
        radial[slot] = dot(w_out_t, jnp.concatenate([high, high, low], axis=0))
        from_hot = one_hot(send[k, :, cols], atoms)
        feats[slot] = dot(lifted_out[p], twice(from_hot, 0))

    def collect(t, slot):
        _, k, cols = chunk_at(table, jnp.maximum(t, 0), chunk)
        to_hot = one_hot(recv[k, :, cols], atoms)
        acc[...] += dot(messages[slot], twice(to_hot, 1), NT)

    def combine(t, slot):
        p, _, cols = chunk_at(table, t, chunk)
        rows = [geo[p, ROW_Y + m : ROW_Y + m + 1, cols] for m in range(16)]
        forward_messages(
            feats.at[slot], radial.at[slot], rows, messages.at[slot], channels, chunk
        )

    def step(i, carry):
        t = 2 * i
        combine(t, 0)
        prepare(t + 1, 1)
        collect(t - 1, 1)
        combine(t + 1, 1)
        prepare(t + 2, 0)
        collect(t, 0)
        return carry

    prepare(0, 0)
    lax.fori_loop(0, total // 2, step, 0)
    collect(total // 2 * 2 - 1, 1)

    @pl.when(total % 2 == 1)
    def _():
        combine(total - 1, 0)
        collect(total - 1, 0)


def forward_kernel(base, slots, chunk, first, node_counts, *refs):
    n = len(slots)
    counts, send, recv, shift, refs = *refs[:4], refs[4:]
    x_own, x_refs, refs = refs[0], refs[1 : 1 + n], refs[1 + n :]
    w_up, w_in, w_mid, w_out, refs = *refs[:4], refs[4:]
    atoms = w_up.shape[1]
    at = 4 * atoms
    if not first:
        acc_in, refs = refs[0], refs[1:]
    before, refs = refs[: 3 if base else 0], refs[3 if base else 0 :]
    if node_counts:
        n_in, n_out = node_counts
        node_in, node_out, refs = refs[:n_in], refs[n_in : n_in + n_out], refs[n_in + n_out :]
        lifted_out, hidden_out, geo, acc, flat, table, feats, radial, messages = refs
    else:
        acc, lifted_out, hidden_out, geo, table, feats, radial, messages = refs
    if first:
        acc[...] = jnp.zeros_like(acc)
    else:
        acc[...] = acc_in[...]
    for ref, out in zip(before, (lifted_out, hidden_out, geo)):
        out[:base] = ref[...]
    tables = []
    for a in range(3):
        rows = [x_own[at + a : at + a + 1, :]] * send.shape[0]
        for k, ref in zip(slots, x_refs):
            rows[k] = ref[at + a : at + a + 1, :]
        tables.append(jnp.concatenate(rows, axis=0))
    edge_forward(
        base, slots, chunk, counts, send, recv, shift, x_own.at[at : at + 8], tables, x_refs, w_up, w_in,
        w_mid, w_out, lifted_out, hidden_out, geo, acc, table, feats, radial, messages,
    )
    if node_counts:
        rows = [x_own[at + 3 : at + 4, :], x_own[at + 5 : at + 6, :]]
        node_stage(acc, flat, *rows, *node_in, *node_out)


def deal(flat, digit, parts):
    rows = parts[0].shape[0]
    for k, part in enumerate(parts):
        at = pl.multiple_of((digit ^ k) * rows, 8)
        part[...] = flat[pl.ds(at, rows), :]


def add_kernel(stage, groups, n_out, *refs):
    digits, refs = refs[0], refs[1:]
    totals = []
    for count, sizes in groups:
        total = functools.reduce(jnp.add, [part[...] for part in refs[:count]])
        refs = refs[count:]
        at = 0
        for size in sizes:
            totals.append(total[at : at + size])
            at += size
    if n_out == 1:
        at = 0
        for total in totals:
            refs[0][at : at + total.shape[0], :] = total
            at += total.shape[0]
        return
    outs, scratch = refs[:n_out], refs[n_out]
    at, out_at = 0, 0
    for total in totals:
        size = total.shape[0]
        scratch[at : at + size, :] = total
        rows = size // n_out
        for k, out in enumerate(outs):
            first = pl.multiple_of(at + (digits[0, stage] ^ k) * rows, 8)
            out[out_at : out_at + rows, :] = scratch[pl.ds(first, rows), :]
        at += size
        out_at += rows


def join_into(out, digit, inputs, sizes):
    at, out_at = 0, 0
    for size in sizes:
        for k, part in enumerate(inputs):
            first = pl.multiple_of(out_at + (digit ^ k) * size, 8)
            out[pl.ds(first, size), :] = part[at : at + size, :]
        at += size
        out_at += size * len(inputs)


def join_kernel(stage, radix, sizes, *refs):
    digits, inputs, out = refs[0], refs[1 : 1 + radix], refs[1 + radix]
    join_into(out, digits[0, stage], inputs, sizes)


def finish_kernel(radix, sizes, n_spec, *refs):
    digits, inputs, refs = refs[0], refs[1 : 1 + radix], refs[1 + radix :]
    node_outs, (g_out, g_up, g_mid, g_in, flat, store) = refs[:6], refs[6:]
    digit = digits[0, 0]
    join_into(flat, digit, inputs, sizes)
    at = 0
    for out in node_outs:
        if len(out.shape) == 3:
            for p in range(out.shape[0]):
                out[p] = flat[at + p * n_spec : at + (p + 1) * n_spec, :]
            at += up8(out.shape[0] * n_spec)
        else:
            out[...] = flat[at : at + out.shape[0], :]
            at += up8(out.shape[0])
    at = sizes[0] * radix
    hid, n_basis = g_out.shape[0], g_in.shape[0]
    for path in range(g_out.shape[1] // LANES):
        g_out[:, path * LANES : (path + 1) * LANES] = flat[at : at + hid, :]
        at += hid
    g_up[...] = flat[at : at + g_up.shape[0], :]
    for k, part in enumerate(inputs):
        store[digit ^ k] = part[sum(sizes) :, :]
    small = store[0]
    for member in range(1, radix):
        small = small + store[member]
    g_mid[0] = small[:hid, :hid]
    g_mid[1] = small[:hid, hid:]
    g_in[...] = small[hid : hid + n_basis, :hid]


DEGREE = (0, 1, 1, 1, 2, 2, 2, 2, 2, 3, 3, 3, 3, 3, 3, 3)


def species_hot(species_row, count):
    atoms = species_row.shape[1]
    which = lax.broadcasted_iota(jnp.int32, (count, atoms), 0)
    return jnp.where(which == species_row, 1.0, 0.0)


def up8(rows):
    return (rows + 7) // 8 * 8


def node_stage(
    acc, flat, species, w_read, digits, w_lin, w_sc_s, w_sc_v, w_prod, g_total, cot_v, skip_s,
    skip_v, g_skip, new_s, new_v, energy, grad_amp, *parts,
):
    channels, atoms = w_lin.shape[1], acc.shape[1]
    n_spec = w_sc_s.shape[1]
    flat[g_skip.shape[0] :, :] = jnp.zeros_like(flat[g_skip.shape[0] :, :])
    flat[: g_skip.shape[0], :] = g_skip[...]
    lin_at = g_skip.shape[0]
    prod_at = lin_at + 4 * channels
    sc_s_at = prod_at + 2 * channels
    sc_v_at = sc_s_at + up8(9 * n_spec)
    read_at = sc_v_at + up8(5 * n_spec)
    members = [[m for m in range(16) if DEGREE[m] == l] for l in range(4)]
    amp_t = [component(acc, m, 16) * NEIGH for m in range(16)]
    amp_t_parts = [split(v) for v in amp_t]
    b = []
    for l in range(4):
        high = jnp.concatenate([amp_t_parts[m][0].T for m in members[l]], axis=0)
        low = jnp.concatenate([amp_t_parts[m][1].T for m in members[l]], axis=0)
        stacked = dot(jnp.concatenate([high, high, low], axis=1), wcat3(w_lin[l], 0))
        b.extend(stacked[j * atoms : (j + 1) * atoms] for j in range(len(members[l])))
    b0 = b[0]
    n1 = b[1] * b[1] + b[2] * b[2] + b[3] * b[3]
    n2 = b[4] * b[4] + b[5] * b[5] + b[6] * b[6] + b[7] * b[7] + b[8] * b[8]
    n3 = functools.reduce(jnp.add, [b[m] * b[m] for m in range(9, 16)])
    species_col = column(species, channels)
    masks = [species_col == float(s) for s in range(n_spec)]

    def per_atom(w, p):
        value = jnp.broadcast_to(w[p, :1, :], (atoms, channels))
        for s in range(1, n_spec):
            value = jnp.where(masks[s], w[p, s : s + 1, :], value)
        return value

    ws = [per_atom(w_sc_s, p) for p in range(9)]
    wv = [per_atom(w_sc_v, p) for p in range(5)]
    sq = b0 * b0
    terms = [b0, sq, n1, n2, n3, sq * b0, b0 * n1, b0 * n2, b0 * n3]
    mixed = functools.reduce(jnp.add, [w * t for w, t in zip(ws, terms)])
    factors = [None, b0, sq, n1, n2]
    factor = wv[0]
    for p in range(1, 5):
        factor = factor + wv[p] * factors[p]
    prod_parts = [split(w_prod[0]), split(w_prod[1])]
    out_s = dot1(mixed, prod_parts[0]) + skip_s[...]
    new_s[...] = out_s
    mixed_v = jnp.concatenate([b[1 + a] * factor for a in range(3)], axis=0)
    for a, value in enumerate(rows_of(dot1(mixed_v, prod_parts[1]), 3)):
        new_v[a] = value + skip_v[a]
    energy[...] = dot3(jnp.broadcast_to(w_read, (8, channels)), out_s, NT)[:1]
    cot_e = g_total[1]
    flat[read_at : read_at + 1, :] = jnp.sum(out_s * cot_e, axis=0, keepdims=True)

    g_s = split(g_total[0])
    g_v = split(jnp.concatenate([cot_v[a] for a in range(3)], axis=0))
    flat[prod_at : prod_at + channels, :] = dot1(mixed.T, g_s)
    flat[prod_at + channels : sc_s_at, :] = dot1(mixed_v.T, g_v)
    g_mixed = dot1(g_s, prod_parts[0], NT)
    g_mixed_v = rows_of(dot1(g_v, prod_parts[1], NT), 3)
    g_factor = functools.reduce(jnp.add, [g_mixed_v[a] * b[1 + a] for a in range(3)])

    hot = species_hot(species.astype(jnp.int32), 8).astype(BF16)
    values = [g_mixed * terms[p] for p in range(9)]
    values += [g_factor] + [g_factor * factors[p] for p in range(1, 5)]
    high, low = split(jnp.concatenate(values, axis=1))
    by_species = dot(twice(hot, 1), jnp.concatenate([high, low], axis=0))
    for p, value in enumerate(columns_of(by_species, len(values))):
        row = sc_s_at + p * n_spec if p < 9 else sc_v_at + (p - 9) * n_spec
        flat[row : row + n_spec, :] = value[:n_spec]

    g_b0 = g_mixed * (
        ws[0] + 2.0 * b0 * ws[1] + 3.0 * sq * ws[5] + n1 * ws[6] + n2 * ws[7] + n3 * ws[8]
    ) + g_factor * (wv[1] + 2.0 * b0 * wv[2])
    g_n1 = 2.0 * (g_mixed * (ws[2] + b0 * ws[6]) + g_factor * wv[3])
    g_n2 = 2.0 * (g_mixed * (ws[3] + b0 * ws[7]) + g_factor * wv[4])
    g_n3 = 2.0 * (g_mixed * (ws[4] + b0 * ws[8]))
    g_b = [g_b0]
    for a in range(3):
        g_b.append(g_mixed_v[a] * factor + g_n1 * b[1 + a])
    for m in range(4, 9):
        g_b.append(g_n2 * b[m])
    for m in range(9, 16):
        g_b.append(g_n3 * b[m])
    g_b_parts = [split(v) for v in g_b]
    grads = []
    for l in range(4):
        row = lin_at + l * channels
        high = jnp.concatenate([g_b_parts[m][0] for m in members[l]], axis=0)
        low = jnp.concatenate([g_b_parts[m][1] for m in members[l]], axis=0)
        amp_high = jnp.concatenate([amp_t_parts[m][0] for m in members[l]], axis=1)
        amp_low = jnp.concatenate([amp_t_parts[m][1] for m in members[l]], axis=1)
        flat[row : row + channels, :] = dot(
            jnp.concatenate([amp_high, amp_high, amp_low], axis=1),
            jnp.concatenate([high, low, high], axis=0),
        )
        back = dot(wcat3(w_lin[l], 1), jnp.concatenate([high, high, low], axis=1), NT) * NEIGH
        grads.extend(
            split(back[:, j * atoms : (j + 1) * atoms]) for j in range(len(members[l]))
        )
    grad_amp[:, :atoms] = by_block([high for high, _ in grads])
    grad_amp[:, atoms:] = by_block([low for _, low in grads])
    deal(flat, digits[0, 0], parts)


def skip_kernel(
    x_own, cot_s, cot_v, w_skip,
    g_total, skip_s, skip_v, skip_gs, skip_gv, g_skip,
):
    atoms, channels = cot_s.shape
    n_spec = w_skip.shape[1]

    at = 4 * atoms + 3
    species, cot_e, w_read = x_own[at : at + 1, :], x_own[at + 1 : at + 2, :], x_own[at + 2 : at + 3, :]
    cot_col = column(cot_e, channels)
    total = cot_s[...] + cot_col * w_read
    g_total[0] = total
    g_total[1] = cot_col
    species_col = column(species, channels)

    def pick(values, masks):
        result = values[0]
        for s in range(1, n_spec):
            result = jnp.where(masks[s], values[s], result)
        return result

    for kind in range(2):
        count = 1 + 2 * kind
        masks = [jnp.concatenate([species_col == float(s)] * count, axis=0) for s in range(n_spec)]
        x = x_own[kind * atoms : (kind + count) * atoms, :]
        g = jnp.concatenate([cot_v[a] for a in range(3)], axis=0) if kind else total
        weights = [split(w_skip[kind, s]) for s in range(n_spec)]
        wide = tuple(jnp.concatenate([w[i] for w in weights], axis=1) for i in range(2))
        tall = tuple(jnp.concatenate([w[i] for w in weights], axis=0) for i in range(2))
        forward = pick(columns_of(dot1(x, wide), n_spec), masks)
        back = pick(columns_of(dot1(g, tall, NT), n_spec), masks)
        if kind:
            for a in range(3):
                skip_v[a] = forward[a * atoms : (a + 1) * atoms]
                skip_gv[a] = back[a * atoms : (a + 1) * atoms]
        else:
            skip_s[...] = forward
            skip_gs[...] = back
        apart = jnp.concatenate([jnp.where(mask, g, 0.0) for mask in masks], axis=1)
        sums = dot1(x.T, apart)
        for s, value in enumerate(columns_of(sums, n_spec)):
            row = (kind * n_spec + s) * channels
            g_skip[row : row + channels, :] = value


def backward_messages(feats, radial, grads, geo_rows, g_radial, g_feats, channels, edges):
    ys = []
    for half in range(edges // LANES):
        cols = slice(half * LANES, (half + 1) * LANES)
        ys.append([jnp.broadcast_to(row[:, cols], (BLOCK, LANES)) for row in geo_rows])
    for c in range(0, channels, BLOCK):
        for half in range(edges // LANES):
            cols = slice(half * LANES, (half + 1) * LANES)
            low_cols = slice(edges + half * LANES, edges + (half + 1) * LANES)
            y = ys[half]

            def load(ref, k, count):
                at = row_of(k, count, c)
                return ref[at : at + BLOCK, cols]

            def grad(m):
                return load(grads, m, 16)

            def rad(k):
                return load(radial, k, 7)

            def put(ref, comp, count, value):
                high, low = split(value)
                at = row_of(comp, count, c)
                ref[at : at + BLOCK, cols] = high
                ref[at : at + BLOCK, low_cols] = low

            s = load(feats, 0, 4)
            third = y[9] * grad(9)
            for m in range(10, 16):
                third = third + y[m] * grad(m)
            put(g_radial, 3, 7, s * third)
            second = y[4] * grad(4)
            for m in range(5, 9):
                second = second + y[m] * grad(m)
            put(g_radial, 2, 7, s * second)
            g = [grad(1 + a) for a in range(3)]
            first = y[1] * g[0] + y[2] * g[1] + y[3] * g[2]
            put(g_radial, 1, 7, s * first)
            zero = grad(0)
            put(g_radial, 0, 7, s * zero)
            put(
                g_feats, 0, 4,
                rad(0) * zero + rad(1) * first + rad(2) * second + rad(3) * third,
            )
            v = [load(feats, 1 + a, 4) for a in range(3)]
            put(g_radial, 4, 7, (y[1] * v[0] + y[2] * v[1] + y[3] * v[2]) * zero)
            put(g_radial, 5, 7, v[0] * g[0] + v[1] * g[1] + v[2] * g[2])
            cross = [
                g[1] * y[3] - g[2] * y[2],
                g[2] * y[1] - g[0] * y[3],
                g[0] * y[2] - g[1] * y[1],
            ]
            put(g_radial, 6, 7, v[0] * cross[0] + v[1] * cross[1] + v[2] * cross[2])
            fourth, fifth, sixth = rad(4) * zero, rad(5), rad(6)
            for a in range(3):
                put(g_feats, 1 + a, 4, fourth * y[1 + a] + fifth * g[a] + sixth * cross[a])


def backward_kernel(slots, chunk, first, last, n_parts, *refs):
    n = len(slots)
    counts, digits, send, recv, grad_amp = refs[:5]
    geo, lifted, hidden = refs[5:8]
    x_refs, refs = refs[8 : 8 + n], refs[8 + n :]
    w_up, w_out, refs = refs[0], refs[1], refs[2:]
    if not first:
        acc_out_in, acc_up_in, refs = refs[0], refs[1], refs[2:]
    x_grads, g_hidden, refs = refs[:n], refs[n], refs[n + 1 :]
    if last:
        parts, refs = refs[:n_parts], refs[n_parts:]
        flat, refs = refs[0], refs[1:]
    else:
        g_out, g_up, refs = refs[0], refs[1], refs[2:]
    table, feats, radial, grads, g_radial, g_feats, g_lifted, acc_out = refs
    channels = w_up.shape[1]
    atoms = g_lifted.shape[2]
    hid = w_out.shape[0]
    total = list_chunks(table, slots, counts, chunk)
    w_blocked = radial_weights(w_out, channels)
    w_out_t = wcat3(w_blocked, 1)
    w_high, w_low = split(w_blocked.T)
    w_both = jnp.concatenate(
        [twice(w_high, 1), jnp.concatenate([w_low, jnp.zeros_like(w_low)], axis=1)], axis=0
    )
    if first:
        acc_out[...] = jnp.zeros_like(acc_out)
    else:
        acc_out[...] = acc_out_in[...]
    g_lifted[...] = jnp.zeros_like(g_lifted)
    g_radial[1] = jnp.zeros_like(g_radial[1])
    g_feats[1] = jnp.zeros_like(g_feats[1])

    def prepare(t, slot):
        p, k, cols = chunk_at(table, jnp.minimum(t, total - 1), chunk)
        high, low = hidden[p, :hid, cols], hidden[p, hid:, cols]
        to_hot = one_hot(recv[k, :, cols], atoms)
        grads[slot] = dot(grad_amp[...], twice(to_hot, 0))
        radial[slot] = dot(w_out_t, jnp.concatenate([high, high, low], axis=0))
        from_hot = one_hot(send[k, :, cols], atoms)
        feats[slot] = dot(lifted[p], twice(from_hot, 0))

    def collect(t, slot):
        p, k, cols = chunk_at(table, jnp.maximum(t, 0), chunk)
        tall = jnp.concatenate([g_radial[slot, :, :chunk], g_radial[slot, :, chunk:]], axis=0)
        both = dot(w_both, tall)
        g_hidden[p, :, cols] = both[:hid] + both[hid:]
        high, low = hidden[p, :hid, cols], hidden[p, hid:, cols]
        stacked = jnp.concatenate(
            [twice(high, 1), jnp.concatenate([low, jnp.zeros_like(low)], axis=1)], axis=0
        )
        acc_out[...] += dot(g_radial[slot], stacked, NT)
        from_hot = one_hot(send[k, :, cols], atoms)
        g_lifted[p] += dot(g_feats[slot], twice(from_hot, 1), NT)

    def combine(t, slot):
        p, _, cols = chunk_at(table, t, chunk)
        rows = [geo[p, ROW_Y + m : ROW_Y + m + 1, cols] for m in range(16)]
        backward_messages(
            feats.at[slot], radial.at[slot], grads.at[slot], rows, g_radial.at[slot],
            g_feats.at[slot], channels, chunk,
        )

    def step(i, carry):
        t = 2 * i
        combine(t, 0)
        prepare(t + 1, 1)
        collect(t - 1, 1)
        combine(t + 1, 1)
        prepare(t + 2, 0)
        collect(t, 0)
        return carry

    prepare(0, 0)
    lax.fori_loop(0, total // 2, step, 0)
    collect(total // 2 * 2 - 1, 1)

    @pl.when(total % 2 == 1)
    def _():
        combine(total - 1, 0)
        collect(total - 1, 0)

    w_up_parts = [split(w_up[0]), split(w_up[1])]
    sums = [None, None] if first else [acc_up_in[0], acc_up_in[1]]
    for p in range(n):
        lifted_grads = [component(g_lifted[p], comp, 4) for comp in range(4)]
        for kind in range(2):
            count = 1 + 2 * kind
            own = lifted_grads[kind : kind + count]
            tall = jnp.concatenate([value.T for value in own], axis=0)
            back = dot1(tall, w_up_parts[kind], NT)
            for a, value in enumerate(rows_of(back, count)):
                x_grads[p][kind + a] = value
            x = x_refs[p][kind * atoms : (kind + count) * atoms, :]
            part = dot1(jnp.concatenate(own, axis=1), x)
            sums[kind] = part if sums[kind] is None else sums[kind] + part
    if last:
        both = acc_out[...]
        both = both[:, :hid] + both[:, hid:]
        paths = both.shape[0] // channels
        up_at = paths * hid
        end = up_at + 2 * channels
        flat[end:, :] = jnp.zeros_like(flat[end:, :])
        for path in range(paths):
            flat[path * hid : (path + 1) * hid, :] = component(both, path, paths).T
        for kind in range(2):
            row = up_at + kind * channels
            flat[row : row + channels, :] = sums[kind].T
        deal(flat, digits[0, 0], parts)
    else:
        for kind in range(2):
            g_up[kind] = sums[kind]
        g_out[...] = acc_out[...]


def mlp_backward_kernel(groups, *refs):
    counts, refs = refs[0], refs[1:]
    number = len(groups)
    geos, grads, refs = refs[:number], refs[number : 2 * number], refs[2 * number :]
    w_in, w_mid, small, acc_in, acc_mid = refs
    n_basis, hid = w_in.shape
    w_in_t = wcat3(w_in[...].T, 1)
    w_mid_t = [wcat3(w_mid[0].T, 1), wcat3(w_mid[1].T, 1)]
    w_mid_n = [wcat3(w_mid[0], 1), wcat3(w_mid[1], 1)]
    acc_in[...] = jnp.zeros_like(acc_in)
    acc_mid[...] = jnp.zeros_like(acc_mid)
    edges = geos[0].shape[2]
    lane = lax.broadcasted_iota(jnp.int32, (hid, edges), 1)

    def stack(v):
        high, low = split(v)
        return jnp.concatenate([high, low], axis=0)

    for slots, geo, grad in zip(groups, geos, grads):
        def one(p, slots=slots, geo=geo, grad=grad):
            k = slots[0]
            for at, slot in enumerate(slots):
                k = jnp.where(p == at, slot, k)
            bessel = geo[p, :8, :]
            h1, s1 = silu_parts(dot(w_in_t, basis_stack(bessel)))
            h2, s2 = silu_parts(dot(w_mid_t[0], cat3(h1, 0)))
            h3, s3 = silu_parts(dot(w_mid_t[1], cat3(h2, 0)))
            g3 = grad[p] * geo[p, ROW_ENV : ROW_ENV + 1, :]
            g3 = jnp.where(lane < counts[0, k], g3, 0.0)
            d3 = g3 * (s3 + h3 * (1.0 - s3))
            acc_mid[1] += dot(stack(h2), stack(d3), NT)
            d2 = dot(w_mid_n[1], cat3(d3, 0)) * (s2 + h2 * (1.0 - s2))
            acc_mid[0] += dot(stack(h1), stack(d2), NT)
            d1 = dot(w_mid_n[0], cat3(d2, 0)) * (s1 + h1 * (1.0 - s1))
            high = bessel.astype(BF16).astype(F32)
            basis = jnp.concatenate([high, bessel - high], axis=0).astype(BF16)
            acc_in[...] += dot(basis, stack(d1), NT)

        in_pairs(len(slots), one)

    def quadrants(v, rows):
        return v[:rows, :hid] + v[:rows, hid:] + v[rows:, :hid]

    small[hid + n_basis :, :] = jnp.zeros_like(small[hid + n_basis :, :])
    small[:hid, :] = jnp.concatenate([quadrants(acc_mid[layer], hid) for layer in range(2)], axis=1)
    basis_grad = quadrants(acc_in[...], n_basis)
    small[hid : hid + n_basis, :] = jnp.concatenate([basis_grad, jnp.zeros_like(basis_grad)], axis=1)


def call(kernel, out_shape, smem, scratch, args, name, us):
    specs = [SMEM] * smem + [VMEM] * (len(args) - smem)
    return call_with(kernel, out_shape, specs, scratch, args, name, us)


def call_with(kernel, out_shape, specs, scratch, args, name, us):
    return pl.pallas_call(
        kernel,
        out_shape=out_shape,
        in_specs=specs,
        out_specs=jax.tree.map(lambda _: VMEM, out_shape),
        scratch_shapes=scratch,
        compiler_params=pltpu.CompilerParams(vmem_limit_bytes=LIMIT),
        cost_estimate=pl.CostEstimate(
            flops=int(us * 5e8), bytes_accessed=int(us * 2e6), transcendentals=0
        ),
        name=name,
    )(*args)


def shape(*dims, dtype=F32):
    return jax.ShapeDtypeStruct(dims, dtype)


def shifted(value, steps):
    count = lax.axis_size("blk")
    return lax.ppermute(value, "blk", [(i, (i + steps) % count) for i in range(count)])


def stages_of(count):
    stages, stride = [], 1
    while stride < count:
        members = 4 if (count // stride) % 4 == 0 else 2
        stages.append((members, stride))
        stride *= members
    return stages


def exchange(values, stage):
    members, stride = stage
    count = lax.axis_size("blk")
    moved = [
        lax.ppermute(values[k], "blk", [(i, i ^ (k * stride)) for i in range(count)])
        for k in range(1, members)
    ]
    return [values[0]] + moved


def add_parts(groups, stages, at, digits):
    arrays = [part for parts, _ in groups for part in parts]
    counts = tuple((len(parts), tuple(sizes)) for parts, sizes in groups)
    total = sum(size for _, sizes in groups for size in sizes)
    out = stages[at + 1][0] if at + 1 < len(stages) else 1
    shapes = shape(total, LANES)
    if out > 1:
        shapes = tuple(shape(total // out, LANES) for _ in range(out))
    return call(
        functools.partial(add_kernel, at + 1, counts, out), shapes, 1,
        [pltpu.VMEM((total, LANES), F32)] if out > 1 else [], (digits, *arrays), f"add_{at}", 1,
    )


def join_parts(parts, sizes, stages, at, digits):
    members = stages[at][0]
    return call(
        functools.partial(join_kernel, at, members, sizes), shape(members * sum(sizes), LANES), 1,
        [], (digits, *parts), f"join_{at}", 1,
    )


def per_device(
    node_scalars, node_vectors, positions, species, edge_senders, edge_receivers, edge_shifts,
    bucket_counts, w_up, w_rad_in, w_rad_mid, w_rad_out, w_lin, w_sc_scalar, w_sc_vector, w_prod,
    w_skip, w_read, cot_scalars, cot_vectors, cot_energy,
):
    _, buckets, slots = edge_senders.shape
    send = edge_senders.reshape(buckets, 1, slots)
    recv = edge_receivers.reshape(buckets, 1, slots)
    shift = edge_shifts.reshape(3 * buckets, 1, slots)
    reach = (buckets - 1) // 2
    atoms, channels = node_scalars.shape
    hid, outs = w_rad_out.shape
    n_basis = w_rad_in.shape[0]
    n_spec = w_skip.shape[1]
    chunk = min(256, slots)
    blocks = lax.axis_size("blk")
    stages = stages_of(blocks)
    me = lax.axis_index("blk")
    digits = jnp.stack([(me // stride) % members for members, stride in stages]).reshape(1, -1)
    rows, at = [], 0
    height = up8(4 * atoms + 6)
    for piece in (node_scalars, node_vectors.reshape(3 * atoms, channels), positions,
                  species.reshape(1, atoms), cot_energy.reshape(1, atoms),
                  w_read.reshape(1, channels)):
        end = at + piece.shape[0]
        rows.append(jnp.pad(piece, ((at, height - end), (0, 0))).astype(F32))
        at = end
    packed = functools.reduce(jnp.add, rows)
    offsets = sorted([d for d in range(-reach, reach + 1) if d], key=abs)
    x_of = {reach: packed, **{reach + d: shifted(packed, -d) for d in offsets}}
    sc_s_t, sc_v_t = jnp.swapaxes(w_sc_scalar, 0, 1), jnp.swapaxes(w_sc_vector, 0, 1)

    skip_rows = 2 * n_spec * channels
    g_total, skip_s, skip_v, skip_gs, skip_gv, g_skip = call(
        skip_kernel,
        (shape(2, atoms, channels), shape(atoms, channels), shape(3, atoms, channels),
         shape(atoms, channels), shape(3, atoms, channels), shape(skip_rows, channels)),
        0, [],
        (packed, cot_scalars, cot_vectors, w_skip),
        "self_connection", 4,
    )

    def padded(rows):
        unit = 8 * blocks
        return -(-rows // unit) * unit

    node_rows = padded(skip_rows + 6 * channels + up8(9 * n_spec) + up8(5 * n_spec) + 8)
    edge_rows = padded(outs // channels * hid + 2 * channels)
    tail_unit = 8 * (blocks // stages[0][0])
    small_rows = -(-(hid + n_basis) // tail_unit) * tail_unit

    near = (reach - 1, reach + 1)
    far = tuple(k for k in range(buckets) if abs(k - reach) > 1)
    groups = [(reach,), near] + ([far] if far else [])
    most = [len(g) * (slots // chunk) for g in groups]
    first_parts = stages[0][0]
    acc = ()
    kept = []
    for at, group in enumerate(groups):
        n = len(group)
        last = at == len(groups) - 1
        base = len(groups[1]) if at == 2 else 0
        out_shapes = (
            shape(base + n, 4 * channels, 2 * atoms, dtype=BF16), shape(base + n, 2 * hid, slots, dtype=BF16),
            shape(base + n, GEO_ROWS, slots),
        )
        scratch = [
            pltpu.SMEM((3, most[at]), jnp.int32),
            pltpu.VMEM((2, 4 * channels, chunk), F32),
            pltpu.VMEM((2, outs, chunk), F32),
            pltpu.VMEM((2, 16 * channels, 2 * chunk), BF16),
        ]
        node_args, node_counts = (), None
        if last:
            node_args = (digits, w_lin, sc_s_t, sc_v_t, w_prod, g_total,
                         cot_vectors, skip_s, skip_v, g_skip)
            node_outs = (
                shape(atoms, channels), shape(3, atoms, channels), shape(1, atoms),
                shape(16 * channels, 2 * atoms, dtype=BF16),
                *[shape(node_rows // first_parts, LANES)] * first_parts,
            )
            node_counts = len(node_args), len(node_outs)
            scratch = [
                pltpu.VMEM((16 * channels, atoms), F32), pltpu.VMEM((node_rows, LANES), F32)
            ] + scratch
            out_shapes = node_outs + out_shapes
        else:
            out_shapes = (shape(16 * channels, atoms),) + out_shapes
        args = (
            bucket_counts, send, recv, shift, packed, *[x_of[k] for k in group], w_up, w_rad_in,
            w_rad_mid, w_rad_out, *acc, *(kept[-1] if base else ()), *node_args,
        )
        specs = [SMEM] + [VMEM] * (len(args) - 1)
        if last:
            specs[len(args) - len(node_args)] = SMEM
        result = call_with(
            functools.partial(forward_kernel, base, group, chunk, at == 0, node_counts), out_shapes,
            specs, scratch, args, f"edges_{at}", 5 * n + (6 if last else 0),
        )
        kept.append(result[-3:])
        if last:
            new_s, new_v, energy, grad_amp = result[:4]
            node_parts = result[4 : 4 + first_parts]
        else:
            acc = result[:1]

    tie = lax.optimization_barrier
    node_parts = exchange(node_parts, stages[0])
    others = tuple(k for group in groups[1:] for k in group)
    sums = ()
    n_early = len(others) // 2
    grads_hidden = []
    home = []
    for group, (lifted, hidden, geo) in ((others, kept[-1]), (groups[0], kept[0])):
        n = len(group)
        first, last = not sums, bool(sums)
        if last:
            final = (shape(edge_rows // first_parts, LANES),) * first_parts
        else:
            final = (shape(outs, 2 * hid), shape(2, channels, channels))
        args = (
            bucket_counts, digits, send, recv, grad_amp, geo, lifted, hidden,
            *[x_of[k] for k in group], w_up, w_rad_out, *sums,
        )
        result = call(
            functools.partial(backward_kernel, group, chunk, first, last, first_parts),
            (*[shape(4, atoms, channels) for _ in group], shape(n, hid, slots), *final), 2,
            ([pltpu.VMEM((edge_rows, LANES), F32)] if last else [])
            + [
                pltpu.SMEM((3, n * (slots // chunk)), jnp.int32),
                pltpu.VMEM((2, 4 * channels, chunk), F32),
                pltpu.VMEM((2, outs, chunk), F32),
                pltpu.VMEM((2, 16 * channels, chunk), F32),
                pltpu.VMEM((2, outs, 2 * chunk), BF16),
                pltpu.VMEM((2, 4 * channels, 2 * chunk), BF16),
                pltpu.VMEM((n, 4 * channels, atoms), F32),
                pltpu.VMEM((outs, 2 * hid), F32),
            ],
            args, "edges_back_own" if last else "edges_back", 6 * n,
        )
        if first:
            result, node_parts = tie((result, node_parts))
            away = [(k - reach, value) for k, value in zip(group, result[:n])]
            away.sort(key=lambda pair: -abs(pair[0]))
            home = [shifted(value, offset) for offset, value in away]
        else:
            early, late = home[: n_early], home[n_early:]
            result, early = tie((result, early))
            edge_parts = exchange(result[n + 1 :], stages[0])
            home = early + [result[0]]
        grads_hidden.append(result[n])
        sums = result[n + 1 :]
    small = call(
        functools.partial(mlp_backward_kernel, (others, groups[0])), shape(small_rows, LANES), 1,
        [pltpu.VMEM((2 * n_basis, 2 * hid), F32), pltpu.VMEM((2, 2 * hid, 2 * hid), F32)],
        (bucket_counts, kept[-1][2], kept[0][2], *grads_hidden, w_rad_in, w_rad_mid),
        "radial_back", 7,
    )
    small, edge_parts, late = tie((small, edge_parts, late))
    home = home + late
    sizes = [node_rows // first_parts, edge_rows // first_parts, small_rows]
    groups = [(node_parts, sizes[:1]), (edge_parts, sizes[1:2]), ([small], sizes[2:])]
    whole = add_parts(groups, stages, 0, digits)
    for at in range(1, len(stages)):
        sizes = [size // stages[at][0] for size in sizes]
        whole = add_parts([(exchange(whole, stages[at]), sizes)], stages, at, digits)
    for at in reversed(range(1, len(stages))):
        parts = exchange([whole] * stages[at][0], stages[at])
        whole = join_parts(parts, sizes, stages, at, digits)
        sizes = [size * stages[at][0] for size in sizes]
    parts = exchange([whole] * first_parts, stages[0])
    g_skip, g_lin, g_prod, g_sc_s, g_sc_v, g_read, g_out, g_up, g_mid, g_in = call(
        functools.partial(finish_kernel, first_parts, sizes[:2], n_spec),
        (shape(skip_rows, channels), shape(4 * channels, channels), shape(2 * channels, channels),
         shape(9, n_spec, channels), shape(5, n_spec, channels), shape(1, channels),
         shape(hid, outs), shape(2 * channels, channels), shape(2, hid, hid), shape(n_basis, hid)),
        1,
        [pltpu.VMEM((node_rows + edge_rows, LANES), F32),
         pltpu.VMEM((first_parts, small_rows, LANES), F32)],
        (digits, *parts), "finish", 2,
    )
    gx = home[0]
    for part in home[1:]:
        gx = gx + part
    return (
        new_s, new_v, energy.reshape(-1), gx[0] + skip_gs, gx[1:] + skip_gv,
        g_up.reshape(1, 2, channels, channels), g_in[None], g_mid[None], g_out[None],
        g_lin.reshape(1, 4, channels, channels), jnp.swapaxes(g_sc_s, 0, 1)[None],
        jnp.swapaxes(g_sc_v, 0, 1)[None], g_prod.reshape(1, 2, channels, channels),
        g_skip.reshape(1, 2, n_spec, channels, channels), g_read,
    )


def solution(mesh):
    atoms = ("cell", "blk")
    in_specs = (
        P(atoms, None), P(None, atoms, None), P(None, atoms), P(atoms), P(atoms, None, None),
        P(atoms, None, None), P(atoms, None, None, None), P(atoms, None),
        P(), P(), P(), P(), P(), P(), P(), P(), P(), P(),
        P(atoms, None), P(None, atoms, None), P(atoms),
    )
    out_specs = (
        P(atoms, None), P(None, atoms, None), P(atoms), P(atoms, None), P(None, atoms, None),
        P("cell", None, None, None), P("cell", None, None), P("cell", None, None, None),
        P("cell", None, None), P("cell", None, None, None), P("cell", None, None, None),
        P("cell", None, None, None), P("cell", None, None, None),
        P("cell", None, None, None, None), P("cell", None),
    )
    return jax.shard_map(
        per_device, mesh=mesh, in_specs=in_specs, out_specs=out_specs, check_vma=False
    )
```

```python
import functools
import math

import jax
import jax.numpy as jnp
from jax import lax
from jax.experimental import pallas as pl
from jax.experimental.pallas import tpu as pltpu
from jax.sharding import PartitionSpec as P

CUTOFF = 5.0
SOFTEN = 0.1
NEIGH = 0.17677669529663687
F32 = jnp.float32
BF16 = jnp.bfloat16
LANES = 128
VMEM = pl.BlockSpec(memory_space=pltpu.VMEM)
SMEM = pl.BlockSpec(memory_space=pltpu.SMEM)
LIMIT = 20 * 1024 * 1024

NN = (((1,), (0,)), ((), ()))
NT = (((1,), (1,)), ((), ()))


BLOCK = 16


def row_of(comp, count, channel):
    return (channel // BLOCK * count + comp) * BLOCK


def by_block(parts):
    channels = parts[0].shape[0]
    return jnp.concatenate(
        [part[c : c + BLOCK] for c in range(0, channels, BLOCK) for part in parts], axis=0
    )


def component(value, comp, count):
    step = count * BLOCK
    at = comp * BLOCK
    return jnp.concatenate(
        [value[r + at : r + at + BLOCK] for r in range(0, value.shape[0], step)], axis=0
    )


def split(v):
    high = v.astype(BF16)
    return high, (v - high.astype(F32)).astype(BF16)


def dot(a, b, dims=NN):
    return lax.dot_general(a, b, dims, preferred_element_type=F32)


def dot3(a, b, dims=NN):
    ah, al = a if isinstance(a, tuple) else split(a)
    bh, bl = b if isinstance(b, tuple) else split(b)
    return dot(ah, bh, dims) + (dot(ah, bl, dims) + dot(al, bh, dims))


def dot1(a, b, dims=NN):
    ah, al = a if isinstance(a, tuple) else split(a)
    bh, bl = b if isinstance(b, tuple) else split(b)
    left = jnp.concatenate([ah, ah, al], axis=1)
    right = jnp.concatenate([bh, bl, bh], axis=dims[0][1][0])
    return dot(left, right, dims)


def rows_of(v, count):
    step = v.shape[0] // count
    return [v[at * step : (at + 1) * step] for at in range(count)]


def columns_of(v, count):
    step = v.shape[1] // count
    return [v[:, at * step : (at + 1) * step] for at in range(count)]


def cat3(v, axis):
    high, low = split(v)
    return jnp.concatenate([high, high, low], axis=axis)


def wcat3(v, axis):
    high, low = split(v)
    return jnp.concatenate([high, low, high], axis=axis)


def column(row, width):
    return jnp.broadcast_to(row, (width, row.shape[1])).T


ROW_Y = 8
ROW_ENV = 24
GEO_ROWS = 32


def write_geometry(geo, base, slots, counts, send, recv, shift, tables, own_pos):
    buckets, _, edges = send.shape
    bucket_of = lax.broadcasted_iota(jnp.int32, (buckets, LANES), 0)
    filled = jnp.zeros((buckets, LANES), jnp.int32)
    for k in slots:
        filled = jnp.where(bucket_of == k, counts[0, k], filled)
    own = [jnp.broadcast_to(own_pos[a : a + 1, :], (buckets, LANES)) for a in range(3)]
    lane = lax.broadcasted_iota(jnp.int32, (buckets, LANES), 1)
    for block in range(edges // LANES):
        cols = slice(block * LANES, (block + 1) * LANES)

        def put(row, value):
            for p, k in enumerate(slots, base):
                geo[p, row : row + 1, cols] = value[k : k + 1]

        from_idx = jnp.concatenate([send[k, :, cols] for k in range(buckets)], axis=0)
        to_idx = jnp.concatenate([recv[k, :, cols] for k in range(buckets)], axis=0)
        rel = []
        for a in range(3):
            there = jnp.take_along_axis(tables[a], from_idx, axis=1, mode="promise_in_bounds")
            here = jnp.take_along_axis(own[a], to_idx, axis=1, mode="promise_in_bounds")
            moved = jnp.concatenate([shift[3 * k + a, :, cols] for k in range(buckets)], axis=0)
            rel.append(there - here + moved.astype(F32))
        dist = jnp.sqrt(rel[0] * rel[0] + rel[1] * rel[1] + rel[2] * rel[2] + SOFTEN)
        inverse = 1.0 / dist
        x, y, z = (r * inverse for r in rel)
        angle = dist * (math.pi / CUTOFF)
        sine, twice = jnp.sin(angle), 2.0 * jnp.cos(angle)
        scale = math.sqrt(2.0 / CUTOFF) * inverse
        before, now = jnp.zeros_like(sine), sine
        for n in range(8):
            put(n, now * scale)
            before, now = now, twice * now - before
        xx, yy, zz = x * x, y * y, z * z
        planar = xx + yy
        rows = [
            jnp.ones_like(x),
            math.sqrt(3.0) * x,
            math.sqrt(3.0) * y,
            math.sqrt(3.0) * z,
            math.sqrt(15.0) * x * y,
            math.sqrt(15.0) * y * z,
            0.5 * math.sqrt(5.0) * (2.0 * zz - planar),
            math.sqrt(15.0) * x * z,
            0.5 * math.sqrt(15.0) * (xx - yy),
            math.sqrt(35.0 / 8.0) * (3.0 * xx - yy) * y,
            math.sqrt(105.0) * x * y * z,
            math.sqrt(21.0 / 8.0) * y * (4.0 * zz - planar),
            0.5 * math.sqrt(7.0) * z * (2.0 * zz - 3.0 * planar),
            math.sqrt(21.0 / 8.0) * x * (4.0 * zz - planar),
            0.5 * math.sqrt(105.0) * z * (xx - yy),
            math.sqrt(35.0 / 8.0) * (xx - 3.0 * yy) * x,
        ]
        for m, row in enumerate(rows):
            put(ROW_Y + m, row)
        q = dist * (1.0 / CUTOFF)
        q6 = q * q * q * q * q * q
        envelope = 1.0 - 28.0 * q6 + 48.0 * q6 * q - 21.0 * q6 * q * q
        put(ROW_ENV, jnp.where(lane + block * LANES < filled, envelope, 0.0))


def one_hot(index_row, atoms):
    edges = index_row.shape[1]
    atom = lax.broadcasted_iota(jnp.int32, (atoms, edges), 0)
    return jnp.where(atom == index_row, 1.0, 0.0).astype(BF16)


def twice(v, axis):
    return jnp.concatenate([v, v], axis=axis)


def silu_parts(v):
    gate = 1.0 / (1.0 + jnp.exp(-v))
    return v * gate, gate


def basis_stack(bessel):
    high = bessel.astype(BF16).astype(F32)
    return jnp.concatenate([high, high, bessel - high], axis=0).astype(BF16)


def lift(x_ref, w_up_t, out):
    atoms = out.shape[1] // 2
    scalars = dot1(w_up_t[0], x_ref[:atoms, :], NT)
    vectors = dot1(w_up_t[1], x_ref[atoms : 4 * atoms, :], NT)
    parts = [split(value) for value in [scalars] + columns_of(vectors, 3)]
    out[:, :atoms] = by_block([high for high, _ in parts])
    out[:, atoms:] = by_block([low for _, low in parts])


def radial_weights(w_out, channels):
    w_t = w_out[...].T
    return by_block([w_t[at : at + channels] for at in range(0, w_t.shape[0], channels)])


def list_chunks(table, slots, counts, chunk, base=0):
    table[0, 0], table[1, 0], table[2, 0] = base, slots[0], 0
    total = 0
    for p, k in enumerate(slots, base):
        number = (counts[0, k] + chunk - 1) // chunk

        def note(j, at, p=p, k=k):
            table[0, at] = p
            table[1, at] = k
            table[2, at] = j * chunk
            return at + 1

        total = lax.fori_loop(0, number, note, total)
    return total


def chunk_at(table, t, chunk):
    return table[0, t], table[1, t], pl.ds(pl.multiple_of(table[2, t], chunk), chunk)


def forward_messages(feats, radial, geo_rows, out, channels, edges):
    ys = []
    for half in range(edges // LANES):
        cols = slice(half * LANES, (half + 1) * LANES)
        ys.append([jnp.broadcast_to(row[:, cols], (BLOCK, LANES)) for row in geo_rows])
    for c in range(0, channels, BLOCK):
        for half in range(edges // LANES):
            cols = slice(half * LANES, (half + 1) * LANES)
            low_cols = slice(edges + half * LANES, edges + (half + 1) * LANES)
            y = ys[half]

            def feat(k):
                at = row_of(k, 4, c)
                return feats[at : at + BLOCK, cols]

            def rad(k):
                at = row_of(k, 7, c)
                return radial[at : at + BLOCK, cols]

            def put(comp, value):
                high, low = split(value)
                at = row_of(comp, 16, c)
                out[at : at + BLOCK, cols] = high
                out[at : at + BLOCK, low_cols] = low

            s, v = feat(0), [feat(1), feat(2), feat(3)]
            inner = y[1] * v[0] + y[2] * v[1] + y[3] * v[2]
            put(0, rad(0) * s + rad(4) * inner)
            first, fifth, sixth = rad(1) * s, rad(5), rad(6)
            put(1, first * y[1] + fifth * v[0] + sixth * (y[2] * v[2] - y[3] * v[1]))
            put(2, first * y[2] + fifth * v[1] + sixth * (y[3] * v[0] - y[1] * v[2]))
            put(3, first * y[3] + fifth * v[2] + sixth * (y[1] * v[1] - y[2] * v[0]))
            second = rad(2) * s
            for m in range(4, 9):
                put(m, second * y[m])
            third = rad(3) * s
            for m in range(9, 16):
                put(m, third * y[m])


def in_pairs(count, one):
    if count > 1:
        def pair(i, carry):
            one(2 * i)
            one(2 * i + 1)
            return carry

        if count < 4:
            pair(0, 0)
        else:
            lax.fori_loop(0, count // 2, pair, 0)
    if count % 2:
        one(count - 1)


def radial_hidden(base, count, w_in, w_mid, geo, hidden_out):
    hid = w_in.shape[1]
    w_in_t = wcat3(w_in[...].T, 1)
    w_mid_t = [wcat3(w_mid[0].T, 1), wcat3(w_mid[1].T, 1)]

    def one(at):
        p = base + at
        h, _ = silu_parts(dot(w_in_t, basis_stack(geo[p, :8, :])))
        h, _ = silu_parts(dot(w_mid_t[0], cat3(h, 0)))
        h, _ = silu_parts(dot(w_mid_t[1], cat3(h, 0)))
        high, low = split(h * geo[p, ROW_ENV : ROW_ENV + 1, :])
        hidden_out[p, :hid, :] = high
        hidden_out[p, hid:, :] = low

    in_pairs(count, one)


def edge_forward(
    base, slots, chunk, counts, send, recv, shift, own_pos, tables, x_refs, w_up, w_in, w_mid, w_out,
    lifted_out, hidden_out, geo, acc, table, feats, radial, messages,
):
    channels, atoms = w_up.shape[1], acc.shape[1]
    hid = w_in.shape[1]
    total = list_chunks(table, slots, counts, chunk, base)
    write_geometry(geo, base, slots, counts, send, recv, shift, tables, own_pos)
    w_up_t = [split(w_up[0].T), split(w_up[1].T)]
    for p in range(len(slots)):
        lift(x_refs[p], w_up_t, lifted_out.at[base + p])
    radial_hidden(base, len(slots), w_in, w_mid, geo, hidden_out)
    w_out_t = wcat3(radial_weights(w_out, channels), 1)
    messages[1] = jnp.zeros_like(messages[1])

    def prepare(t, slot):
        p, k, cols = chunk_at(table, jnp.minimum(t, total - 1), chunk)
        high, low = hidden_out[p, :hid, cols], hidden_out[p, hid:, cols]
        radial[slot] = dot(w_out_t, jnp.concatenate([high, high, low], axis=0))
        from_hot = one_hot(send[k, :, cols], atoms)
        feats[slot] = dot(lifted_out[p], twice(from_hot, 0))

    def collect(t, slot):
        _, k, cols = chunk_at(table, jnp.maximum(t, 0), chunk)
        to_hot = one_hot(recv[k, :, cols], atoms)
        acc[...] += dot(messages[slot], twice(to_hot, 1), NT)

    def combine(t, slot):
        p, _, cols = chunk_at(table, t, chunk)
        rows = [geo[p, ROW_Y + m : ROW_Y + m + 1, cols] for m in range(16)]
        forward_messages(
            feats.at[slot], radial.at[slot], rows, messages.at[slot], channels, chunk
        )

    def step(i, carry):
        t = 2 * i
        combine(t, 0)
        prepare(t + 1, 1)
        collect(t - 1, 1)
        combine(t + 1, 1)
        prepare(t + 2, 0)
        collect(t, 0)
        return carry

    prepare(0, 0)
    lax.fori_loop(0, total // 2, step, 0)
    collect(total // 2 * 2 - 1, 1)

    @pl.when(total % 2 == 1)
    def _():
        combine(total - 1, 0)
        collect(total - 1, 0)


def forward_kernel(base, slots, chunk, first, node_counts, *refs):
    n = len(slots)
    counts, send, recv, shift, refs = *refs[:4], refs[4:]
    x_own, x_refs, refs = refs[0], refs[1 : 1 + n], refs[1 + n :]
    w_up, w_in, w_mid, w_out, refs = *refs[:4], refs[4:]
    atoms = w_up.shape[1]
    at = 4 * atoms
    if not first:
        acc_in, refs = refs[0], refs[1:]
    before, refs = refs[: 3 if base else 0], refs[3 if base else 0 :]
    if node_counts:
        n_in, n_out = node_counts
        node_in, node_out, refs = refs[:n_in], refs[n_in : n_in + n_out], refs[n_in + n_out :]
        lifted_out, hidden_out, geo, acc, flat, table, feats, radial, messages = refs
    else:
        acc, lifted_out, hidden_out, geo, table, feats, radial, messages = refs
    if first:
        acc[...] = jnp.zeros_like(acc)
    else:
        acc[...] = acc_in[...]
    for ref, out in zip(before, (lifted_out, hidden_out, geo)):
        out[:base] = ref[...]
    tables = []
    for a in range(3):
        rows = [x_own[at + a : at + a + 1, :]] * send.shape[0]
        for k, ref in zip(slots, x_refs):
            rows[k] = ref[at + a : at + a + 1, :]
        tables.append(jnp.concatenate(rows, axis=0))
    edge_forward(
        base, slots, chunk, counts, send, recv, shift, x_own.at[at : at + 8], tables, x_refs, w_up, w_in,
        w_mid, w_out, lifted_out, hidden_out, geo, acc, table, feats, radial, messages,
    )
    if node_counts:
        rows = [x_own[at + 3 : at + 4, :], x_own[at + 5 : at + 6, :]]
        node_stage(acc, flat, *rows, *node_in, *node_out)


def deal(flat, digit, parts):
    rows = parts[0].shape[0]
    for k, part in enumerate(parts):
        at = pl.multiple_of((digit ^ k) * rows, 8)
        part[...] = flat[pl.ds(at, rows), :]


def add_kernel(stage, groups, n_out, *refs):
    digits, refs = refs[0], refs[1:]
    totals = []
    for count, sizes in groups:
        total = functools.reduce(jnp.add, [part[...] for part in refs[:count]])
        refs = refs[count:]
        at = 0
        for size in sizes:
            totals.append(total[at : at + size])
            at += size
    if n_out == 1:
        at = 0
        for total in totals:
            refs[0][at : at + total.shape[0], :] = total
            at += total.shape[0]
        return
    outs, scratch = refs[:n_out], refs[n_out]
    at, out_at = 0, 0
    for total in totals:
        size = total.shape[0]
        scratch[at : at + size, :] = total
        rows = size // n_out
        for k, out in enumerate(outs):
            first = pl.multiple_of(at + (digits[0, stage] ^ k) * rows, 8)
            out[out_at : out_at + rows, :] = scratch[pl.ds(first, rows), :]
        at += size
        out_at += rows


def join_into(out, digit, inputs, segments):
    radix = len(inputs)
    at, out_at = 0, 0
    for rows, blocks in segments:
        for _ in range(blocks):
            for k, part in enumerate(inputs):
                first = pl.multiple_of(out_at + (digit ^ k) * rows, 8)
                out[pl.ds(first, rows), :] = part[at : at + rows, :]
            at += rows
            out_at += rows * radix


def join_kernel(stage, radix, segments, tail, *refs):
    digits, inputs, out = refs[0], refs[1 : 1 + radix], refs[1 + radix]
    digit = digits[0, stage]
    join_into(out, digit, inputs, segments)
    if tail:
        store = refs[2 + radix]
        for k, part in enumerate(inputs):
            store[digit ^ k] = part[part.shape[0] - tail :, :]
        total = store[0]
        for member in range(1, radix):
            total = total + store[member]
        out[out.shape[0] - tail :, :] = total


def finish_kernel(stage, radix, segments, n_spec, *refs):
    digits, inputs, refs = refs[0], refs[1 : 1 + radix], refs[1 + radix :]
    node_outs, (g_out, g_up, g_mid, g_in, flat) = refs[:6], refs[6:]
    join_into(flat, digits[0, stage], inputs, segments)
    ends = []
    for rows, blocks in segments:
        ends.append((ends[-1] if ends else 0) + rows * blocks * radix)
    at = 0
    for out in node_outs:
        if len(out.shape) == 3:
            for p in range(out.shape[0]):
                out[p] = flat[at + p * n_spec : at + (p + 1) * n_spec, :]
            at += up8(out.shape[0] * n_spec)
        else:
            out[...] = flat[at : at + out.shape[0], :]
            at += up8(out.shape[0])
    at = ends[0]
    hid, n_basis = g_out.shape[0], g_in.shape[0]
    for path in range(g_out.shape[1] // LANES):
        g_out[:, path * LANES : (path + 1) * LANES] = flat[at : at + hid, :]
        at += hid
    g_up[...] = flat[at : at + g_up.shape[0], :]
    small = flat[ends[1] : ends[2], :]
    g_mid[0] = small[:hid, :hid]
    g_mid[1] = small[:hid, hid:]
    g_in[...] = small[hid : hid + n_basis, :hid]


DEGREE = (0, 1, 1, 1, 2, 2, 2, 2, 2, 3, 3, 3, 3, 3, 3, 3)


def species_hot(species_row, count):
    atoms = species_row.shape[1]
    which = lax.broadcasted_iota(jnp.int32, (count, atoms), 0)
    return jnp.where(which == species_row, 1.0, 0.0)


def up8(rows):
    return (rows + 7) // 8 * 8


def node_stage(
    acc, flat, species, w_read, digits, w_lin, w_sc_s, w_sc_v, w_prod, g_total, cot_v, skip_s,
    skip_v, g_skip, new_s, new_v, energy, grad_amp, *parts,
):
    channels, atoms = w_lin.shape[1], acc.shape[1]
    n_spec = w_sc_s.shape[1]
    flat[g_skip.shape[0] :, :] = jnp.zeros_like(flat[g_skip.shape[0] :, :])
    flat[: g_skip.shape[0], :] = g_skip[...]
    lin_at = g_skip.shape[0]
    prod_at = lin_at + 4 * channels
    sc_s_at = prod_at + 2 * channels
    sc_v_at = sc_s_at + up8(9 * n_spec)
    read_at = sc_v_at + up8(5 * n_spec)
    members = [[m for m in range(16) if DEGREE[m] == l] for l in range(4)]
    amp_t = [component(acc, m, 16) * NEIGH for m in range(16)]
    amp_t_parts = [split(v) for v in amp_t]
    b = []
    for l in range(4):
        high = jnp.concatenate([amp_t_parts[m][0].T for m in members[l]], axis=0)
        low = jnp.concatenate([amp_t_parts[m][1].T for m in members[l]], axis=0)
        stacked = dot(jnp.concatenate([high, high, low], axis=1), wcat3(w_lin[l], 0))
        b.extend(stacked[j * atoms : (j + 1) * atoms] for j in range(len(members[l])))
    b0 = b[0]
    n1 = b[1] * b[1] + b[2] * b[2] + b[3] * b[3]
    n2 = b[4] * b[4] + b[5] * b[5] + b[6] * b[6] + b[7] * b[7] + b[8] * b[8]
    n3 = functools.reduce(jnp.add, [b[m] * b[m] for m in range(9, 16)])
    species_col = column(species, channels)
    masks = [species_col == float(s) for s in range(n_spec)]

    def per_atom(w, p):
        value = jnp.broadcast_to(w[p, :1, :], (atoms, channels))
        for s in range(1, n_spec):
            value = jnp.where(masks[s], w[p, s : s + 1, :], value)
        return value

    ws = [per_atom(w_sc_s, p) for p in range(9)]
    wv = [per_atom(w_sc_v, p) for p in range(5)]
    sq = b0 * b0
    terms = [b0, sq, n1, n2, n3, sq * b0, b0 * n1, b0 * n2, b0 * n3]
    mixed = functools.reduce(jnp.add, [w * t for w, t in zip(ws, terms)])
    factors = [None, b0, sq, n1, n2]
    factor = wv[0]
    for p in range(1, 5):
        factor = factor + wv[p] * factors[p]
    prod_parts = [split(w_prod[0]), split(w_prod[1])]
    out_s = dot1(mixed, prod_parts[0]) + skip_s[...]
    new_s[...] = out_s
    mixed_v = jnp.concatenate([b[1 + a] * factor for a in range(3)], axis=0)
    for a, value in enumerate(rows_of(dot1(mixed_v, prod_parts[1]), 3)):
        new_v[a] = value + skip_v[a]
    energy[...] = dot3(jnp.broadcast_to(w_read, (8, channels)), out_s, NT)[:1]
    cot_e = g_total[1]
    flat[read_at : read_at + 1, :] = jnp.sum(out_s * cot_e, axis=0, keepdims=True)

    g_s = split(g_total[0])
    g_v = split(jnp.concatenate([cot_v[a] for a in range(3)], axis=0))
    flat[prod_at : prod_at + channels, :] = dot1(mixed.T, g_s)
    flat[prod_at + channels : sc_s_at, :] = dot1(mixed_v.T, g_v)
    g_mixed = dot1(g_s, prod_parts[0], NT)
    g_mixed_v = rows_of(dot1(g_v, prod_parts[1], NT), 3)
    g_factor = functools.reduce(jnp.add, [g_mixed_v[a] * b[1 + a] for a in range(3)])

    hot = species_hot(species.astype(jnp.int32), 8).astype(BF16)
    values = [g_mixed * terms[p] for p in range(9)]
    values += [g_factor] + [g_factor * factors[p] for p in range(1, 5)]
    high, low = split(jnp.concatenate(values, axis=1))
    by_species = dot(twice(hot, 1), jnp.concatenate([high, low], axis=0))
    for p, value in enumerate(columns_of(by_species, len(values))):
        row = sc_s_at + p * n_spec if p < 9 else sc_v_at + (p - 9) * n_spec
        flat[row : row + n_spec, :] = value[:n_spec]

    g_b0 = g_mixed * (
        ws[0] + 2.0 * b0 * ws[1] + 3.0 * sq * ws[5] + n1 * ws[6] + n2 * ws[7] + n3 * ws[8]
    ) + g_factor * (wv[1] + 2.0 * b0 * wv[2])
    g_n1 = 2.0 * (g_mixed * (ws[2] + b0 * ws[6]) + g_factor * wv[3])
    g_n2 = 2.0 * (g_mixed * (ws[3] + b0 * ws[7]) + g_factor * wv[4])
    g_n3 = 2.0 * (g_mixed * (ws[4] + b0 * ws[8]))
    g_b = [g_b0]
    for a in range(3):
        g_b.append(g_mixed_v[a] * factor + g_n1 * b[1 + a])
    for m in range(4, 9):
        g_b.append(g_n2 * b[m])
    for m in range(9, 16):
        g_b.append(g_n3 * b[m])
    g_b_parts = [split(v) for v in g_b]
    grads = []
    for l in range(4):
        row = lin_at + l * channels
        high = jnp.concatenate([g_b_parts[m][0] for m in members[l]], axis=0)
        low = jnp.concatenate([g_b_parts[m][1] for m in members[l]], axis=0)
        amp_high = jnp.concatenate([amp_t_parts[m][0] for m in members[l]], axis=1)
        amp_low = jnp.concatenate([amp_t_parts[m][1] for m in members[l]], axis=1)
        flat[row : row + channels, :] = dot(
            jnp.concatenate([amp_high, amp_high, amp_low], axis=1),
            jnp.concatenate([high, low, high], axis=0),
        )
        back = dot(wcat3(w_lin[l], 1), jnp.concatenate([high, high, low], axis=1), NT) * NEIGH
        grads.extend(
            split(back[:, j * atoms : (j + 1) * atoms]) for j in range(len(members[l]))
        )
    grad_amp[:, :atoms] = by_block([high for high, _ in grads])
    grad_amp[:, atoms:] = by_block([low for _, low in grads])
    deal(flat, digits[0, 0], parts)


def skip_kernel(
    x_own, cot_s, cot_v, w_skip,
    g_total, skip_s, skip_v, skip_gs, skip_gv, g_skip,
):
    atoms, channels = cot_s.shape
    n_spec = w_skip.shape[1]

    at = 4 * atoms + 3
    species, cot_e, w_read = x_own[at : at + 1, :], x_own[at + 1 : at + 2, :], x_own[at + 2 : at + 3, :]
    cot_col = column(cot_e, channels)
    total = cot_s[...] + cot_col * w_read
    g_total[0] = total
    g_total[1] = cot_col
    species_col = column(species, channels)

    def pick(values, masks):
        result = values[0]
        for s in range(1, n_spec):
            result = jnp.where(masks[s], values[s], result)
        return result

    for kind in range(2):
        count = 1 + 2 * kind
        masks = [jnp.concatenate([species_col == float(s)] * count, axis=0) for s in range(n_spec)]
        x = x_own[kind * atoms : (kind + count) * atoms, :]
        g = jnp.concatenate([cot_v[a] for a in range(3)], axis=0) if kind else total
        weights = [split(w_skip[kind, s]) for s in range(n_spec)]
        wide = tuple(jnp.concatenate([w[i] for w in weights], axis=1) for i in range(2))
        tall = tuple(jnp.concatenate([w[i] for w in weights], axis=0) for i in range(2))
        forward = pick(columns_of(dot1(x, wide), n_spec), masks)
        back = pick(columns_of(dot1(g, tall, NT), n_spec), masks)
        if kind:
            for a in range(3):
                skip_v[a] = forward[a * atoms : (a + 1) * atoms]
                skip_gv[a] = back[a * atoms : (a + 1) * atoms]
        else:
            skip_s[...] = forward
            skip_gs[...] = back
        apart = jnp.concatenate([jnp.where(mask, g, 0.0) for mask in masks], axis=1)
        sums = dot1(x.T, apart)
        for s, value in enumerate(columns_of(sums, n_spec)):
            row = (kind * n_spec + s) * channels
            g_skip[row : row + channels, :] = value


def backward_messages(feats, radial, grads, geo_rows, g_radial, g_feats, channels, edges):
    ys = []
    for half in range(edges // LANES):
        cols = slice(half * LANES, (half + 1) * LANES)
        ys.append([jnp.broadcast_to(row[:, cols], (BLOCK, LANES)) for row in geo_rows])
    for c in range(0, channels, BLOCK):
        for half in range(edges // LANES):
            cols = slice(half * LANES, (half + 1) * LANES)
            low_cols = slice(edges + half * LANES, edges + (half + 1) * LANES)
            y = ys[half]

            def load(ref, k, count):
                at = row_of(k, count, c)
                return ref[at : at + BLOCK, cols]

            def grad(m):
                return load(grads, m, 16)

            def rad(k):
                return load(radial, k, 7)

            def put(ref, comp, count, value):
                high, low = split(value)
                at = row_of(comp, count, c)
                ref[at : at + BLOCK, cols] = high
                ref[at : at + BLOCK, low_cols] = low

            s = load(feats, 0, 4)
            third = y[9] * grad(9)
            for m in range(10, 16):
                third = third + y[m] * grad(m)
            put(g_radial, 3, 7, s * third)
            second = y[4] * grad(4)
            for m in range(5, 9):
                second = second + y[m] * grad(m)
            put(g_radial, 2, 7, s * second)
            g = [grad(1 + a) for a in range(3)]
            first = y[1] * g[0] + y[2] * g[1] + y[3] * g[2]
            put(g_radial, 1, 7, s * first)
            zero = grad(0)
            put(g_radial, 0, 7, s * zero)
            put(
                g_feats, 0, 4,
                rad(0) * zero + rad(1) * first + rad(2) * second + rad(3) * third,
            )
            v = [load(feats, 1 + a, 4) for a in range(3)]
            put(g_radial, 4, 7, (y[1] * v[0] + y[2] * v[1] + y[3] * v[2]) * zero)
            put(g_radial, 5, 7, v[0] * g[0] + v[1] * g[1] + v[2] * g[2])
            cross = [
                g[1] * y[3] - g[2] * y[2],
                g[2] * y[1] - g[0] * y[3],
                g[0] * y[2] - g[1] * y[1],
            ]
            put(g_radial, 6, 7, v[0] * cross[0] + v[1] * cross[1] + v[2] * cross[2])
            fourth, fifth, sixth = rad(4) * zero, rad(5), rad(6)
            for a in range(3):
                put(g_feats, 1 + a, 4, fourth * y[1 + a] + fifth * g[a] + sixth * cross[a])


def backward_kernel(slots, chunk, first, last, n_parts, *refs):
    n = len(slots)
    counts, digits, send, recv, grad_amp = refs[:5]
    geo, lifted, hidden = refs[5:8]
    x_refs, refs = refs[8 : 8 + n], refs[8 + n :]
    w_up, w_out, refs = refs[0], refs[1], refs[2:]
    if not first:
        acc_out_in, acc_up_in, refs = refs[0], refs[1], refs[2:]
    x_grads, g_hidden, refs = refs[:n], refs[n], refs[n + 1 :]
    if last:
        parts, refs = refs[:n_parts], refs[n_parts:]
        flat, refs = refs[0], refs[1:]
    else:
        g_out, g_up, refs = refs[0], refs[1], refs[2:]
    table, feats, radial, grads, g_radial, g_feats, g_lifted, acc_out = refs
    channels = w_up.shape[1]
    atoms = g_lifted.shape[2]
    hid = w_out.shape[0]
    total = list_chunks(table, slots, counts, chunk)
    w_blocked = radial_weights(w_out, channels)
    w_out_t = wcat3(w_blocked, 1)
    w_high, w_low = split(w_blocked.T)
    w_both = jnp.concatenate(
        [twice(w_high, 1), jnp.concatenate([w_low, jnp.zeros_like(w_low)], axis=1)], axis=0
    )
    if first:
        acc_out[...] = jnp.zeros_like(acc_out)
    else:
        acc_out[...] = acc_out_in[...]
    g_lifted[...] = jnp.zeros_like(g_lifted)
    g_radial[1] = jnp.zeros_like(g_radial[1])
    g_feats[1] = jnp.zeros_like(g_feats[1])

    def prepare(t, slot):
        p, k, cols = chunk_at(table, jnp.minimum(t, total - 1), chunk)
        high, low = hidden[p, :hid, cols], hidden[p, hid:, cols]
        to_hot = one_hot(recv[k, :, cols], atoms)
        grads[slot] = dot(grad_amp[...], twice(to_hot, 0))
        radial[slot] = dot(w_out_t, jnp.concatenate([high, high, low], axis=0))
        from_hot = one_hot(send[k, :, cols], atoms)
        feats[slot] = dot(lifted[p], twice(from_hot, 0))

    def collect(t, slot):
        p, k, cols = chunk_at(table, jnp.maximum(t, 0), chunk)
        tall = jnp.concatenate([g_radial[slot, :, :chunk], g_radial[slot, :, chunk:]], axis=0)
        both = dot(w_both, tall)
        g_hidden[p, :, cols] = both[:hid] + both[hid:]
        high, low = hidden[p, :hid, cols], hidden[p, hid:, cols]
        stacked = jnp.concatenate(
            [twice(high, 1), jnp.concatenate([low, jnp.zeros_like(low)], axis=1)], axis=0
        )
        acc_out[...] += dot(g_radial[slot], stacked, NT)
        from_hot = one_hot(send[k, :, cols], atoms)
        g_lifted[p] += dot(g_feats[slot], twice(from_hot, 1), NT)

    def combine(t, slot):
        p, _, cols = chunk_at(table, t, chunk)
        rows = [geo[p, ROW_Y + m : ROW_Y + m + 1, cols] for m in range(16)]
        backward_messages(
            feats.at[slot], radial.at[slot], grads.at[slot], rows, g_radial.at[slot],
            g_feats.at[slot], channels, chunk,
        )

    def step(i, carry):
        t = 2 * i
        combine(t, 0)
        prepare(t + 1, 1)
        collect(t - 1, 1)
        combine(t + 1, 1)
        prepare(t + 2, 0)
        collect(t, 0)
        return carry

    prepare(0, 0)
    lax.fori_loop(0, total // 2, step, 0)
    collect(total // 2 * 2 - 1, 1)

    @pl.when(total % 2 == 1)
    def _():
        combine(total - 1, 0)
        collect(total - 1, 0)

    w_up_parts = [split(w_up[0]), split(w_up[1])]
    sums = [None, None] if first else [acc_up_in[0], acc_up_in[1]]
    for p in range(n):
        lifted_grads = [component(g_lifted[p], comp, 4) for comp in range(4)]
        for kind in range(2):
            count = 1 + 2 * kind
            own = lifted_grads[kind : kind + count]
            tall = jnp.concatenate([value.T for value in own], axis=0)
            back = dot1(tall, w_up_parts[kind], NT)
            for a, value in enumerate(rows_of(back, count)):
                x_grads[p][kind + a] = value
            x = x_refs[p][kind * atoms : (kind + count) * atoms, :]
            part = dot1(jnp.concatenate(own, axis=1), x)
            sums[kind] = part if sums[kind] is None else sums[kind] + part
    if last:
        both = acc_out[...]
        both = both[:, :hid] + both[:, hid:]
        paths = both.shape[0] // channels
        up_at = paths * hid
        end = up_at + 2 * channels
        flat[end:, :] = jnp.zeros_like(flat[end:, :])
        for path in range(paths):
            flat[path * hid : (path + 1) * hid, :] = component(both, path, paths).T
        for kind in range(2):
            row = up_at + kind * channels
            flat[row : row + channels, :] = sums[kind].T
        deal(flat, digits[0, 0], parts)
    else:
        for kind in range(2):
            g_up[kind] = sums[kind]
        g_out[...] = acc_out[...]


def mlp_backward_kernel(groups, *refs):
    counts, refs = refs[0], refs[1:]
    number = len(groups)
    geos, grads, refs = refs[:number], refs[number : 2 * number], refs[2 * number :]
    w_in, w_mid, small, acc_in, acc_mid = refs
    n_basis, hid = w_in.shape
    w_in_t = wcat3(w_in[...].T, 1)
    w_mid_t = [wcat3(w_mid[0].T, 1), wcat3(w_mid[1].T, 1)]
    w_mid_n = [wcat3(w_mid[0], 1), wcat3(w_mid[1], 1)]
    acc_in[...] = jnp.zeros_like(acc_in)
    acc_mid[...] = jnp.zeros_like(acc_mid)
    edges = geos[0].shape[2]
    lane = lax.broadcasted_iota(jnp.int32, (hid, edges), 1)

    def stack(v):
        high, low = split(v)
        return jnp.concatenate([high, low], axis=0)

    for slots, geo, grad in zip(groups, geos, grads):
        def one(p, slots=slots, geo=geo, grad=grad):
            k = slots[0]
            for at, slot in enumerate(slots):
                k = jnp.where(p == at, slot, k)
            bessel = geo[p, :8, :]
            h1, s1 = silu_parts(dot(w_in_t, basis_stack(bessel)))
            h2, s2 = silu_parts(dot(w_mid_t[0], cat3(h1, 0)))
            h3, s3 = silu_parts(dot(w_mid_t[1], cat3(h2, 0)))
            g3 = grad[p] * geo[p, ROW_ENV : ROW_ENV + 1, :]
            g3 = jnp.where(lane < counts[0, k], g3, 0.0)
            d3 = g3 * (s3 + h3 * (1.0 - s3))
            acc_mid[1] += dot(stack(h2), stack(d3), NT)
            d2 = dot(w_mid_n[1], cat3(d3, 0)) * (s2 + h2 * (1.0 - s2))
            acc_mid[0] += dot(stack(h1), stack(d2), NT)
            d1 = dot(w_mid_n[0], cat3(d2, 0)) * (s1 + h1 * (1.0 - s1))
            high = bessel.astype(BF16).astype(F32)
            basis = jnp.concatenate([high, bessel - high], axis=0).astype(BF16)
            acc_in[...] += dot(basis, stack(d1), NT)

        in_pairs(len(slots), one)

    def quadrants(v, rows):
        return v[:rows, :hid] + v[:rows, hid:] + v[rows:, :hid]

    small[hid + n_basis :, :] = jnp.zeros_like(small[hid + n_basis :, :])
    small[:hid, :] = jnp.concatenate([quadrants(acc_mid[layer], hid) for layer in range(2)], axis=1)
    basis_grad = quadrants(acc_in[...], n_basis)
    small[hid : hid + n_basis, :] = jnp.concatenate([basis_grad, jnp.zeros_like(basis_grad)], axis=1)


def call(kernel, out_shape, smem, scratch, args, name, us):
    specs = [SMEM] * smem + [VMEM] * (len(args) - smem)
    return call_with(kernel, out_shape, specs, scratch, args, name, us)


def call_with(kernel, out_shape, specs, scratch, args, name, us):
    return pl.pallas_call(
        kernel,
        out_shape=out_shape,
        in_specs=specs,
        out_specs=jax.tree.map(lambda _: VMEM, out_shape),
        scratch_shapes=scratch,
        compiler_params=pltpu.CompilerParams(vmem_limit_bytes=LIMIT),
        cost_estimate=pl.CostEstimate(
            flops=int(us * 5e8), bytes_accessed=int(us * 2e6), transcendentals=0
        ),
        name=name,
    )(*args)


def shape(*dims, dtype=F32):
    return jax.ShapeDtypeStruct(dims, dtype)


def shifted(value, steps):
    count = lax.axis_size("blk")
    return lax.ppermute(value, "blk", [(i, (i + steps) % count) for i in range(count)])


def stages_of(count):
    stages, stride = [], 1
    while stride < count:
        members = 4 if (count // stride) % 4 == 0 else 2
        stages.append((members, stride))
        stride *= members
    return stages[::-1]


def exchange(values, stage):
    members, stride = stage
    count = lax.axis_size("blk")
    moved = [
        lax.ppermute(values[k], "blk", [(i, i ^ (k * stride)) for i in range(count)])
        for k in range(1, members)
    ]
    return [values[0]] + moved


def add_parts(groups, stages, at, digits):
    arrays = [part for parts, _ in groups for part in parts]
    counts = tuple((len(parts), tuple(sizes)) for parts, sizes in groups)
    total = sum(size for _, sizes in groups for size in sizes)
    out = stages[at + 1][0] if at + 1 < len(stages) else 1
    shapes = shape(total, LANES)
    if out > 1:
        shapes = tuple(shape(total // out, LANES) for _ in range(out))
    return call(
        functools.partial(add_kernel, at + 1, counts, out), shapes, 1,
        [pltpu.VMEM((total, LANES), F32)] if out > 1 else [], (digits, *arrays), f"add_{at}", 1,
    )


def join_parts(parts, segments, stages, at, digits, tail):
    members = stages[at][0]
    rows = members * sum(rows * blocks for rows, blocks in segments) + tail
    return call(
        functools.partial(join_kernel, at, members, segments, tail), shape(rows, LANES), 1,
        [pltpu.VMEM((members, tail, LANES), F32)] if tail else [], (digits, *parts),
        f"join_{at}", 1,
    )


def per_device(
    node_scalars, node_vectors, positions, species, edge_senders, edge_receivers, edge_shifts,
    bucket_counts, w_up, w_rad_in, w_rad_mid, w_rad_out, w_lin, w_sc_scalar, w_sc_vector, w_prod,
    w_skip, w_read, cot_scalars, cot_vectors, cot_energy,
):
    _, buckets, slots = edge_senders.shape
    send = edge_senders.reshape(buckets, 1, slots)
    recv = edge_receivers.reshape(buckets, 1, slots)
    shift = edge_shifts.reshape(3 * buckets, 1, slots)
    reach = (buckets - 1) // 2
    atoms, channels = node_scalars.shape
    hid, outs = w_rad_out.shape
    n_basis = w_rad_in.shape[0]
    n_spec = w_skip.shape[1]
    chunk = min(256, slots)
    blocks = lax.axis_size("blk")
    stages = stages_of(blocks)
    me = lax.axis_index("blk")
    digits = jnp.stack([(me // stride) % members for members, stride in stages]).reshape(1, -1)
    rows, at = [], 0
    height = up8(4 * atoms + 6)
    for piece in (node_scalars, node_vectors.reshape(3 * atoms, channels), positions,
                  species.reshape(1, atoms), cot_energy.reshape(1, atoms),
                  w_read.reshape(1, channels)):
        end = at + piece.shape[0]
        rows.append(jnp.pad(piece, ((at, height - end), (0, 0))).astype(F32))
        at = end
    packed = functools.reduce(jnp.add, rows)
    offsets = sorted([d for d in range(-reach, reach + 1) if d], key=abs)
    x_of = {reach: packed, **{reach + d: shifted(packed, -d) for d in offsets}}
    sc_s_t, sc_v_t = jnp.swapaxes(w_sc_scalar, 0, 1), jnp.swapaxes(w_sc_vector, 0, 1)

    skip_rows = 2 * n_spec * channels
    g_total, skip_s, skip_v, skip_gs, skip_gv, g_skip = call(
        skip_kernel,
        (shape(2, atoms, channels), shape(atoms, channels), shape(3, atoms, channels),
         shape(atoms, channels), shape(3, atoms, channels), shape(skip_rows, channels)),
        0, [],
        (packed, cot_scalars, cot_vectors, w_skip),
        "self_connection", 4,
    )

    def padded(rows):
        unit = 8 * blocks
        return -(-rows // unit) * unit

    node_rows = padded(skip_rows + 6 * channels + up8(9 * n_spec) + up8(5 * n_spec) + 8)
    edge_rows = padded(outs // channels * hid + 2 * channels)
    tail_unit = 8 * (blocks // stages[0][0])
    small_rows = -(-(hid + n_basis) // tail_unit) * tail_unit

    near = (reach - 1, reach + 1)
    far = tuple(k for k in range(buckets) if abs(k - reach) > 1)
    groups = [(reach,), near] + ([far] if far else [])
    most = [len(g) * (slots // chunk) for g in groups]
    first_parts = stages[0][0]
    acc = ()
    kept = []
    for at, group in enumerate(groups):
        n = len(group)
        last = at == len(groups) - 1
        base = len(groups[1]) if at == 2 else 0
        out_shapes = (
            shape(base + n, 4 * channels, 2 * atoms, dtype=BF16), shape(base + n, 2 * hid, slots, dtype=BF16),
            shape(base + n, GEO_ROWS, slots),
        )
        scratch = [
            pltpu.SMEM((3, most[at]), jnp.int32),
            pltpu.VMEM((2, 4 * channels, chunk), F32),
            pltpu.VMEM((2, outs, chunk), F32),
            pltpu.VMEM((2, 16 * channels, 2 * chunk), BF16),
        ]
        node_args, node_counts = (), None
        if last:
            node_args = (digits, w_lin, sc_s_t, sc_v_t, w_prod, g_total,
                         cot_vectors, skip_s, skip_v, g_skip)
            node_outs = (
                shape(atoms, channels), shape(3, atoms, channels), shape(1, atoms),
                shape(16 * channels, 2 * atoms, dtype=BF16),
                *[shape(node_rows // first_parts, LANES)] * first_parts,
            )
            node_counts = len(node_args), len(node_outs)
            scratch = [
                pltpu.VMEM((16 * channels, atoms), F32), pltpu.VMEM((node_rows, LANES), F32)
            ] + scratch
            out_shapes = node_outs + out_shapes
        else:
            out_shapes = (shape(16 * channels, atoms),) + out_shapes
        args = (
            bucket_counts, send, recv, shift, packed, *[x_of[k] for k in group], w_up, w_rad_in,
            w_rad_mid, w_rad_out, *acc, *(kept[-1] if base else ()), *node_args,
        )
        specs = [SMEM] + [VMEM] * (len(args) - 1)
        if last:
            specs[len(args) - len(node_args)] = SMEM
        result = call_with(
            functools.partial(forward_kernel, base, group, chunk, at == 0, node_counts), out_shapes,
            specs, scratch, args, f"edges_{at}", 5 * n + (6 if last else 0),
        )
        kept.append(result[-3:])
        if last:
            new_s, new_v, energy, grad_amp = result[:4]
            node_parts = result[4 : 4 + first_parts]
        else:
            acc = result[:1]

    tie = lax.optimization_barrier
    node_parts = exchange(node_parts, stages[0])
    others = tuple(k for group in groups[1:] for k in group)
    sums = ()
    n_early = len(others) // 2
    grads_hidden = []
    home = []
    for group, (lifted, hidden, geo) in ((others, kept[-1]), (groups[0], kept[0])):
        n = len(group)
        first, last = not sums, bool(sums)
        if last:
            final = (shape(edge_rows // first_parts, LANES),) * first_parts
        else:
            final = (shape(outs, 2 * hid), shape(2, channels, channels))
        args = (
            bucket_counts, digits, send, recv, grad_amp, geo, lifted, hidden,
            *[x_of[k] for k in group], w_up, w_rad_out, *sums,
        )
        result = call(
            functools.partial(backward_kernel, group, chunk, first, last, first_parts),
            (*[shape(4, atoms, channels) for _ in group], shape(n, hid, slots), *final), 2,
            ([pltpu.VMEM((edge_rows, LANES), F32)] if last else [])
            + [
                pltpu.SMEM((3, n * (slots // chunk)), jnp.int32),
                pltpu.VMEM((2, 4 * channels, chunk), F32),
                pltpu.VMEM((2, outs, chunk), F32),
                pltpu.VMEM((2, 16 * channels, chunk), F32),
                pltpu.VMEM((2, outs, 2 * chunk), BF16),
                pltpu.VMEM((2, 4 * channels, 2 * chunk), BF16),
                pltpu.VMEM((n, 4 * channels, atoms), F32),
                pltpu.VMEM((outs, 2 * hid), F32),
            ],
            args, "edges_back_own" if last else "edges_back", 6 * n,
        )
        if first:
            result, node_parts = tie((result, node_parts))
            away = [(k - reach, value) for k, value in zip(group, result[:n])]
            away.sort(key=lambda pair: -abs(pair[0]))
            home = [shifted(value, offset) for offset, value in away]
        else:
            early, late = home[: n_early], home[n_early:]
            result, early = tie((result, early))
            edge_parts = exchange(result[n + 1 :], stages[0])
            home = early + [result[0]]
        grads_hidden.append(result[n])
        sums = result[n + 1 :]
    small = call(
        functools.partial(mlp_backward_kernel, (others, groups[0])), shape(small_rows, LANES), 1,
        [pltpu.VMEM((2 * n_basis, 2 * hid), F32), pltpu.VMEM((2, 2 * hid, 2 * hid), F32)],
        (bucket_counts, kept[-1][2], kept[0][2], *grads_hidden, w_rad_in, w_rad_mid),
        "radial_back", 7,
    )
    small, edge_parts, late = tie((small, edge_parts, late))
    home = home + late
    sizes = [node_rows // first_parts, edge_rows // first_parts, small_rows]
    groups = [(node_parts, sizes[:1]), (edge_parts, sizes[1:2]), ([small], sizes[2:])]
    whole = add_parts(groups, stages, 0, digits)
    for at in range(1, len(stages)):
        sizes = [size // stages[at][0] for size in sizes]
        whole = add_parts([(exchange(whole, stages[at]), sizes)], stages, at, digits)
    blocks_now, tail_blocks = 1, 1
    for at in range(len(stages)):
        members = stages[at][0]
        parts = exchange([whole] * members, stages[at])
        segments = [(sizes[0], blocks_now), (sizes[1], blocks_now)]
        if at:
            segments.append((sizes[2], tail_blocks))
            tail_blocks *= members
        blocks_now *= members
        if at + 1 < len(stages):
            whole = join_parts(parts, segments, stages, at, digits, 0 if at else sizes[2])
    g_skip, g_lin, g_prod, g_sc_s, g_sc_v, g_read, g_out, g_up, g_mid, g_in = call(
        functools.partial(finish_kernel, len(stages) - 1, stages[-1][0], segments, n_spec),
        (shape(skip_rows, channels), shape(4 * channels, channels), shape(2 * channels, channels),
         shape(9, n_spec, channels), shape(5, n_spec, channels), shape(1, channels),
         shape(hid, outs), shape(2 * channels, channels), shape(2, hid, hid), shape(n_basis, hid)),
        1,
        [pltpu.VMEM((node_rows + edge_rows + small_rows, LANES), F32)],
        (digits, *parts), "finish", 2,
    )
    gx = home[0]
    for part in home[1:]:
        gx = gx + part
    return (
        new_s, new_v, energy.reshape(-1), gx[0] + skip_gs, gx[1:] + skip_gv,
        g_up.reshape(1, 2, channels, channels), g_in[None], g_mid[None], g_out[None],
        g_lin.reshape(1, 4, channels, channels), jnp.swapaxes(g_sc_s, 0, 1)[None],
        jnp.swapaxes(g_sc_v, 0, 1)[None], g_prod.reshape(1, 2, channels, channels),
        g_skip.reshape(1, 2, n_spec, channels, channels), g_read,
    )


def solution(mesh):
    atoms = ("cell", "blk")
    in_specs = (
        P(atoms, None), P(None, atoms, None), P(None, atoms), P(atoms), P(atoms, None, None),
        P(atoms, None, None), P(atoms, None, None, None), P(atoms, None),
        P(), P(), P(), P(), P(), P(), P(), P(), P(), P(),
        P(atoms, None), P(None, atoms, None), P(atoms),
    )
    out_specs = (
        P(atoms, None), P(None, atoms, None), P(atoms), P(atoms, None), P(None, atoms, None),
        P("cell", None, None, None), P("cell", None, None), P("cell", None, None, None),
        P("cell", None, None), P("cell", None, None, None), P("cell", None, None, None),
        P("cell", None, None, None), P("cell", None, None, None),
        P("cell", None, None, None, None), P("cell", None),
    )
    return jax.shard_map(
        per_device, mesh=mesh, in_specs=in_specs, out_specs=out_specs, check_vma=False
    )
```

```python
import functools
import math

import jax
import jax.numpy as jnp
from jax import lax
from jax.experimental import pallas as pl
from jax.experimental.pallas import tpu as pltpu
from jax.sharding import PartitionSpec as P

CUTOFF = 5.0
SOFTEN = 0.1
NEIGH = 0.17677669529663687
F32 = jnp.float32
BF16 = jnp.bfloat16
LANES = 128
VMEM = pl.BlockSpec(memory_space=pltpu.VMEM)
SMEM = pl.BlockSpec(memory_space=pltpu.SMEM)
LIMIT = 20 * 1024 * 1024

NN = (((1,), (0,)), ((), ()))
NT = (((1,), (1,)), ((), ()))


BLOCK = 16


def row_of(comp, count, channel):
    return (channel // BLOCK * count + comp) * BLOCK


def by_block(parts):
    channels = parts[0].shape[0]
    return jnp.concatenate(
        [part[c : c + BLOCK] for c in range(0, channels, BLOCK) for part in parts], axis=0
    )


def component(value, comp, count):
    step = count * BLOCK
    at = comp * BLOCK
    return jnp.concatenate(
        [value[r + at : r + at + BLOCK] for r in range(0, value.shape[0], step)], axis=0
    )


def split(v):
    high = v.astype(BF16)
    return high, (v - high.astype(F32)).astype(BF16)


def dot(a, b, dims=NN):
    return lax.dot_general(a, b, dims, preferred_element_type=F32)


def dot3(a, b, dims=NN):
    ah, al = a if isinstance(a, tuple) else split(a)
    bh, bl = b if isinstance(b, tuple) else split(b)
    return dot(ah, bh, dims) + (dot(ah, bl, dims) + dot(al, bh, dims))


def dot1(a, b, dims=NN):
    ah, al = a if isinstance(a, tuple) else split(a)
    bh, bl = b if isinstance(b, tuple) else split(b)
    left = jnp.concatenate([ah, ah, al], axis=1)
    right = jnp.concatenate([bh, bl, bh], axis=dims[0][1][0])
    return dot(left, right, dims)


def rows_of(v, count):
    step = v.shape[0] // count
    return [v[at * step : (at + 1) * step] for at in range(count)]


def columns_of(v, count):
    step = v.shape[1] // count
    return [v[:, at * step : (at + 1) * step] for at in range(count)]


def cat3(v, axis):
    high, low = split(v)
    return jnp.concatenate([high, high, low], axis=axis)


def wcat3(v, axis):
    high, low = split(v)
    return jnp.concatenate([high, low, high], axis=axis)


def column(row, width):
    return jnp.broadcast_to(row, (width, row.shape[1])).T


ROW_Y = 8
ROW_ENV = 24
GEO_ROWS = 32


def write_geometry(geo, base, slots, counts, send, recv, shift, tables, own_pos):
    buckets, _, edges = send.shape
    bucket_of = lax.broadcasted_iota(jnp.int32, (buckets, LANES), 0)
    filled = jnp.zeros((buckets, LANES), jnp.int32)
    for k in slots:
        filled = jnp.where(bucket_of == k, counts[0, k], filled)
    own = [jnp.broadcast_to(own_pos[a : a + 1, :], (buckets, LANES)) for a in range(3)]
    lane = lax.broadcasted_iota(jnp.int32, (buckets, LANES), 1)
    for block in range(edges // LANES):
        cols = slice(block * LANES, (block + 1) * LANES)

        def put(row, value):
            for p, k in enumerate(slots, base):
                geo[p, row : row + 1, cols] = value[k : k + 1]

        from_idx = jnp.concatenate([send[k, :, cols] for k in range(buckets)], axis=0)
        to_idx = jnp.concatenate([recv[k, :, cols] for k in range(buckets)], axis=0)
        rel = []
        for a in range(3):
            there = jnp.take_along_axis(tables[a], from_idx, axis=1, mode="promise_in_bounds")
            here = jnp.take_along_axis(own[a], to_idx, axis=1, mode="promise_in_bounds")
            moved = jnp.concatenate([shift[3 * k + a, :, cols] for k in range(buckets)], axis=0)
            rel.append(there - here + moved.astype(F32))
        dist = jnp.sqrt(rel[0] * rel[0] + rel[1] * rel[1] + rel[2] * rel[2] + SOFTEN)
        inverse = 1.0 / dist
        x, y, z = (r * inverse for r in rel)
        angle = dist * (math.pi / CUTOFF)
        sine, twice = jnp.sin(angle), 2.0 * jnp.cos(angle)
        scale = math.sqrt(2.0 / CUTOFF) * inverse
        before, now = jnp.zeros_like(sine), sine
        for n in range(8):
            put(n, now * scale)
            before, now = now, twice * now - before
        xx, yy, zz = x * x, y * y, z * z
        planar = xx + yy
        rows = [
            jnp.ones_like(x),
            math.sqrt(3.0) * x,
            math.sqrt(3.0) * y,
            math.sqrt(3.0) * z,
            math.sqrt(15.0) * x * y,
            math.sqrt(15.0) * y * z,
            0.5 * math.sqrt(5.0) * (2.0 * zz - planar),
            math.sqrt(15.0) * x * z,
            0.5 * math.sqrt(15.0) * (xx - yy),
            math.sqrt(35.0 / 8.0) * (3.0 * xx - yy) * y,
            math.sqrt(105.0) * x * y * z,
            math.sqrt(21.0 / 8.0) * y * (4.0 * zz - planar),
            0.5 * math.sqrt(7.0) * z * (2.0 * zz - 3.0 * planar),
            math.sqrt(21.0 / 8.0) * x * (4.0 * zz - planar),
            0.5 * math.sqrt(105.0) * z * (xx - yy),
            math.sqrt(35.0 / 8.0) * (xx - 3.0 * yy) * x,
        ]
        for m, row in enumerate(rows):
            put(ROW_Y + m, row)
        q = dist * (1.0 / CUTOFF)
        q6 = q * q * q * q * q * q
        envelope = 1.0 - 28.0 * q6 + 48.0 * q6 * q - 21.0 * q6 * q * q
        put(ROW_ENV, jnp.where(lane + block * LANES < filled, envelope, 0.0))


def one_hot(index_row, atoms):
    edges = index_row.shape[1]
    atom = lax.broadcasted_iota(jnp.int32, (atoms, edges), 0)
    return jnp.where(atom == index_row, 1.0, 0.0).astype(BF16)


def twice(v, axis):
    return jnp.concatenate([v, v], axis=axis)


def silu_parts(v):
    gate = 1.0 / (1.0 + jnp.exp(-v))
    return v * gate, gate


def basis_stack(bessel):
    high = bessel.astype(BF16).astype(F32)
    return jnp.concatenate([high, high, bessel - high], axis=0).astype(BF16)


def lift(x_ref, w_up_t, out):
    atoms = out.shape[1] // 2
    scalars = dot1(w_up_t[0], x_ref[:atoms, :], NT)
    vectors = dot1(w_up_t[1], x_ref[atoms : 4 * atoms, :], NT)
    parts = [split(value) for value in [scalars] + columns_of(vectors, 3)]
    out[:, :atoms] = by_block([high for high, _ in parts])
    out[:, atoms:] = by_block([low for _, low in parts])


def radial_weights(w_out, channels):
    w_t = w_out[...].T
    return by_block([w_t[at : at + channels] for at in range(0, w_t.shape[0], channels)])


def list_chunks(table, slots, counts, chunk, base=0):
    table[0, 0], table[1, 0], table[2, 0] = base, slots[0], 0
    total = 0
    for p, k in enumerate(slots, base):
        number = (counts[0, k] + chunk - 1) // chunk

        def note(j, at, p=p, k=k):
            table[0, at] = p
            table[1, at] = k
            table[2, at] = j * chunk
            return at + 1

        total = lax.fori_loop(0, number, note, total)
    return total


def chunk_at(table, t, chunk):
    return table[0, t], table[1, t], pl.ds(pl.multiple_of(table[2, t], chunk), chunk)


def forward_messages(feats, radial, geo_rows, out, channels, edges):
    ys = []
    for half in range(edges // LANES):
        cols = slice(half * LANES, (half + 1) * LANES)
        ys.append([jnp.broadcast_to(row[:, cols], (BLOCK, LANES)) for row in geo_rows])
    for c in range(0, channels, BLOCK):
        for half in range(edges // LANES):
            cols = slice(half * LANES, (half + 1) * LANES)
            low_cols = slice(edges + half * LANES, edges + (half + 1) * LANES)
            y = ys[half]

            def feat(k):
                at = row_of(k, 4, c)
                return feats[at : at + BLOCK, cols]

            def rad(k):
                at = row_of(k, 7, c)
                return radial[at : at + BLOCK, cols]

            def put(comp, value):
                high, low = split(value)
                at = row_of(comp, 16, c)
                out[at : at + BLOCK, cols] = high
                out[at : at + BLOCK, low_cols] = low

            s, v = feat(0), [feat(1), feat(2), feat(3)]
            inner = y[1] * v[0] + y[2] * v[1] + y[3] * v[2]
            put(0, rad(0) * s + rad(4) * inner)
            first, fifth, sixth = rad(1) * s, rad(5), rad(6)
            put(1, first * y[1] + fifth * v[0] + sixth * (y[2] * v[2] - y[3] * v[1]))
            put(2, first * y[2] + fifth * v[1] + sixth * (y[3] * v[0] - y[1] * v[2]))
            put(3, first * y[3] + fifth * v[2] + sixth * (y[1] * v[1] - y[2] * v[0]))
            second = rad(2) * s
            for m in range(4, 9):
                put(m, second * y[m])
            third = rad(3) * s
            for m in range(9, 16):
                put(m, third * y[m])


def in_pairs(count, one):
    if count > 1:
        def pair(i, carry):
            one(2 * i)
            one(2 * i + 1)
            return carry

        if count < 4:
            pair(0, 0)
        else:
            lax.fori_loop(0, count // 2, pair, 0)
    if count % 2:
        one(count - 1)


def radial_hidden(base, count, w_in, w_mid, geo, hidden_out, kept_h, kept_d):
    hid = w_in.shape[1]
    w_in_t = wcat3(w_in[...].T, 1)
    w_mid_t = [wcat3(w_mid[0].T, 1), wcat3(w_mid[1].T, 1)]

    def one(at):
        p = base + at
        value = dot(w_in_t, basis_stack(geo[p, :8, :]))
        for layer in range(3):
            h, gate = silu_parts(value)
            kept_d[at, layer * hid : (layer + 1) * hid, :] = gate + h * (1.0 - gate)
            if layer < 2:
                high, low = split(h)
                kept_h[at, 2 * layer * hid : (2 * layer + 1) * hid, :] = high
                kept_h[at, (2 * layer + 1) * hid : (2 * layer + 2) * hid, :] = low
                value = dot(w_mid_t[layer], jnp.concatenate([high, high, low], axis=0))
        high, low = split(h * geo[p, ROW_ENV : ROW_ENV + 1, :])
        hidden_out[p, :hid, :] = high
        hidden_out[p, hid:, :] = low

    in_pairs(count, one)


def edge_forward(
    base, slots, chunk, counts, send, recv, shift, own_pos, tables, x_refs, w_up, w_in, w_mid, w_out,
    lifted_out, hidden_out, geo, kept_h, kept_d, acc, table, feats, radial, messages,
):
    channels, atoms = w_up.shape[1], acc.shape[1]
    hid = w_in.shape[1]
    total = list_chunks(table, slots, counts, chunk, base)
    write_geometry(geo, base, slots, counts, send, recv, shift, tables, own_pos)
    w_up_t = [split(w_up[0].T), split(w_up[1].T)]
    for p in range(len(slots)):
        lift(x_refs[p], w_up_t, lifted_out.at[base + p])
    radial_hidden(base, len(slots), w_in, w_mid, geo, hidden_out, kept_h, kept_d)
    w_out_t = wcat3(radial_weights(w_out, channels), 1)
    messages[1] = jnp.zeros_like(messages[1])

    def prepare(t, slot):
        p, k, cols = chunk_at(table, jnp.minimum(t, total - 1), chunk)
        high, low = hidden_out[p, :hid, cols], hidden_out[p, hid:, cols]
        radial[slot] = dot(w_out_t, jnp.concatenate([high, high, low], axis=0))
        from_hot = one_hot(send[k, :, cols], atoms)
        feats[slot] = dot(lifted_out[p], twice(from_hot, 0))

    def collect(t, slot):
        _, k, cols = chunk_at(table, jnp.maximum(t, 0), chunk)
        to_hot = one_hot(recv[k, :, cols], atoms)
        acc[...] += dot(messages[slot], twice(to_hot, 1), NT)

    def combine(t, slot):
        p, _, cols = chunk_at(table, t, chunk)
        rows = [geo[p, ROW_Y + m : ROW_Y + m + 1, cols] for m in range(16)]
        forward_messages(
            feats.at[slot], radial.at[slot], rows, messages.at[slot], channels, chunk
        )

    def step(i, carry):
        t = 2 * i
        combine(t, 0)
        prepare(t + 1, 1)
        collect(t - 1, 1)
        combine(t + 1, 1)
        prepare(t + 2, 0)
        collect(t, 0)
        return carry

    prepare(0, 0)
    lax.fori_loop(0, total // 2, step, 0)
    collect(total // 2 * 2 - 1, 1)

    @pl.when(total % 2 == 1)
    def _():
        combine(total - 1, 0)
        collect(total - 1, 0)


def forward_kernel(base, slots, chunk, first, node_counts, *refs):
    n = len(slots)
    counts, send, recv, shift, refs = *refs[:4], refs[4:]
    x_own, x_refs, refs = refs[0], refs[1 : 1 + n], refs[1 + n :]
    w_up, w_in, w_mid, w_out, refs = *refs[:4], refs[4:]
    atoms = w_up.shape[1]
    at = 4 * atoms
    if not first:
        acc_in, refs = refs[0], refs[1:]
    before, refs = refs[: 3 if base else 0], refs[3 if base else 0 :]
    if node_counts:
        n_in, n_out = node_counts
        node_in, node_out, refs = refs[:n_in], refs[n_in : n_in + n_out], refs[n_in + n_out :]
        lifted_out, hidden_out, geo, kept_h, kept_d, acc, flat = refs[:7]
        table, feats, radial, messages = refs[7:]
    else:
        acc, lifted_out, hidden_out, geo, kept_h, kept_d = refs[:6]
        table, feats, radial, messages = refs[6:]
    if first:
        acc[...] = jnp.zeros_like(acc)
    else:
        acc[...] = acc_in[...]
    for ref, out in zip(before, (lifted_out, hidden_out, geo)):
        out[:base] = ref[...]
    tables = []
    for a in range(3):
        rows = [x_own[at + a : at + a + 1, :]] * send.shape[0]
        for k, ref in zip(slots, x_refs):
            rows[k] = ref[at + a : at + a + 1, :]
        tables.append(jnp.concatenate(rows, axis=0))
    edge_forward(
        base, slots, chunk, counts, send, recv, shift, x_own.at[at : at + 8], tables, x_refs, w_up, w_in,
        w_mid, w_out, lifted_out, hidden_out, geo, kept_h, kept_d, acc, table, feats, radial,
        messages,
    )
    if node_counts:
        rows = [x_own[at + 3 : at + 4, :], x_own[at + 5 : at + 6, :]]
        node_stage(acc, flat, *rows, *node_in, *node_out)


def deal(flat, digit, parts):
    rows = parts[0].shape[0]
    for k, part in enumerate(parts):
        at = pl.multiple_of((digit ^ k) * rows, 8)
        part[...] = flat[pl.ds(at, rows), :]


def add_kernel(stage, groups, n_out, *refs):
    digits, refs = refs[0], refs[1:]
    totals = []
    for count, sizes in groups:
        total = functools.reduce(jnp.add, [part[...] for part in refs[:count]])
        refs = refs[count:]
        at = 0
        for size in sizes:
            totals.append(total[at : at + size])
            at += size
    if n_out == 1:
        at = 0
        for total in totals:
            refs[0][at : at + total.shape[0], :] = total
            at += total.shape[0]
        return
    outs, scratch = refs[:n_out], refs[n_out]
    at, out_at = 0, 0
    for total in totals:
        size = total.shape[0]
        scratch[at : at + size, :] = total
        rows = size // n_out
        for k, out in enumerate(outs):
            first = pl.multiple_of(at + (digits[0, stage] ^ k) * rows, 8)
            out[out_at : out_at + rows, :] = scratch[pl.ds(first, rows), :]
        at += size
        out_at += rows


def join_into(out, digit, inputs, segments):
    radix = len(inputs)
    at, out_at = 0, 0
    for rows, blocks in segments:
        for _ in range(blocks):
            for k, part in enumerate(inputs):
                first = pl.multiple_of(out_at + (digit ^ k) * rows, 8)
                out[pl.ds(first, rows), :] = part[at : at + rows, :]
            at += rows
            out_at += rows * radix


def join_kernel(stage, radix, segments, tail, *refs):
    digits, inputs, out = refs[0], refs[1 : 1 + radix], refs[1 + radix]
    digit = digits[0, stage]
    join_into(out, digit, inputs, segments)
    if tail:
        store = refs[2 + radix]
        for k, part in enumerate(inputs):
            store[digit ^ k] = part[part.shape[0] - tail :, :]
        total = store[0]
        for member in range(1, radix):
            total = total + store[member]
        out[out.shape[0] - tail :, :] = total


def finish_kernel(stage, radix, segments, n_spec, *refs):
    digits, inputs, refs = refs[0], refs[1 : 1 + radix], refs[1 + radix :]
    node_outs, (g_out, g_up, g_mid, g_in, flat) = refs[:6], refs[6:]
    join_into(flat, digits[0, stage], inputs, segments)
    ends = []
    for rows, blocks in segments:
        ends.append((ends[-1] if ends else 0) + rows * blocks * radix)
    at = 0
    for out in node_outs:
        if len(out.shape) == 3:
            for p in range(out.shape[0]):
                out[p] = flat[at + p * n_spec : at + (p + 1) * n_spec, :]
            at += up8(out.shape[0] * n_spec)
        else:
            out[...] = flat[at : at + out.shape[0], :]
            at += up8(out.shape[0])
    at = ends[0]
    hid, n_basis = g_out.shape[0], g_in.shape[0]
    for path in range(g_out.shape[1] // LANES):
        g_out[:, path * LANES : (path + 1) * LANES] = flat[at : at + hid, :]
        at += hid
    g_up[...] = flat[at : at + g_up.shape[0], :]
    small = flat[ends[1] : ends[2], :]
    g_mid[0] = small[:hid, :hid]
    g_mid[1] = small[:hid, hid:]
    g_in[...] = small[hid : hid + n_basis, :hid]


DEGREE = (0, 1, 1, 1, 2, 2, 2, 2, 2, 3, 3, 3, 3, 3, 3, 3)


def species_hot(species_row, count):
    atoms = species_row.shape[1]
    which = lax.broadcasted_iota(jnp.int32, (count, atoms), 0)
    return jnp.where(which == species_row, 1.0, 0.0)


def up8(rows):
    return (rows + 7) // 8 * 8


def node_stage(
    acc, flat, species, w_read, digits, w_lin, w_sc_s, w_sc_v, w_prod, g_total, cot_v, skip_s,
    skip_v, g_skip, new_s, new_v, energy, grad_amp, *parts,
):
    channels, atoms = w_lin.shape[1], acc.shape[1]
    n_spec = w_sc_s.shape[1]
    flat[g_skip.shape[0] :, :] = jnp.zeros_like(flat[g_skip.shape[0] :, :])
    flat[: g_skip.shape[0], :] = g_skip[...]
    lin_at = g_skip.shape[0]
    prod_at = lin_at + 4 * channels
    sc_s_at = prod_at + 2 * channels
    sc_v_at = sc_s_at + up8(9 * n_spec)
    read_at = sc_v_at + up8(5 * n_spec)
    members = [[m for m in range(16) if DEGREE[m] == l] for l in range(4)]
    amp_t = [component(acc, m, 16) * NEIGH for m in range(16)]
    amp_t_parts = [split(v) for v in amp_t]
    b = []
    for l in range(4):
        high = jnp.concatenate([amp_t_parts[m][0].T for m in members[l]], axis=0)
        low = jnp.concatenate([amp_t_parts[m][1].T for m in members[l]], axis=0)
        stacked = dot(jnp.concatenate([high, high, low], axis=1), wcat3(w_lin[l], 0))
        b.extend(stacked[j * atoms : (j + 1) * atoms] for j in range(len(members[l])))
    b0 = b[0]
    n1 = b[1] * b[1] + b[2] * b[2] + b[3] * b[3]
    n2 = b[4] * b[4] + b[5] * b[5] + b[6] * b[6] + b[7] * b[7] + b[8] * b[8]
    n3 = functools.reduce(jnp.add, [b[m] * b[m] for m in range(9, 16)])
    species_col = column(species, channels)
    masks = [species_col == float(s) for s in range(n_spec)]

    def per_atom(w, p):
        value = jnp.broadcast_to(w[p, :1, :], (atoms, channels))
        for s in range(1, n_spec):
            value = jnp.where(masks[s], w[p, s : s + 1, :], value)
        return value

    ws = [per_atom(w_sc_s, p) for p in range(9)]
    wv = [per_atom(w_sc_v, p) for p in range(5)]
    sq = b0 * b0
    terms = [b0, sq, n1, n2, n3, sq * b0, b0 * n1, b0 * n2, b0 * n3]
    mixed = functools.reduce(jnp.add, [w * t for w, t in zip(ws, terms)])
    factors = [None, b0, sq, n1, n2]
    factor = wv[0]
    for p in range(1, 5):
        factor = factor + wv[p] * factors[p]
    prod_parts = [split(w_prod[0]), split(w_prod[1])]
    out_s = dot1(mixed, prod_parts[0]) + skip_s[...]
    new_s[...] = out_s
    mixed_v = jnp.concatenate([b[1 + a] * factor for a in range(3)], axis=0)
    for a, value in enumerate(rows_of(dot1(mixed_v, prod_parts[1]), 3)):
        new_v[a] = value + skip_v[a]
    energy[...] = dot3(jnp.broadcast_to(w_read, (8, channels)), out_s, NT)[:1]
    cot_e = g_total[1]
    flat[read_at : read_at + 1, :] = jnp.sum(out_s * cot_e, axis=0, keepdims=True)

    g_s = split(g_total[0])
    g_v = split(jnp.concatenate([cot_v[a] for a in range(3)], axis=0))
    flat[prod_at : prod_at + channels, :] = dot1(mixed.T, g_s)
    flat[prod_at + channels : sc_s_at, :] = dot1(mixed_v.T, g_v)
    g_mixed = dot1(g_s, prod_parts[0], NT)
    g_mixed_v = rows_of(dot1(g_v, prod_parts[1], NT), 3)
    g_factor = functools.reduce(jnp.add, [g_mixed_v[a] * b[1 + a] for a in range(3)])

    hot = species_hot(species.astype(jnp.int32), 8).astype(BF16)
    values = [g_mixed * terms[p] for p in range(9)]
    values += [g_factor] + [g_factor * factors[p] for p in range(1, 5)]
    high, low = split(jnp.concatenate(values, axis=1))
    by_species = dot(twice(hot, 1), jnp.concatenate([high, low], axis=0))
    for p, value in enumerate(columns_of(by_species, len(values))):
        row = sc_s_at + p * n_spec if p < 9 else sc_v_at + (p - 9) * n_spec
        flat[row : row + n_spec, :] = value[:n_spec]

    g_b0 = g_mixed * (
        ws[0] + 2.0 * b0 * ws[1] + 3.0 * sq * ws[5] + n1 * ws[6] + n2 * ws[7] + n3 * ws[8]
    ) + g_factor * (wv[1] + 2.0 * b0 * wv[2])
    g_n1 = 2.0 * (g_mixed * (ws[2] + b0 * ws[6]) + g_factor * wv[3])
    g_n2 = 2.0 * (g_mixed * (ws[3] + b0 * ws[7]) + g_factor * wv[4])
    g_n3 = 2.0 * (g_mixed * (ws[4] + b0 * ws[8]))
    g_b = [g_b0]
    for a in range(3):
        g_b.append(g_mixed_v[a] * factor + g_n1 * b[1 + a])
    for m in range(4, 9):
        g_b.append(g_n2 * b[m])
    for m in range(9, 16):
        g_b.append(g_n3 * b[m])
    g_b_parts = [split(v) for v in g_b]
    grads = []
    for l in range(4):
        row = lin_at + l * channels
        high = jnp.concatenate([g_b_parts[m][0] for m in members[l]], axis=0)
        low = jnp.concatenate([g_b_parts[m][1] for m in members[l]], axis=0)
        amp_high = jnp.concatenate([amp_t_parts[m][0] for m in members[l]], axis=1)
        amp_low = jnp.concatenate([amp_t_parts[m][1] for m in members[l]], axis=1)
        flat[row : row + channels, :] = dot(
            jnp.concatenate([amp_high, amp_high, amp_low], axis=1),
            jnp.concatenate([high, low, high], axis=0),
        )
        back = dot(wcat3(w_lin[l], 1), jnp.concatenate([high, high, low], axis=1), NT) * NEIGH
        grads.extend(
            split(back[:, j * atoms : (j + 1) * atoms]) for j in range(len(members[l]))
        )
    grad_amp[:, :atoms] = by_block([high for high, _ in grads])
    grad_amp[:, atoms:] = by_block([low for _, low in grads])
    deal(flat, digits[0, 0], parts)


def skip_kernel(
    x_own, cot_s, cot_v, w_skip,
    g_total, skip_s, skip_v, skip_gs, skip_gv, g_skip,
):
    atoms, channels = cot_s.shape
    n_spec = w_skip.shape[1]

    at = 4 * atoms + 3
    species, cot_e, w_read = x_own[at : at + 1, :], x_own[at + 1 : at + 2, :], x_own[at + 2 : at + 3, :]
    cot_col = column(cot_e, channels)
    total = cot_s[...] + cot_col * w_read
    g_total[0] = total
    g_total[1] = cot_col
    species_col = column(species, channels)

    def pick(values, masks):
        result = values[0]
        for s in range(1, n_spec):
            result = jnp.where(masks[s], values[s], result)
        return result

    for kind in range(2):
        count = 1 + 2 * kind
        masks = [jnp.concatenate([species_col == float(s)] * count, axis=0) for s in range(n_spec)]
        x = x_own[kind * atoms : (kind + count) * atoms, :]
        g = jnp.concatenate([cot_v[a] for a in range(3)], axis=0) if kind else total
        weights = [split(w_skip[kind, s]) for s in range(n_spec)]
        wide = tuple(jnp.concatenate([w[i] for w in weights], axis=1) for i in range(2))
        tall = tuple(jnp.concatenate([w[i] for w in weights], axis=0) for i in range(2))
        forward = pick(columns_of(dot1(x, wide), n_spec), masks)
        back = pick(columns_of(dot1(g, tall, NT), n_spec), masks)
        if kind:
            for a in range(3):
                skip_v[a] = forward[a * atoms : (a + 1) * atoms]
                skip_gv[a] = back[a * atoms : (a + 1) * atoms]
        else:
            skip_s[...] = forward
            skip_gs[...] = back
        apart = jnp.concatenate([jnp.where(mask, g, 0.0) for mask in masks], axis=1)
        sums = dot1(x.T, apart)
        for s, value in enumerate(columns_of(sums, n_spec)):
            row = (kind * n_spec + s) * channels
            g_skip[row : row + channels, :] = value


def backward_messages(feats, radial, grads, geo_rows, g_radial, g_feats, channels, edges):
    ys = []
    for half in range(edges // LANES):
        cols = slice(half * LANES, (half + 1) * LANES)
        ys.append([jnp.broadcast_to(row[:, cols], (BLOCK, LANES)) for row in geo_rows])
    for c in range(0, channels, BLOCK):
        for half in range(edges // LANES):
            cols = slice(half * LANES, (half + 1) * LANES)
            low_cols = slice(edges + half * LANES, edges + (half + 1) * LANES)
            y = ys[half]

            def load(ref, k, count):
                at = row_of(k, count, c)
                return ref[at : at + BLOCK, cols]

            def grad(m):
                return load(grads, m, 16)

            def rad(k):
                return load(radial, k, 7)

            def put(ref, comp, count, value):
                high, low = split(value)
                at = row_of(comp, count, c)
                ref[at : at + BLOCK, cols] = high
                ref[at : at + BLOCK, low_cols] = low

            s = load(feats, 0, 4)
            third = y[9] * grad(9)
            for m in range(10, 16):
                third = third + y[m] * grad(m)
            put(g_radial, 3, 7, s * third)
            second = y[4] * grad(4)
            for m in range(5, 9):
                second = second + y[m] * grad(m)
            put(g_radial, 2, 7, s * second)
            g = [grad(1 + a) for a in range(3)]
            first = y[1] * g[0] + y[2] * g[1] + y[3] * g[2]
            put(g_radial, 1, 7, s * first)
            zero = grad(0)
            put(g_radial, 0, 7, s * zero)
            put(
                g_feats, 0, 4,
                rad(0) * zero + rad(1) * first + rad(2) * second + rad(3) * third,
            )
            v = [load(feats, 1 + a, 4) for a in range(3)]
            put(g_radial, 4, 7, (y[1] * v[0] + y[2] * v[1] + y[3] * v[2]) * zero)
            put(g_radial, 5, 7, v[0] * g[0] + v[1] * g[1] + v[2] * g[2])
            cross = [
                g[1] * y[3] - g[2] * y[2],
                g[2] * y[1] - g[0] * y[3],
                g[0] * y[2] - g[1] * y[1],
            ]
            put(g_radial, 6, 7, v[0] * cross[0] + v[1] * cross[1] + v[2] * cross[2])
            fourth, fifth, sixth = rad(4) * zero, rad(5), rad(6)
            for a in range(3):
                put(g_feats, 1 + a, 4, fourth * y[1 + a] + fifth * g[a] + sixth * cross[a])


def backward_kernel(slots, chunk, first, last, n_parts, *refs):
    n = len(slots)
    counts, digits, send, recv, grad_amp = refs[:5]
    geo, lifted, hidden = refs[5:8]
    x_refs, refs = refs[8 : 8 + n], refs[8 + n :]
    w_up, w_out, refs = refs[0], refs[1], refs[2:]
    if not first:
        acc_out_in, acc_up_in, refs = refs[0], refs[1], refs[2:]
    x_grads, g_hidden, refs = refs[:n], refs[n], refs[n + 1 :]
    if last:
        parts, refs = refs[:n_parts], refs[n_parts:]
        flat, refs = refs[0], refs[1:]
    else:
        g_out, g_up, refs = refs[0], refs[1], refs[2:]
    table, feats, radial, grads, g_radial, g_feats, g_lifted, acc_out = refs
    channels = w_up.shape[1]
    atoms = g_lifted.shape[2]
    hid = w_out.shape[0]
    total = list_chunks(table, slots, counts, chunk)
    w_blocked = radial_weights(w_out, channels)
    w_out_t = wcat3(w_blocked, 1)
    w_high, w_low = split(w_blocked.T)
    w_both = jnp.concatenate(
        [twice(w_high, 1), jnp.concatenate([w_low, jnp.zeros_like(w_low)], axis=1)], axis=0
    )
    if first:
        acc_out[...] = jnp.zeros_like(acc_out)
    else:
        acc_out[...] = acc_out_in[...]
    g_lifted[...] = jnp.zeros_like(g_lifted)
    g_radial[1] = jnp.zeros_like(g_radial[1])
    g_feats[1] = jnp.zeros_like(g_feats[1])

    def prepare(t, slot):
        p, k, cols = chunk_at(table, jnp.minimum(t, total - 1), chunk)
        high, low = hidden[p, :hid, cols], hidden[p, hid:, cols]
        to_hot = one_hot(recv[k, :, cols], atoms)
        grads[slot] = dot(grad_amp[...], twice(to_hot, 0))
        radial[slot] = dot(w_out_t, jnp.concatenate([high, high, low], axis=0))
        from_hot = one_hot(send[k, :, cols], atoms)
        feats[slot] = dot(lifted[p], twice(from_hot, 0))

    def collect(t, slot):
        p, k, cols = chunk_at(table, jnp.maximum(t, 0), chunk)
        tall = jnp.concatenate([g_radial[slot, :, :chunk], g_radial[slot, :, chunk:]], axis=0)
        both = dot(w_both, tall)
        g_hidden[p, :, cols] = both[:hid] + both[hid:]
        high, low = hidden[p, :hid, cols], hidden[p, hid:, cols]
        stacked = jnp.concatenate(
            [twice(high, 1), jnp.concatenate([low, jnp.zeros_like(low)], axis=1)], axis=0
        )
        acc_out[...] += dot(g_radial[slot], stacked, NT)
        from_hot = one_hot(send[k, :, cols], atoms)
        g_lifted[p] += dot(g_feats[slot], twice(from_hot, 1), NT)

    def combine(t, slot):
        p, _, cols = chunk_at(table, t, chunk)
        rows = [geo[p, ROW_Y + m : ROW_Y + m + 1, cols] for m in range(16)]
        backward_messages(
            feats.at[slot], radial.at[slot], grads.at[slot], rows, g_radial.at[slot],
            g_feats.at[slot], channels, chunk,
        )

    def step(i, carry):
        t = 2 * i
        combine(t, 0)
        prepare(t + 1, 1)
        collect(t - 1, 1)
        combine(t + 1, 1)
        prepare(t + 2, 0)
        collect(t, 0)
        return carry

    prepare(0, 0)
    lax.fori_loop(0, total // 2, step, 0)
    collect(total // 2 * 2 - 1, 1)

    @pl.when(total % 2 == 1)
    def _():
        combine(total - 1, 0)
        collect(total - 1, 0)

    w_up_parts = [split(w_up[0]), split(w_up[1])]
    sums = [None, None] if first else [acc_up_in[0], acc_up_in[1]]
    for p in range(n):
        lifted_grads = [component(g_lifted[p], comp, 4) for comp in range(4)]
        for kind in range(2):
            count = 1 + 2 * kind
            own = lifted_grads[kind : kind + count]
            tall = jnp.concatenate([value.T for value in own], axis=0)
            back = dot1(tall, w_up_parts[kind], NT)
            for a, value in enumerate(rows_of(back, count)):
                x_grads[p][kind + a] = value
            x = x_refs[p][kind * atoms : (kind + count) * atoms, :]
            part = dot1(jnp.concatenate(own, axis=1), x)
            sums[kind] = part if sums[kind] is None else sums[kind] + part
    if last:
        both = acc_out[...]
        both = both[:, :hid] + both[:, hid:]
        paths = both.shape[0] // channels
        up_at = paths * hid
        end = up_at + 2 * channels
        flat[end:, :] = jnp.zeros_like(flat[end:, :])
        for path in range(paths):
            flat[path * hid : (path + 1) * hid, :] = component(both, path, paths).T
        for kind in range(2):
            row = up_at + kind * channels
            flat[row : row + channels, :] = sums[kind].T
        deal(flat, digits[0, 0], parts)
    else:
        for kind in range(2):
            g_up[kind] = sums[kind]
        g_out[...] = acc_out[...]


def mlp_backward_kernel(groups, sources, *refs):
    counts, refs = refs[0], refs[1:]
    number = len(groups)
    geos, grads, refs = refs[:number], refs[number : 2 * number], refs[2 * number :]
    tapes, refs = refs[: 2 * len(sources)], refs[2 * len(sources) :]
    w_in, w_mid, small, acc_in, acc_mid = refs
    n_basis, hid = w_in.shape
    w_mid_n = [wcat3(w_mid[0], 1), wcat3(w_mid[1], 1)]
    acc_in[...] = jnp.zeros_like(acc_in)
    acc_mid[...] = jnp.zeros_like(acc_mid)
    edges = geos[0].shape[2]
    lane = lax.broadcasted_iota(jnp.int32, (hid, edges), 1)

    for i, (place, first) in enumerate(sources):
        kept_h, kept_d = tapes[2 * i], tapes[2 * i + 1]

        def one(at, place=place, first=first, kept_h=kept_h, kept_d=kept_d):
            slots, geo, grad = groups[place], geos[place], grads[place]
            p = first + at
            k = slots[0]
            for position, slot in enumerate(slots):
                k = jnp.where(p == position, slot, k)
            g3 = grad[p] * geo[p, ROW_ENV : ROW_ENV + 1, :]
            d3 = jnp.where(lane < counts[0, k], g3, 0.0) * kept_d[at, 2 * hid :, :]
            high, low = split(d3)
            acc_mid[1] += dot(kept_h[at, 2 * hid :, :], jnp.concatenate([high, low], axis=0), NT)
            d2 = dot(w_mid_n[1], jnp.concatenate([high, high, low], axis=0))
            d2 = d2 * kept_d[at, hid : 2 * hid, :]
            high, low = split(d2)
            acc_mid[0] += dot(kept_h[at, : 2 * hid, :], jnp.concatenate([high, low], axis=0), NT)
            d1 = dot(w_mid_n[0], jnp.concatenate([high, high, low], axis=0)) * kept_d[at, :hid, :]
            bessel = geo[p, :8, :]
            b_high = bessel.astype(BF16).astype(F32)
            basis = jnp.concatenate([b_high, bessel - b_high], axis=0).astype(BF16)
            high, low = split(d1)
            acc_in[...] += dot(basis, jnp.concatenate([high, low], axis=0), NT)

        in_pairs(kept_h.shape[0], one)

    def quadrants(v, rows):
        return v[:rows, :hid] + v[:rows, hid:] + v[rows:, :hid]

    small[hid + n_basis :, :] = jnp.zeros_like(small[hid + n_basis :, :])
    small[:hid, :] = jnp.concatenate([quadrants(acc_mid[layer], hid) for layer in range(2)], axis=1)
    basis_grad = quadrants(acc_in[...], n_basis)
    small[hid : hid + n_basis, :] = jnp.concatenate([basis_grad, jnp.zeros_like(basis_grad)], axis=1)


def call(kernel, out_shape, smem, scratch, args, name, us):
    specs = [SMEM] * smem + [VMEM] * (len(args) - smem)
    return call_with(kernel, out_shape, specs, scratch, args, name, us)


def call_with(kernel, out_shape, specs, scratch, args, name, us):
    return pl.pallas_call(
        kernel,
        out_shape=out_shape,
        in_specs=specs,
        out_specs=jax.tree.map(lambda _: VMEM, out_shape),
        scratch_shapes=scratch,
        compiler_params=pltpu.CompilerParams(vmem_limit_bytes=LIMIT),
        cost_estimate=pl.CostEstimate(
            flops=int(us * 5e8), bytes_accessed=int(us * 2e6), transcendentals=0
        ),
        name=name,
    )(*args)


def shape(*dims, dtype=F32):
    return jax.ShapeDtypeStruct(dims, dtype)


def shifted(value, steps):
    count = lax.axis_size("blk")
    return lax.ppermute(value, "blk", [(i, (i + steps) % count) for i in range(count)])


def stages_of(count):
    stages, stride = [], 1
    while stride < count:
        members = 4 if (count // stride) % 4 == 0 else 2
        stages.append((members, stride))
        stride *= members
    return stages[::-1]


def exchange(values, stage):
    members, stride = stage
    count = lax.axis_size("blk")
    moved = [
        lax.ppermute(values[k], "blk", [(i, i ^ (k * stride)) for i in range(count)])
        for k in range(1, members)
    ]
    return [values[0]] + moved


def add_parts(groups, stages, at, digits):
    arrays = [part for parts, _ in groups for part in parts]
    counts = tuple((len(parts), tuple(sizes)) for parts, sizes in groups)
    total = sum(size for _, sizes in groups for size in sizes)
    out = stages[at + 1][0] if at + 1 < len(stages) else 1
    shapes = shape(total, LANES)
    if out > 1:
        shapes = tuple(shape(total // out, LANES) for _ in range(out))
    return call(
        functools.partial(add_kernel, at + 1, counts, out), shapes, 1,
        [pltpu.VMEM((total, LANES), F32)] if out > 1 else [], (digits, *arrays), f"add_{at}", 1,
    )


def join_parts(parts, segments, stages, at, digits, tail):
    members = stages[at][0]
    rows = members * sum(rows * blocks for rows, blocks in segments) + tail
    return call(
        functools.partial(join_kernel, at, members, segments, tail), shape(rows, LANES), 1,
        [pltpu.VMEM((members, tail, LANES), F32)] if tail else [], (digits, *parts),
        f"join_{at}", 1,
    )


def per_device(
    node_scalars, node_vectors, positions, species, edge_senders, edge_receivers, edge_shifts,
    bucket_counts, w_up, w_rad_in, w_rad_mid, w_rad_out, w_lin, w_sc_scalar, w_sc_vector, w_prod,
    w_skip, w_read, cot_scalars, cot_vectors, cot_energy,
):
    _, buckets, slots = edge_senders.shape
    send = edge_senders.reshape(buckets, 1, slots)
    recv = edge_receivers.reshape(buckets, 1, slots)
    shift = edge_shifts.reshape(3 * buckets, 1, slots)
    reach = (buckets - 1) // 2
    atoms, channels = node_scalars.shape
    hid, outs = w_rad_out.shape
    n_basis = w_rad_in.shape[0]
    n_spec = w_skip.shape[1]
    chunk = min(256, slots)
    blocks = lax.axis_size("blk")
    stages = stages_of(blocks)
    me = lax.axis_index("blk")
    digits = jnp.stack([(me // stride) % members for members, stride in stages]).reshape(1, -1)
    rows, at = [], 0
    height = up8(4 * atoms + 6)
    for piece in (node_scalars, node_vectors.reshape(3 * atoms, channels), positions,
                  species.reshape(1, atoms), cot_energy.reshape(1, atoms),
                  w_read.reshape(1, channels)):
        end = at + piece.shape[0]
        rows.append(jnp.pad(piece, ((at, height - end), (0, 0))).astype(F32))
        at = end
    packed = functools.reduce(jnp.add, rows)
    offsets = sorted([d for d in range(-reach, reach + 1) if d], key=abs)
    x_of = {reach: packed, **{reach + d: shifted(packed, -d) for d in offsets}}
    sc_s_t, sc_v_t = jnp.swapaxes(w_sc_scalar, 0, 1), jnp.swapaxes(w_sc_vector, 0, 1)

    skip_rows = 2 * n_spec * channels
    g_total, skip_s, skip_v, skip_gs, skip_gv, g_skip = call(
        skip_kernel,
        (shape(2, atoms, channels), shape(atoms, channels), shape(3, atoms, channels),
         shape(atoms, channels), shape(3, atoms, channels), shape(skip_rows, channels)),
        0, [],
        (packed, cot_scalars, cot_vectors, w_skip),
        "self_connection", 4,
    )

    def padded(rows):
        unit = 8 * blocks
        return -(-rows // unit) * unit

    node_rows = padded(skip_rows + 6 * channels + up8(9 * n_spec) + up8(5 * n_spec) + 8)
    edge_rows = padded(outs // channels * hid + 2 * channels)
    tail_unit = 8 * (blocks // stages[0][0])
    small_rows = -(-(hid + n_basis) // tail_unit) * tail_unit

    near = (reach - 1, reach + 1)
    far = tuple(k for k in range(buckets) if abs(k - reach) > 1)
    groups = [(reach,), near] + ([far] if far else [])
    most = [len(g) * (slots // chunk) for g in groups]
    first_parts = stages[0][0]
    acc = ()
    kept, tapes = [], []
    for at, group in enumerate(groups):
        n = len(group)
        last = at == len(groups) - 1
        base = len(groups[1]) if at == 2 else 0
        out_shapes = (
            shape(base + n, 4 * channels, 2 * atoms, dtype=BF16), shape(base + n, 2 * hid, slots, dtype=BF16),
            shape(base + n, GEO_ROWS, slots), shape(n, 4 * hid, slots, dtype=BF16),
            shape(n, 3 * hid, slots),
        )
        scratch = [
            pltpu.SMEM((3, most[at]), jnp.int32),
            pltpu.VMEM((2, 4 * channels, chunk), F32),
            pltpu.VMEM((2, outs, chunk), F32),
            pltpu.VMEM((2, 16 * channels, 2 * chunk), BF16),
        ]
        node_args, node_counts = (), None
        if last:
            node_args = (digits, w_lin, sc_s_t, sc_v_t, w_prod, g_total,
                         cot_vectors, skip_s, skip_v, g_skip)
            node_outs = (
                shape(atoms, channels), shape(3, atoms, channels), shape(1, atoms),
                shape(16 * channels, 2 * atoms, dtype=BF16),
                *[shape(node_rows // first_parts, LANES)] * first_parts,
            )
            node_counts = len(node_args), len(node_outs)
            scratch = [
                pltpu.VMEM((16 * channels, atoms), F32), pltpu.VMEM((node_rows, LANES), F32)
            ] + scratch
            out_shapes = node_outs + out_shapes
        else:
            out_shapes = (shape(16 * channels, atoms),) + out_shapes
        args = (
            bucket_counts, send, recv, shift, packed, *[x_of[k] for k in group], w_up, w_rad_in,
            w_rad_mid, w_rad_out, *acc, *(kept[-1] if base else ()), *node_args,
        )
        specs = [SMEM] + [VMEM] * (len(args) - 1)
        if last:
            specs[len(args) - len(node_args)] = SMEM
        result = call_with(
            functools.partial(forward_kernel, base, group, chunk, at == 0, node_counts), out_shapes,
            specs, scratch, args, f"edges_{at}", 5 * n + (6 if last else 0),
        )
        kept.append(result[-5:-2])
        tapes.append(result[-2:])
        if last:
            new_s, new_v, energy, grad_amp = result[:4]
            node_parts = result[4 : 4 + first_parts]
        else:
            acc = result[:1]

    tie = lax.optimization_barrier
    node_parts = exchange(node_parts, stages[0])
    others = tuple(k for group in groups[1:] for k in group)
    sums = ()
    n_early = len(others) // 2
    grads_hidden = []
    home = []
    for group, (lifted, hidden, geo) in ((others, kept[-1]), (groups[0], kept[0])):
        n = len(group)
        first, last = not sums, bool(sums)
        if last:
            final = (shape(edge_rows // first_parts, LANES),) * first_parts
        else:
            final = (shape(outs, 2 * hid), shape(2, channels, channels))
        args = (
            bucket_counts, digits, send, recv, grad_amp, geo, lifted, hidden,
            *[x_of[k] for k in group], w_up, w_rad_out, *sums,
        )
        result = call(
            functools.partial(backward_kernel, group, chunk, first, last, first_parts),
            (*[shape(4, atoms, channels) for _ in group], shape(n, hid, slots), *final), 2,
            ([pltpu.VMEM((edge_rows, LANES), F32)] if last else [])
            + [
                pltpu.SMEM((3, n * (slots // chunk)), jnp.int32),
                pltpu.VMEM((2, 4 * channels, chunk), F32),
                pltpu.VMEM((2, outs, chunk), F32),
                pltpu.VMEM((2, 16 * channels, chunk), F32),
                pltpu.VMEM((2, outs, 2 * chunk), BF16),
                pltpu.VMEM((2, 4 * channels, 2 * chunk), BF16),
                pltpu.VMEM((n, 4 * channels, atoms), F32),
                pltpu.VMEM((outs, 2 * hid), F32),
            ],
            args, "edges_back_own" if last else "edges_back", 6 * n,
        )
        if first:
            result, node_parts = tie((result, node_parts))
            away = [(k - reach, value) for k, value in zip(group, result[:n])]
            away.sort(key=lambda pair: -abs(pair[0]))
            home = [shifted(value, offset) for offset, value in away[:n_early]]
        else:
            values = [value for _, value in away[n_early:]]
            result, early, values = tie((result, home, values))
            late = [shifted(value, offset) for (offset, _), value in zip(away[n_early:], values)]
            edge_parts = exchange(result[n + 1 :], stages[0])
            home = early + [result[0]]
        grads_hidden.append(result[n])
        sums = result[n + 1 :]
    sources, first = [], 0
    for tape in tapes[1:]:
        sources.append((0, first))
        first += tape[0].shape[0]
    sources.append((1, 0))
    small = call(
        functools.partial(mlp_backward_kernel, (others, groups[0]), sources),
        shape(small_rows, LANES), 1,
        [pltpu.VMEM((2 * n_basis, 2 * hid), F32), pltpu.VMEM((2, 2 * hid, 2 * hid), F32)],
        (bucket_counts, kept[-1][2], kept[0][2], *grads_hidden,
         *[array for tape in tapes[1:] + tapes[:1] for array in tape], w_rad_in, w_rad_mid),
        "radial_back", 7,
    )
    small, edge_parts = tie((small, edge_parts))
    sizes = [node_rows // first_parts, edge_rows // first_parts, small_rows]
    groups = [(node_parts, sizes[:1]), (edge_parts, sizes[1:2]), ([small], sizes[2:])]
    whole = add_parts(groups, stages, 0, digits)
    for at in range(1, len(stages)):
        sizes = [size // stages[at][0] for size in sizes]
        parts = exchange(whole, stages[at])
        if at == 1:
            parts, late = tie((parts, late))
            home = home + late
        whole = add_parts([(parts, sizes)], stages, at, digits)
    blocks_now, tail_blocks = 1, 1
    for at in range(len(stages)):
        members = stages[at][0]
        parts = exchange([whole] * members, stages[at])
        segments = [(sizes[0], blocks_now), (sizes[1], blocks_now)]
        if at:
            segments.append((sizes[2], tail_blocks))
            tail_blocks *= members
        blocks_now *= members
        if at + 1 < len(stages):
            whole = join_parts(parts, segments, stages, at, digits, 0 if at else sizes[2])
    g_skip, g_lin, g_prod, g_sc_s, g_sc_v, g_read, g_out, g_up, g_mid, g_in = call(
        functools.partial(finish_kernel, len(stages) - 1, stages[-1][0], segments, n_spec),
        (shape(skip_rows, channels), shape(4 * channels, channels), shape(2 * channels, channels),
         shape(9, n_spec, channels), shape(5, n_spec, channels), shape(1, channels),
         shape(hid, outs), shape(2 * channels, channels), shape(2, hid, hid), shape(n_basis, hid)),
        1,
        [pltpu.VMEM((node_rows + edge_rows + small_rows, LANES), F32)],
        (digits, *parts), "finish", 2,
    )
    gx = home[0]
    for part in home[1:]:
        gx = gx + part
    return (
        new_s, new_v, energy.reshape(-1), gx[0] + skip_gs, gx[1:] + skip_gv,
        g_up.reshape(1, 2, channels, channels), g_in[None], g_mid[None], g_out[None],
        g_lin.reshape(1, 4, channels, channels), jnp.swapaxes(g_sc_s, 0, 1)[None],
        jnp.swapaxes(g_sc_v, 0, 1)[None], g_prod.reshape(1, 2, channels, channels),
        g_skip.reshape(1, 2, n_spec, channels, channels), g_read,
    )


def solution(mesh):
    atoms = ("cell", "blk")
    in_specs = (
        P(atoms, None), P(None, atoms, None), P(None, atoms), P(atoms), P(atoms, None, None),
        P(atoms, None, None), P(atoms, None, None, None), P(atoms, None),
        P(), P(), P(), P(), P(), P(), P(), P(), P(), P(),
        P(atoms, None), P(None, atoms, None), P(atoms),
    )
    out_specs = (
        P(atoms, None), P(None, atoms, None), P(atoms), P(atoms, None), P(None, atoms, None),
        P("cell", None, None, None), P("cell", None, None), P("cell", None, None, None),
        P("cell", None, None), P("cell", None, None, None), P("cell", None, None, None),
        P("cell", None, None, None), P("cell", None, None, None),
        P("cell", None, None, None, None), P("cell", None),
    )
    return jax.shard_map(
        per_device, mesh=mesh, in_specs=in_specs, out_specs=out_specs, check_vma=False
    )
```

```python
import functools
import math

import jax
import jax.numpy as jnp
from jax import lax
from jax.experimental import pallas as pl
from jax.experimental.pallas import tpu as pltpu
from jax.sharding import PartitionSpec as P

CUTOFF = 5.0
SOFTEN = 0.1
NEIGH = 0.17677669529663687
F32 = jnp.float32
BF16 = jnp.bfloat16
LANES = 128
VMEM = pl.BlockSpec(memory_space=pltpu.VMEM)
SMEM = pl.BlockSpec(memory_space=pltpu.SMEM)
LIMIT = 20 * 1024 * 1024

NN = (((1,), (0,)), ((), ()))
NT = (((1,), (1,)), ((), ()))


BLOCK = 16


def row_of(comp, count, channel):
    return (channel // BLOCK * count + comp) * BLOCK


def by_block(parts):
    channels = parts[0].shape[0]
    return jnp.concatenate(
        [part[c : c + BLOCK] for c in range(0, channels, BLOCK) for part in parts], axis=0
    )


def component(value, comp, count):
    step = count * BLOCK
    at = comp * BLOCK
    return jnp.concatenate(
        [value[r + at : r + at + BLOCK] for r in range(0, value.shape[0], step)], axis=0
    )


def split(v):
    high = v.astype(BF16)
    return high, (v - high.astype(F32)).astype(BF16)


def dot(a, b, dims=NN):
    return lax.dot_general(a, b, dims, preferred_element_type=F32)


def dot3(a, b, dims=NN):
    ah, al = a if isinstance(a, tuple) else split(a)
    bh, bl = b if isinstance(b, tuple) else split(b)
    return dot(ah, bh, dims) + (dot(ah, bl, dims) + dot(al, bh, dims))


def dot1(a, b, dims=NN):
    ah, al = a if isinstance(a, tuple) else split(a)
    bh, bl = b if isinstance(b, tuple) else split(b)
    left = jnp.concatenate([ah, ah, al], axis=1)
    right = jnp.concatenate([bh, bl, bh], axis=dims[0][1][0])
    return dot(left, right, dims)


def rows_of(v, count):
    step = v.shape[0] // count
    return [v[at * step : (at + 1) * step] for at in range(count)]


def columns_of(v, count):
    step = v.shape[1] // count
    return [v[:, at * step : (at + 1) * step] for at in range(count)]


def cat3(v, axis):
    high, low = split(v)
    return jnp.concatenate([high, high, low], axis=axis)


def wcat3(v, axis):
    high, low = split(v)
    return jnp.concatenate([high, low, high], axis=axis)


def column(row, width):
    return jnp.broadcast_to(row, (width, row.shape[1])).T


ROW_Y = 8
ROW_ENV = 24
GEO_ROWS = 32


def write_geometry(geo, base, slots, counts, send, recv, shift, tables, own_pos):
    buckets, _, edges = send.shape
    bucket_of = lax.broadcasted_iota(jnp.int32, (buckets, LANES), 0)
    filled = jnp.zeros((buckets, LANES), jnp.int32)
    for k in slots:
        filled = jnp.where(bucket_of == k, counts[0, k], filled)
    own = [jnp.broadcast_to(own_pos[a : a + 1, :], (buckets, LANES)) for a in range(3)]
    lane = lax.broadcasted_iota(jnp.int32, (buckets, LANES), 1)
    for block in range(edges // LANES):
        cols = slice(block * LANES, (block + 1) * LANES)

        def put(row, value):
            for p, k in enumerate(slots, base):
                geo[p, row : row + 1, cols] = value[k : k + 1]

        from_idx = jnp.concatenate([send[k, :, cols] for k in range(buckets)], axis=0)
        to_idx = jnp.concatenate([recv[k, :, cols] for k in range(buckets)], axis=0)
        rel = []
        for a in range(3):
            there = jnp.take_along_axis(tables[a], from_idx, axis=1, mode="promise_in_bounds")
            here = jnp.take_along_axis(own[a], to_idx, axis=1, mode="promise_in_bounds")
            moved = jnp.concatenate([shift[3 * k + a, :, cols] for k in range(buckets)], axis=0)
            rel.append(there - here + moved.astype(F32))
        dist = jnp.sqrt(rel[0] * rel[0] + rel[1] * rel[1] + rel[2] * rel[2] + SOFTEN)
        inverse = 1.0 / dist
        x, y, z = (r * inverse for r in rel)
        angle = dist * (math.pi / CUTOFF)
        sine, twice = jnp.sin(angle), 2.0 * jnp.cos(angle)
        scale = math.sqrt(2.0 / CUTOFF) * inverse
        before, now = jnp.zeros_like(sine), sine
        for n in range(8):
            put(n, now * scale)
            before, now = now, twice * now - before
        xx, yy, zz = x * x, y * y, z * z
        planar = xx + yy
        rows = [
            jnp.ones_like(x),
            math.sqrt(3.0) * x,
            math.sqrt(3.0) * y,
            math.sqrt(3.0) * z,
            math.sqrt(15.0) * x * y,
            math.sqrt(15.0) * y * z,
            0.5 * math.sqrt(5.0) * (2.0 * zz - planar),
            math.sqrt(15.0) * x * z,
            0.5 * math.sqrt(15.0) * (xx - yy),
            math.sqrt(35.0 / 8.0) * (3.0 * xx - yy) * y,
            math.sqrt(105.0) * x * y * z,
            math.sqrt(21.0 / 8.0) * y * (4.0 * zz - planar),
            0.5 * math.sqrt(7.0) * z * (2.0 * zz - 3.0 * planar),
            math.sqrt(21.0 / 8.0) * x * (4.0 * zz - planar),
            0.5 * math.sqrt(105.0) * z * (xx - yy),
            math.sqrt(35.0 / 8.0) * (xx - 3.0 * yy) * x,
        ]
        for m, row in enumerate(rows):
            put(ROW_Y + m, row)
        q = dist * (1.0 / CUTOFF)
        q6 = q * q * q * q * q * q
        envelope = 1.0 - 28.0 * q6 + 48.0 * q6 * q - 21.0 * q6 * q * q
        put(ROW_ENV, jnp.where(lane + block * LANES < filled, envelope, 0.0))


def one_hot(index_row, atoms):
    edges = index_row.shape[1]
    atom = lax.broadcasted_iota(jnp.int32, (atoms, edges), 0)
    return jnp.where(atom == index_row, 1.0, 0.0).astype(BF16)


def twice(v, axis):
    return jnp.concatenate([v, v], axis=axis)


def silu_parts(v):
    gate = 0.5 + 0.5 * jnp.tanh(0.5 * v)
    return v * gate, gate


def basis_stack(bessel):
    high = bessel.astype(BF16).astype(F32)
    return jnp.concatenate([high, high, bessel - high], axis=0).astype(BF16)


def lift(x_ref, w_up_t, out):
    atoms = out.shape[1] // 2
    scalars = dot1(w_up_t[0], x_ref[:atoms, :], NT)
    vectors = dot1(w_up_t[1], x_ref[atoms : 4 * atoms, :], NT)
    parts = [split(value) for value in [scalars] + columns_of(vectors, 3)]
    out[:, :atoms] = by_block([high for high, _ in parts])
    out[:, atoms:] = by_block([low for _, low in parts])


def radial_weights(w_out, channels):
    w_t = w_out[...].T
    return by_block([w_t[at : at + channels] for at in range(0, w_t.shape[0], channels)])


def list_chunks(table, slots, counts, chunk, base=0):
    table[0, 0], table[1, 0], table[2, 0] = base, slots[0], 0
    total = 0
    for p, k in enumerate(slots, base):
        number = (counts[0, k] + chunk - 1) // chunk

        def note(j, at, p=p, k=k):
            table[0, at] = p
            table[1, at] = k
            table[2, at] = j * chunk
            return at + 1

        total = lax.fori_loop(0, number, note, total)
    return total


def chunk_at(table, t, chunk):
    return table[0, t], table[1, t], pl.ds(pl.multiple_of(table[2, t], chunk), chunk)


def forward_messages(feats, radial, geo_rows, out, channels, edges):
    ys = []
    for half in range(edges // LANES):
        cols = slice(half * LANES, (half + 1) * LANES)
        ys.append([jnp.broadcast_to(row[:, cols], (BLOCK, LANES)) for row in geo_rows])
    for c in range(0, channels, BLOCK):
        for half in range(edges // LANES):
            cols = slice(half * LANES, (half + 1) * LANES)
            low_cols = slice(edges + half * LANES, edges + (half + 1) * LANES)
            y = ys[half]

            def feat(k):
                at = row_of(k, 4, c)
                return feats[at : at + BLOCK, cols]

            def rad(k):
                at = row_of(k, 7, c)
                return radial[at : at + BLOCK, cols]

            def put(comp, value):
                high, low = split(value)
                at = row_of(comp, 16, c)
                out[at : at + BLOCK, cols] = high
                out[at : at + BLOCK, low_cols] = low

            s, v = feat(0), [feat(1), feat(2), feat(3)]
            inner = y[1] * v[0] + y[2] * v[1] + y[3] * v[2]
            put(0, rad(0) * s + rad(4) * inner)
            first, fifth, sixth = rad(1) * s, rad(5), rad(6)
            put(1, first * y[1] + fifth * v[0] + sixth * (y[2] * v[2] - y[3] * v[1]))
            put(2, first * y[2] + fifth * v[1] + sixth * (y[3] * v[0] - y[1] * v[2]))
            put(3, first * y[3] + fifth * v[2] + sixth * (y[1] * v[1] - y[2] * v[0]))
            second = rad(2) * s
            for m in range(4, 9):
                put(m, second * y[m])
            third = rad(3) * s
            for m in range(9, 16):
                put(m, third * y[m])


def in_pairs(count, one):
    if count > 1:
        def pair(i, carry):
            one(2 * i)
            one(2 * i + 1)
            return carry

        if count < 4:
            pair(0, 0)
        else:
            lax.fori_loop(0, count // 2, pair, 0)
    if count % 2:
        one(count - 1)


def radial_hidden(base, count, w_in, w_mid, geo, hidden_out, kept_h, kept_d):
    hid = w_in.shape[1]
    w_in_t = wcat3(w_in[...].T, 1)
    w_mid_t = [wcat3(w_mid[0].T, 1), wcat3(w_mid[1].T, 1)]

    def one(at):
        p = base + at
        value = dot(w_in_t, basis_stack(geo[p, :8, :]))
        for layer in range(3):
            h, gate = silu_parts(value)
            kept_d[at, layer * hid : (layer + 1) * hid, :] = gate + h * (1.0 - gate)
            if layer < 2:
                high, low = split(h)
                kept_h[at, 2 * layer * hid : (2 * layer + 1) * hid, :] = high
                kept_h[at, (2 * layer + 1) * hid : (2 * layer + 2) * hid, :] = low
                value = dot(w_mid_t[layer], jnp.concatenate([high, high, low], axis=0))
        high, low = split(h * geo[p, ROW_ENV : ROW_ENV + 1, :])
        hidden_out[p, :hid, :] = high
        hidden_out[p, hid:, :] = low

    in_pairs(count, one)


def edge_forward(
    base, slots, chunk, counts, send, recv, shift, own_pos, tables, x_refs, w_up, w_in, w_mid, w_out,
    lifted_out, hidden_out, geo, kept_h, kept_d, acc, table, feats, radial, messages,
):
    channels, atoms = w_up.shape[1], acc.shape[1]
    hid = w_in.shape[1]
    total = list_chunks(table, slots, counts, chunk, base)
    write_geometry(geo, base, slots, counts, send, recv, shift, tables, own_pos)
    w_up_t = [split(w_up[0].T), split(w_up[1].T)]
    for p in range(len(slots)):
        lift(x_refs[p], w_up_t, lifted_out.at[base + p])
    radial_hidden(base, len(slots), w_in, w_mid, geo, hidden_out, kept_h, kept_d)
    w_out_t = wcat3(radial_weights(w_out, channels), 1)
    messages[1] = jnp.zeros_like(messages[1])

    def prepare(t, slot):
        p, k, cols = chunk_at(table, jnp.minimum(t, total - 1), chunk)
        high, low = hidden_out[p, :hid, cols], hidden_out[p, hid:, cols]
        radial[slot] = dot(w_out_t, jnp.concatenate([high, high, low], axis=0))
        from_hot = one_hot(send[k, :, cols], atoms)
        feats[slot] = dot(lifted_out[p], twice(from_hot, 0))

    def collect(t, slot):
        _, k, cols = chunk_at(table, jnp.maximum(t, 0), chunk)
        to_hot = one_hot(recv[k, :, cols], atoms)
        acc[...] += dot(messages[slot], twice(to_hot, 1), NT)

    def combine(t, slot):
        p, _, cols = chunk_at(table, t, chunk)
        rows = [geo[p, ROW_Y + m : ROW_Y + m + 1, cols] for m in range(16)]
        forward_messages(
            feats.at[slot], radial.at[slot], rows, messages.at[slot], channels, chunk
        )

    def step(i, carry):
        t = 2 * i
        combine(t, 0)
        prepare(t + 1, 1)
        collect(t - 1, 1)
        combine(t + 1, 1)
        prepare(t + 2, 0)
        collect(t, 0)
        return carry

    prepare(0, 0)
    lax.fori_loop(0, total // 2, step, 0)
    collect(total // 2 * 2 - 1, 1)

    @pl.when(total % 2 == 1)
    def _():
        combine(total - 1, 0)
        collect(total - 1, 0)


def forward_kernel(base, slots, chunk, first, node_counts, *refs):
    n = len(slots)
    counts, send, recv, shift, refs = *refs[:4], refs[4:]
    x_own, x_refs, refs = refs[0], refs[1 : 1 + n], refs[1 + n :]
    w_up, w_in, w_mid, w_out, refs = *refs[:4], refs[4:]
    atoms = w_up.shape[1]
    at = 4 * atoms
    if not first:
        acc_in, refs = refs[0], refs[1:]
    before, refs = refs[: 3 if base else 0], refs[3 if base else 0 :]
    if node_counts:
        n_in, n_out = node_counts
        node_in, node_out, refs = refs[:n_in], refs[n_in : n_in + n_out], refs[n_in + n_out :]
        lifted_out, hidden_out, geo, kept_h, kept_d, acc, flat = refs[:7]
        table, feats, radial, messages = refs[7:]
    else:
        acc, lifted_out, hidden_out, geo, kept_h, kept_d = refs[:6]
        table, feats, radial, messages = refs[6:]
    if first:
        acc[...] = jnp.zeros_like(acc)
    else:
        acc[...] = acc_in[...]
    for ref, out in zip(before, (lifted_out, hidden_out, geo)):
        out[:base] = ref[...]
    tables = []
    for a in range(3):
        rows = [x_own[at + a : at + a + 1, :]] * send.shape[0]
        for k, ref in zip(slots, x_refs):
            rows[k] = ref[at + a : at + a + 1, :]
        tables.append(jnp.concatenate(rows, axis=0))
    edge_forward(
        base, slots, chunk, counts, send, recv, shift, x_own.at[at : at + 8], tables, x_refs, w_up, w_in,
        w_mid, w_out, lifted_out, hidden_out, geo, kept_h, kept_d, acc, table, feats, radial,
        messages,
    )
    if node_counts:
        rows = [x_own[at + 3 : at + 4, :], x_own[at + 5 : at + 6, :]]
        node_stage(acc, flat, *rows, *node_in, *node_out)


def deal(flat, digit, parts):
    rows = parts[0].shape[0]
    for k, part in enumerate(parts):
        at = pl.multiple_of((digit ^ k) * rows, 8)
        part[...] = flat[pl.ds(at, rows), :]


def add_kernel(stage, groups, n_out, *refs):
    digits, refs = refs[0], refs[1:]
    totals = []
    for count, sizes in groups:
        total = functools.reduce(jnp.add, [part[...] for part in refs[:count]])
        refs = refs[count:]
        at = 0
        for size in sizes:
            totals.append(total[at : at + size])
            at += size
    if n_out == 1:
        at = 0
        for total in totals:
            refs[0][at : at + total.shape[0], :] = total
            at += total.shape[0]
        return
    outs, scratch = refs[:n_out], refs[n_out]
    at, out_at = 0, 0
    for total in totals:
        size = total.shape[0]
        scratch[at : at + size, :] = total
        rows = size // n_out
        for k, out in enumerate(outs):
            first = pl.multiple_of(at + (digits[0, stage] ^ k) * rows, 8)
            out[out_at : out_at + rows, :] = scratch[pl.ds(first, rows), :]
        at += size
        out_at += rows


def join_into(out, digit, inputs, segments):
    radix = len(inputs)
    at, out_at = 0, 0
    for rows, blocks in segments:
        for _ in range(blocks):
            for k, part in enumerate(inputs):
                first = pl.multiple_of(out_at + (digit ^ k) * rows, 8)
                out[pl.ds(first, rows), :] = part[at : at + rows, :]
            at += rows
            out_at += rows * radix


def join_kernel(stage, radix, segments, tail, *refs):
    digits, inputs, out = refs[0], refs[1 : 1 + radix], refs[1 + radix]
    digit = digits[0, stage]
    join_into(out, digit, inputs, segments)
    if tail:
        store = refs[2 + radix]
        for k, part in enumerate(inputs):
            store[digit ^ k] = part[part.shape[0] - tail :, :]
        total = store[0]
        for member in range(1, radix):
            total = total + store[member]
        out[out.shape[0] - tail :, :] = total


def finish_kernel(stage, radix, segments, n_spec, *refs):
    digits, inputs, refs = refs[0], refs[1 : 1 + radix], refs[1 + radix :]
    node_outs, (g_out, g_up, g_mid, g_in, flat) = refs[:6], refs[6:]
    join_into(flat, digits[0, stage], inputs, segments)
    ends = []
    for rows, blocks in segments:
        ends.append((ends[-1] if ends else 0) + rows * blocks * radix)
    at = 0
    for out in node_outs:
        if len(out.shape) == 3:
            for p in range(out.shape[0]):
                out[p] = flat[at + p * n_spec : at + (p + 1) * n_spec, :]
            at += up8(out.shape[0] * n_spec)
        else:
            out[...] = flat[at : at + out.shape[0], :]
            at += up8(out.shape[0])
    at = ends[0]
    hid, n_basis = g_out.shape[0], g_in.shape[0]
    for path in range(g_out.shape[1] // LANES):
        g_out[:, path * LANES : (path + 1) * LANES] = flat[at : at + hid, :]
        at += hid
    g_up[...] = flat[at : at + g_up.shape[0], :]
    small = flat[ends[1] : ends[2], :]
    g_mid[0] = small[:hid, :hid]
    g_mid[1] = small[:hid, hid:]
    g_in[...] = small[hid : hid + n_basis, :hid]


DEGREE = (0, 1, 1, 1, 2, 2, 2, 2, 2, 3, 3, 3, 3, 3, 3, 3)


def species_hot(species_row, count):
    atoms = species_row.shape[1]
    which = lax.broadcasted_iota(jnp.int32, (count, atoms), 0)
    return jnp.where(which == species_row, 1.0, 0.0)


def up8(rows):
    return (rows + 7) // 8 * 8


def node_stage(
    acc, flat, species, w_read, digits, w_lin, w_sc_s, w_sc_v, w_prod, g_total, cot_v, skip_s,
    skip_v, g_skip, new_s, new_v, energy, grad_amp, *parts,
):
    channels, atoms = w_lin.shape[1], acc.shape[1]
    n_spec = w_sc_s.shape[1]
    flat[g_skip.shape[0] :, :] = jnp.zeros_like(flat[g_skip.shape[0] :, :])
    flat[: g_skip.shape[0], :] = g_skip[...]
    lin_at = g_skip.shape[0]
    prod_at = lin_at + 4 * channels
    sc_s_at = prod_at + 2 * channels
    sc_v_at = sc_s_at + up8(9 * n_spec)
    read_at = sc_v_at + up8(5 * n_spec)
    members = [[m for m in range(16) if DEGREE[m] == l] for l in range(4)]
    amp_t = [component(acc, m, 16) * NEIGH for m in range(16)]
    amp_t_parts = [split(v) for v in amp_t]
    b = []
    for l in range(4):
        high = jnp.concatenate([amp_t_parts[m][0].T for m in members[l]], axis=0)
        low = jnp.concatenate([amp_t_parts[m][1].T for m in members[l]], axis=0)
        stacked = dot(jnp.concatenate([high, high, low], axis=1), wcat3(w_lin[l], 0))
        b.extend(stacked[j * atoms : (j + 1) * atoms] for j in range(len(members[l])))
    b0 = b[0]
    n1 = b[1] * b[1] + b[2] * b[2] + b[3] * b[3]
    n2 = b[4] * b[4] + b[5] * b[5] + b[6] * b[6] + b[7] * b[7] + b[8] * b[8]
    n3 = functools.reduce(jnp.add, [b[m] * b[m] for m in range(9, 16)])
    species_col = column(species, channels)
    masks = [species_col == float(s) for s in range(n_spec)]

    def per_atom(w, p):
        value = jnp.broadcast_to(w[p, :1, :], (atoms, channels))
        for s in range(1, n_spec):
            value = jnp.where(masks[s], w[p, s : s + 1, :], value)
        return value

    ws = [per_atom(w_sc_s, p) for p in range(9)]
    wv = [per_atom(w_sc_v, p) for p in range(5)]
    sq = b0 * b0
    terms = [b0, sq, n1, n2, n3, sq * b0, b0 * n1, b0 * n2, b0 * n3]
    mixed = functools.reduce(jnp.add, [w * t for w, t in zip(ws, terms)])
    factors = [None, b0, sq, n1, n2]
    factor = wv[0]
    for p in range(1, 5):
        factor = factor + wv[p] * factors[p]
    prod_parts = [split(w_prod[0]), split(w_prod[1])]
    out_s = dot1(mixed, prod_parts[0]) + skip_s[...]
    new_s[...] = out_s
    mixed_v = jnp.concatenate([b[1 + a] * factor for a in range(3)], axis=0)
    for a, value in enumerate(rows_of(dot1(mixed_v, prod_parts[1]), 3)):
        new_v[a] = value + skip_v[a]
    energy[...] = dot3(jnp.broadcast_to(w_read, (8, channels)), out_s, NT)[:1]
    cot_e = g_total[1]
    flat[read_at : read_at + 1, :] = jnp.sum(out_s * cot_e, axis=0, keepdims=True)

    g_s = split(g_total[0])
    g_v = split(jnp.concatenate([cot_v[a] for a in range(3)], axis=0))
    flat[prod_at : prod_at + channels, :] = dot1(mixed.T, g_s)
    flat[prod_at + channels : sc_s_at, :] = dot1(mixed_v.T, g_v)
    g_mixed = dot1(g_s, prod_parts[0], NT)
    g_mixed_v = rows_of(dot1(g_v, prod_parts[1], NT), 3)
    g_factor = functools.reduce(jnp.add, [g_mixed_v[a] * b[1 + a] for a in range(3)])

    hot = species_hot(species.astype(jnp.int32), 8).astype(BF16)
    values = [g_mixed * terms[p] for p in range(9)]
    values += [g_factor] + [g_factor * factors[p] for p in range(1, 5)]
    high, low = split(jnp.concatenate(values, axis=1))
    by_species = dot(twice(hot, 1), jnp.concatenate([high, low], axis=0))
    for p, value in enumerate(columns_of(by_species, len(values))):
        row = sc_s_at + p * n_spec if p < 9 else sc_v_at + (p - 9) * n_spec
        flat[row : row + n_spec, :] = value[:n_spec]

    g_b0 = g_mixed * (
        ws[0] + 2.0 * b0 * ws[1] + 3.0 * sq * ws[5] + n1 * ws[6] + n2 * ws[7] + n3 * ws[8]
    ) + g_factor * (wv[1] + 2.0 * b0 * wv[2])
    g_n1 = 2.0 * (g_mixed * (ws[2] + b0 * ws[6]) + g_factor * wv[3])
    g_n2 = 2.0 * (g_mixed * (ws[3] + b0 * ws[7]) + g_factor * wv[4])
    g_n3 = 2.0 * (g_mixed * (ws[4] + b0 * ws[8]))
    g_b = [g_b0]
    for a in range(3):
        g_b.append(g_mixed_v[a] * factor + g_n1 * b[1 + a])
    for m in range(4, 9):
        g_b.append(g_n2 * b[m])
    for m in range(9, 16):
        g_b.append(g_n3 * b[m])
    g_b_parts = [split(v) for v in g_b]
    grads = []
    for l in range(4):
        row = lin_at + l * channels
        high = jnp.concatenate([g_b_parts[m][0] for m in members[l]], axis=0)
        low = jnp.concatenate([g_b_parts[m][1] for m in members[l]], axis=0)
        amp_high = jnp.concatenate([amp_t_parts[m][0] for m in members[l]], axis=1)
        amp_low = jnp.concatenate([amp_t_parts[m][1] for m in members[l]], axis=1)
        flat[row : row + channels, :] = dot(
            jnp.concatenate([amp_high, amp_high, amp_low], axis=1),
            jnp.concatenate([high, low, high], axis=0),
        )
        back = dot(wcat3(w_lin[l], 1), jnp.concatenate([high, high, low], axis=1), NT) * NEIGH
        grads.extend(
            split(back[:, j * atoms : (j + 1) * atoms]) for j in range(len(members[l]))
        )
    grad_amp[:, :atoms] = by_block([high for high, _ in grads])
    grad_amp[:, atoms:] = by_block([low for _, low in grads])
    deal(flat, digits[0, 0], parts)


def skip_kernel(
    x_own, cot_s, cot_v, w_skip,
    g_total, skip_s, skip_v, skip_gs, skip_gv, g_skip,
):
    atoms, channels = cot_s.shape
    n_spec = w_skip.shape[1]

    at = 4 * atoms + 3
    species, cot_e, w_read = x_own[at : at + 1, :], x_own[at + 1 : at + 2, :], x_own[at + 2 : at + 3, :]
    cot_col = column(cot_e, channels)
    total = cot_s[...] + cot_col * w_read
    g_total[0] = total
    g_total[1] = cot_col
    species_col = column(species, channels)

    def pick(values, masks):
        result = values[0]
        for s in range(1, n_spec):
            result = jnp.where(masks[s], values[s], result)
        return result

    for kind in range(2):
        count = 1 + 2 * kind
        masks = [jnp.concatenate([species_col == float(s)] * count, axis=0) for s in range(n_spec)]
        x = x_own[kind * atoms : (kind + count) * atoms, :]
        g = jnp.concatenate([cot_v[a] for a in range(3)], axis=0) if kind else total
        weights = [split(w_skip[kind, s]) for s in range(n_spec)]
        wide = tuple(jnp.concatenate([w[i] for w in weights], axis=1) for i in range(2))
        tall = tuple(jnp.concatenate([w[i] for w in weights], axis=0) for i in range(2))
        forward = pick(columns_of(dot1(x, wide), n_spec), masks)
        back = pick(columns_of(dot1(g, tall, NT), n_spec), masks)
        if kind:
            for a in range(3):
                skip_v[a] = forward[a * atoms : (a + 1) * atoms]
                skip_gv[a] = back[a * atoms : (a + 1) * atoms]
        else:
            skip_s[...] = forward
            skip_gs[...] = back
        apart = jnp.concatenate([jnp.where(mask, g, 0.0) for mask in masks], axis=1)
        sums = dot1(x.T, apart)
        for s, value in enumerate(columns_of(sums, n_spec)):
            row = (kind * n_spec + s) * channels
            g_skip[row : row + channels, :] = value


def backward_messages(feats, radial, grads, geo_rows, g_radial, g_feats, channels, edges):
    ys = []
    for half in range(edges // LANES):
        cols = slice(half * LANES, (half + 1) * LANES)
        ys.append([jnp.broadcast_to(row[:, cols], (BLOCK, LANES)) for row in geo_rows])
    for c in range(0, channels, BLOCK):
        for half in range(edges // LANES):
            cols = slice(half * LANES, (half + 1) * LANES)
            low_cols = slice(edges + half * LANES, edges + (half + 1) * LANES)
            y = ys[half]

            def load(ref, k, count):
                at = row_of(k, count, c)
                return ref[at : at + BLOCK, cols]

            def grad(m):
                return load(grads, m, 16)

            def rad(k):
                return load(radial, k, 7)

            def put(ref, comp, count, value):
                high, low = split(value)
                at = row_of(comp, count, c)
                ref[at : at + BLOCK, cols] = high
                ref[at : at + BLOCK, low_cols] = low

            s = load(feats, 0, 4)
            third = y[9] * grad(9)
            for m in range(10, 16):
                third = third + y[m] * grad(m)
            put(g_radial, 3, 7, s * third)
            second = y[4] * grad(4)
            for m in range(5, 9):
                second = second + y[m] * grad(m)
            put(g_radial, 2, 7, s * second)
            g = [grad(1 + a) for a in range(3)]
            first = y[1] * g[0] + y[2] * g[1] + y[3] * g[2]
            put(g_radial, 1, 7, s * first)
            zero = grad(0)
            put(g_radial, 0, 7, s * zero)
            put(
                g_feats, 0, 4,
                rad(0) * zero + rad(1) * first + rad(2) * second + rad(3) * third,
            )
            v = [load(feats, 1 + a, 4) for a in range(3)]
            put(g_radial, 4, 7, (y[1] * v[0] + y[2] * v[1] + y[3] * v[2]) * zero)
            put(g_radial, 5, 7, v[0] * g[0] + v[1] * g[1] + v[2] * g[2])
            cross = [
                g[1] * y[3] - g[2] * y[2],
                g[2] * y[1] - g[0] * y[3],
                g[0] * y[2] - g[1] * y[1],
            ]
            put(g_radial, 6, 7, v[0] * cross[0] + v[1] * cross[1] + v[2] * cross[2])
            fourth, fifth, sixth = rad(4) * zero, rad(5), rad(6)
            for a in range(3):
                put(g_feats, 1 + a, 4, fourth * y[1 + a] + fifth * g[a] + sixth * cross[a])


def backward_kernel(slots, chunk, first, last, n_parts, *refs):
    n = len(slots)
    counts, digits, send, recv, grad_amp = refs[:5]
    geo, lifted, hidden = refs[5:8]
    x_refs, refs = refs[8 : 8 + n], refs[8 + n :]
    w_up, w_out, refs = refs[0], refs[1], refs[2:]
    if not first:
        acc_out_in, acc_up_in, refs = refs[0], refs[1], refs[2:]
    x_grads, g_hidden, refs = refs[:n], refs[n], refs[n + 1 :]
    if last:
        parts, refs = refs[:n_parts], refs[n_parts:]
        flat, refs = refs[0], refs[1:]
    else:
        g_out, g_up, refs = refs[0], refs[1], refs[2:]
    table, feats, radial, grads, g_radial, g_feats, g_lifted, acc_out = refs
    channels = w_up.shape[1]
    atoms = g_lifted.shape[2]
    hid = w_out.shape[0]
    total = list_chunks(table, slots, counts, chunk)
    w_blocked = radial_weights(w_out, channels)
    w_out_t = wcat3(w_blocked, 1)
    w_high, w_low = split(w_blocked.T)
    w_both = jnp.concatenate(
        [twice(w_high, 1), jnp.concatenate([w_low, jnp.zeros_like(w_low)], axis=1)], axis=0
    )
    if first:
        acc_out[...] = jnp.zeros_like(acc_out)
    else:
        acc_out[...] = acc_out_in[...]
    g_lifted[...] = jnp.zeros_like(g_lifted)
    g_radial[1] = jnp.zeros_like(g_radial[1])
    g_feats[1] = jnp.zeros_like(g_feats[1])

    def prepare(t, slot):
        p, k, cols = chunk_at(table, jnp.minimum(t, total - 1), chunk)
        high, low = hidden[p, :hid, cols], hidden[p, hid:, cols]
        to_hot = one_hot(recv[k, :, cols], atoms)
        grads[slot] = dot(grad_amp[...], twice(to_hot, 0))
        radial[slot] = dot(w_out_t, jnp.concatenate([high, high, low], axis=0))
        from_hot = one_hot(send[k, :, cols], atoms)
        feats[slot] = dot(lifted[p], twice(from_hot, 0))

    def collect(t, slot):
        p, k, cols = chunk_at(table, jnp.maximum(t, 0), chunk)
        tall = jnp.concatenate([g_radial[slot, :, :chunk], g_radial[slot, :, chunk:]], axis=0)
        both = dot(w_both, tall)
        g_hidden[p, :, cols] = both[:hid] + both[hid:]
        high, low = hidden[p, :hid, cols], hidden[p, hid:, cols]
        stacked = jnp.concatenate(
            [twice(high, 1), jnp.concatenate([low, jnp.zeros_like(low)], axis=1)], axis=0
        )
        acc_out[...] += dot(g_radial[slot], stacked, NT)
        from_hot = one_hot(send[k, :, cols], atoms)
        g_lifted[p] += dot(g_feats[slot], twice(from_hot, 1), NT)

    def combine(t, slot):
        p, _, cols = chunk_at(table, t, chunk)
        rows = [geo[p, ROW_Y + m : ROW_Y + m + 1, cols] for m in range(16)]
        backward_messages(
            feats.at[slot], radial.at[slot], grads.at[slot], rows, g_radial.at[slot],
            g_feats.at[slot], channels, chunk,
        )

    def step(i, carry):
        t = 2 * i
        combine(t, 0)
        prepare(t + 1, 1)
        collect(t - 1, 1)
        combine(t + 1, 1)
        prepare(t + 2, 0)
        collect(t, 0)
        return carry

    prepare(0, 0)
    lax.fori_loop(0, total // 2, step, 0)
    collect(total // 2 * 2 - 1, 1)

    @pl.when(total % 2 == 1)
    def _():
        combine(total - 1, 0)
        collect(total - 1, 0)

    w_up_parts = [split(w_up[0]), split(w_up[1])]
    sums = [None, None] if first else [acc_up_in[0], acc_up_in[1]]
    for p in range(n):
        lifted_grads = [component(g_lifted[p], comp, 4) for comp in range(4)]
        for kind in range(2):
            count = 1 + 2 * kind
            own = lifted_grads[kind : kind + count]
            tall = jnp.concatenate([value.T for value in own], axis=0)
            back = dot1(tall, w_up_parts[kind], NT)
            for a, value in enumerate(rows_of(back, count)):
                x_grads[p][kind + a] = value
            x = x_refs[p][kind * atoms : (kind + count) * atoms, :]
            part = dot1(jnp.concatenate(own, axis=1), x)
            sums[kind] = part if sums[kind] is None else sums[kind] + part
    if last:
        both = acc_out[...]
        both = both[:, :hid] + both[:, hid:]
        paths = both.shape[0] // channels
        up_at = paths * hid
        end = up_at + 2 * channels
        flat[end:, :] = jnp.zeros_like(flat[end:, :])
        for path in range(paths):
            flat[path * hid : (path + 1) * hid, :] = component(both, path, paths).T
        for kind in range(2):
            row = up_at + kind * channels
            flat[row : row + channels, :] = sums[kind].T
        deal(flat, digits[0, 0], parts)
    else:
        for kind in range(2):
            g_up[kind] = sums[kind]
        g_out[...] = acc_out[...]


def mlp_backward_kernel(groups, sources, *refs):
    counts, refs = refs[0], refs[1:]
    number = len(groups)
    geos, grads, refs = refs[:number], refs[number : 2 * number], refs[2 * number :]
    tapes, refs = refs[: 2 * len(sources)], refs[2 * len(sources) :]
    w_in, w_mid, small, acc_in, acc_mid = refs
    n_basis, hid = w_in.shape
    w_mid_n = [wcat3(w_mid[0], 1), wcat3(w_mid[1], 1)]
    acc_in[...] = jnp.zeros_like(acc_in)
    acc_mid[...] = jnp.zeros_like(acc_mid)
    edges = geos[0].shape[2]
    lane = lax.broadcasted_iota(jnp.int32, (hid, edges), 1)

    for i, (place, first) in enumerate(sources):
        kept_h, kept_d = tapes[2 * i], tapes[2 * i + 1]

        def one(at, place=place, first=first, kept_h=kept_h, kept_d=kept_d):
            slots, geo, grad = groups[place], geos[place], grads[place]
            p = first + at
            k = slots[0]
            for position, slot in enumerate(slots):
                k = jnp.where(p == position, slot, k)
            g3 = grad[p] * geo[p, ROW_ENV : ROW_ENV + 1, :]
            d3 = jnp.where(lane < counts[0, k], g3, 0.0) * kept_d[at, 2 * hid :, :]
            high, low = split(d3)
            acc_mid[1] += dot(kept_h[at, 2 * hid :, :], jnp.concatenate([high, low], axis=0), NT)
            d2 = dot(w_mid_n[1], jnp.concatenate([high, high, low], axis=0))
            d2 = d2 * kept_d[at, hid : 2 * hid, :]
            high, low = split(d2)
            acc_mid[0] += dot(kept_h[at, : 2 * hid, :], jnp.concatenate([high, low], axis=0), NT)
            d1 = dot(w_mid_n[0], jnp.concatenate([high, high, low], axis=0)) * kept_d[at, :hid, :]
            bessel = geo[p, :8, :]
            b_high = bessel.astype(BF16).astype(F32)
            basis = jnp.concatenate([b_high, bessel - b_high], axis=0).astype(BF16)
            high, low = split(d1)
            acc_in[...] += dot(basis, jnp.concatenate([high, low], axis=0), NT)

        in_pairs(kept_h.shape[0], one)

    def quadrants(v, rows):
        return v[:rows, :hid] + v[:rows, hid:] + v[rows:, :hid]

    small[hid + n_basis :, :] = jnp.zeros_like(small[hid + n_basis :, :])
    small[:hid, :] = jnp.concatenate([quadrants(acc_mid[layer], hid) for layer in range(2)], axis=1)
    basis_grad = quadrants(acc_in[...], n_basis)
    small[hid : hid + n_basis, :] = jnp.concatenate([basis_grad, jnp.zeros_like(basis_grad)], axis=1)


def call(kernel, out_shape, smem, scratch, args, name, us):
    specs = [SMEM] * smem + [VMEM] * (len(args) - smem)
    return call_with(kernel, out_shape, specs, scratch, args, name, us)


def call_with(kernel, out_shape, specs, scratch, args, name, us):
    return pl.pallas_call(
        kernel,
        out_shape=out_shape,
        in_specs=specs,
        out_specs=jax.tree.map(lambda _: VMEM, out_shape),
        scratch_shapes=scratch,
        compiler_params=pltpu.CompilerParams(vmem_limit_bytes=LIMIT),
        cost_estimate=pl.CostEstimate(
            flops=int(us * 5e8), bytes_accessed=int(us * 2e6), transcendentals=0
        ),
        name=name,
    )(*args)


def shape(*dims, dtype=F32):
    return jax.ShapeDtypeStruct(dims, dtype)


def shifted(value, steps):
    count = lax.axis_size("blk")
    return lax.ppermute(value, "blk", [(i, (i + steps) % count) for i in range(count)])


def stages_of(count):
    stages, stride = [], 1
    while stride < count:
        members = 4 if (count // stride) % 4 == 0 else 2
        stages.append((members, stride))
        stride *= members
    return stages[::-1]


def exchange(values, stage):
    members, stride = stage
    count = lax.axis_size("blk")
    moved = [
        lax.ppermute(values[k], "blk", [(i, i ^ (k * stride)) for i in range(count)])
        for k in range(1, members)
    ]
    return [values[0]] + moved


def add_parts(groups, stages, at, digits):
    arrays = [part for parts, _ in groups for part in parts]
    counts = tuple((len(parts), tuple(sizes)) for parts, sizes in groups)
    total = sum(size for _, sizes in groups for size in sizes)
    out = stages[at + 1][0] if at + 1 < len(stages) else 1
    shapes = shape(total, LANES)
    if out > 1:
        shapes = tuple(shape(total // out, LANES) for _ in range(out))
    return call(
        functools.partial(add_kernel, at + 1, counts, out), shapes, 1,
        [pltpu.VMEM((total, LANES), F32)] if out > 1 else [], (digits, *arrays), f"add_{at}", 1,
    )


def join_parts(parts, segments, stages, at, digits, tail):
    members = stages[at][0]
    rows = members * sum(rows * blocks for rows, blocks in segments) + tail
    return call(
        functools.partial(join_kernel, at, members, segments, tail), shape(rows, LANES), 1,
        [pltpu.VMEM((members, tail, LANES), F32)] if tail else [], (digits, *parts),
        f"join_{at}", 1,
    )


def per_device(
    node_scalars, node_vectors, positions, species, edge_senders, edge_receivers, edge_shifts,
    bucket_counts, w_up, w_rad_in, w_rad_mid, w_rad_out, w_lin, w_sc_scalar, w_sc_vector, w_prod,
    w_skip, w_read, cot_scalars, cot_vectors, cot_energy,
):
    _, buckets, slots = edge_senders.shape
    send = edge_senders.reshape(buckets, 1, slots)
    recv = edge_receivers.reshape(buckets, 1, slots)
    shift = edge_shifts.reshape(3 * buckets, 1, slots)
    reach = (buckets - 1) // 2
    atoms, channels = node_scalars.shape
    hid, outs = w_rad_out.shape
    n_basis = w_rad_in.shape[0]
    n_spec = w_skip.shape[1]
    chunk = min(256, slots)
    blocks = lax.axis_size("blk")
    stages = stages_of(blocks)
    me = lax.axis_index("blk")
    digits = jnp.stack([(me // stride) % members for members, stride in stages]).reshape(1, -1)
    rows, at = [], 0
    height = up8(4 * atoms + 6)
    for piece in (node_scalars, node_vectors.reshape(3 * atoms, channels), positions,
                  species.reshape(1, atoms), cot_energy.reshape(1, atoms),
                  w_read.reshape(1, channels)):
        end = at + piece.shape[0]
        rows.append(jnp.pad(piece, ((at, height - end), (0, 0))).astype(F32))
        at = end
    packed = functools.reduce(jnp.add, rows)
    offsets = sorted([d for d in range(-reach, reach + 1) if d], key=abs)
    x_of = {reach: packed, **{reach + d: shifted(packed, -d) for d in offsets}}
    sc_s_t, sc_v_t = jnp.swapaxes(w_sc_scalar, 0, 1), jnp.swapaxes(w_sc_vector, 0, 1)

    skip_rows = 2 * n_spec * channels
    g_total, skip_s, skip_v, skip_gs, skip_gv, g_skip = call(
        skip_kernel,
        (shape(2, atoms, channels), shape(atoms, channels), shape(3, atoms, channels),
         shape(atoms, channels), shape(3, atoms, channels), shape(skip_rows, channels)),
        0, [],
        (packed, cot_scalars, cot_vectors, w_skip),
        "self_connection", 4,
    )

    def padded(rows):
        unit = 8 * blocks
        return -(-rows // unit) * unit

    node_rows = padded(skip_rows + 6 * channels + up8(9 * n_spec) + up8(5 * n_spec) + 8)
    edge_rows = padded(outs // channels * hid + 2 * channels)
    tail_unit = 8 * (blocks // stages[0][0])
    small_rows = -(-(hid + n_basis) // tail_unit) * tail_unit

    near = (reach - 1, reach + 1)
    far = tuple(k for k in range(buckets) if abs(k - reach) > 1)
    groups = [(reach,), near] + ([far] if far else [])
    most = [len(g) * (slots // chunk) for g in groups]
    first_parts = stages[0][0]
    acc = ()
    kept, tapes = [], []
    for at, group in enumerate(groups):
        n = len(group)
        last = at == len(groups) - 1
        base = len(groups[1]) if at == 2 else 0
        out_shapes = (
            shape(base + n, 4 * channels, 2 * atoms, dtype=BF16), shape(base + n, 2 * hid, slots, dtype=BF16),
            shape(base + n, GEO_ROWS, slots), shape(n, 4 * hid, slots, dtype=BF16),
            shape(n, 3 * hid, slots),
        )
        scratch = [
            pltpu.SMEM((3, most[at]), jnp.int32),
            pltpu.VMEM((2, 4 * channels, chunk), F32),
            pltpu.VMEM((2, outs, chunk), F32),
            pltpu.VMEM((2, 16 * channels, 2 * chunk), BF16),
        ]
        node_args, node_counts = (), None
        if last:
            node_args = (digits, w_lin, sc_s_t, sc_v_t, w_prod, g_total,
                         cot_vectors, skip_s, skip_v, g_skip)
            node_outs = (
                shape(atoms, channels), shape(3, atoms, channels), shape(1, atoms),
                shape(16 * channels, 2 * atoms, dtype=BF16),
                *[shape(node_rows // first_parts, LANES)] * first_parts,
            )
            node_counts = len(node_args), len(node_outs)
            scratch = [
                pltpu.VMEM((16 * channels, atoms), F32), pltpu.VMEM((node_rows, LANES), F32)
            ] + scratch
            out_shapes = node_outs + out_shapes
        else:
            out_shapes = (shape(16 * channels, atoms),) + out_shapes
        args = (
            bucket_counts, send, recv, shift, packed, *[x_of[k] for k in group], w_up, w_rad_in,
            w_rad_mid, w_rad_out, *acc, *(kept[-1] if base else ()), *node_args,
        )
        specs = [SMEM] + [VMEM] * (len(args) - 1)
        if last:
            specs[len(args) - len(node_args)] = SMEM
        result = call_with(
            functools.partial(forward_kernel, base, group, chunk, at == 0, node_counts), out_shapes,
            specs, scratch, args, f"edges_{at}", 5 * n + (6 if last else 0),
        )
        kept.append(result[-5:-2])
        tapes.append(result[-2:])
        if last:
            new_s, new_v, energy, grad_amp = result[:4]
            node_parts = result[4 : 4 + first_parts]
        else:
            acc = result[:1]

    tie = lax.optimization_barrier
    node_parts = exchange(node_parts, stages[0])
    others = tuple(k for group in groups[1:] for k in group)
    sums = ()
    n_early = len(others) // 2
    grads_hidden = []
    home = []
    for group, (lifted, hidden, geo) in ((others, kept[-1]), (groups[0], kept[0])):
        n = len(group)
        first, last = not sums, bool(sums)
        if last:
            final = (shape(edge_rows // first_parts, LANES),) * first_parts
        else:
            final = (shape(outs, 2 * hid), shape(2, channels, channels))
        args = (
            bucket_counts, digits, send, recv, grad_amp, geo, lifted, hidden,
            *[x_of[k] for k in group], w_up, w_rad_out, *sums,
        )
        result = call(
            functools.partial(backward_kernel, group, chunk, first, last, first_parts),
            (*[shape(4, atoms, channels) for _ in group], shape(n, hid, slots), *final), 2,
            ([pltpu.VMEM((edge_rows, LANES), F32)] if last else [])
            + [
                pltpu.SMEM((3, n * (slots // chunk)), jnp.int32),
                pltpu.VMEM((2, 4 * channels, chunk), F32),
                pltpu.VMEM((2, outs, chunk), F32),
                pltpu.VMEM((2, 16 * channels, chunk), F32),
                pltpu.VMEM((2, outs, 2 * chunk), BF16),
                pltpu.VMEM((2, 4 * channels, 2 * chunk), BF16),
                pltpu.VMEM((n, 4 * channels, atoms), F32),
                pltpu.VMEM((outs, 2 * hid), F32),
            ],
            args, "edges_back_own" if last else "edges_back", 6 * n,
        )
        if first:
            result, node_parts = tie((result, node_parts))
            away = [(k - reach, value) for k, value in zip(group, result[:n])]
            away.sort(key=lambda pair: -abs(pair[0]))
            home = [shifted(value, offset) for offset, value in away[:n_early]]
        else:
            values = [value for _, value in away[n_early:]]
            result, early, values = tie((result, home, values))
            late = [shifted(value, offset) for (offset, _), value in zip(away[n_early:], values)]
            edge_parts = exchange(result[n + 1 :], stages[0])
            home = early + [result[0]]
        grads_hidden.append(result[n])
        sums = result[n + 1 :]
    sources, first = [], 0
    for tape in tapes[1:]:
        sources.append((0, first))
        first += tape[0].shape[0]
    sources.append((1, 0))
    small = call(
        functools.partial(mlp_backward_kernel, (others, groups[0]), sources),
        shape(small_rows, LANES), 1,
        [pltpu.VMEM((2 * n_basis, 2 * hid), F32), pltpu.VMEM((2, 2 * hid, 2 * hid), F32)],
        (bucket_counts, kept[-1][2], kept[0][2], *grads_hidden,
         *[array for tape in tapes[1:] + tapes[:1] for array in tape], w_rad_in, w_rad_mid),
        "radial_back", 7,
    )
    small, edge_parts = tie((small, edge_parts))
    sizes = [node_rows // first_parts, edge_rows // first_parts, small_rows]
    groups = [(node_parts, sizes[:1]), (edge_parts, sizes[1:2]), ([small], sizes[2:])]
    whole = add_parts(groups, stages, 0, digits)
    for at in range(1, len(stages)):
        sizes = [size // stages[at][0] for size in sizes]
        parts = exchange(whole, stages[at])
        if at == 1:
            parts, late = tie((parts, late))
            home = home + late
        whole = add_parts([(parts, sizes)], stages, at, digits)
    blocks_now, tail_blocks = 1, 1
    for at in range(len(stages)):
        members = stages[at][0]
        parts = exchange([whole] * members, stages[at])
        segments = [(sizes[0], blocks_now), (sizes[1], blocks_now)]
        if at:
            segments.append((sizes[2], tail_blocks))
            tail_blocks *= members
        blocks_now *= members
        if at + 1 < len(stages):
            whole = join_parts(parts, segments, stages, at, digits, 0 if at else sizes[2])
    g_skip, g_lin, g_prod, g_sc_s, g_sc_v, g_read, g_out, g_up, g_mid, g_in = call(
        functools.partial(finish_kernel, len(stages) - 1, stages[-1][0], segments, n_spec),
        (shape(skip_rows, channels), shape(4 * channels, channels), shape(2 * channels, channels),
         shape(9, n_spec, channels), shape(5, n_spec, channels), shape(1, channels),
         shape(hid, outs), shape(2 * channels, channels), shape(2, hid, hid), shape(n_basis, hid)),
        1,
        [pltpu.VMEM((node_rows + edge_rows + small_rows, LANES), F32)],
        (digits, *parts), "finish", 2,
    )
    gx = home[0]
    for part in home[1:]:
        gx = gx + part
    return (
        new_s, new_v, energy.reshape(-1), gx[0] + skip_gs, gx[1:] + skip_gv,
        g_up.reshape(1, 2, channels, channels), g_in[None], g_mid[None], g_out[None],
        g_lin.reshape(1, 4, channels, channels), jnp.swapaxes(g_sc_s, 0, 1)[None],
        jnp.swapaxes(g_sc_v, 0, 1)[None], g_prod.reshape(1, 2, channels, channels),
        g_skip.reshape(1, 2, n_spec, channels, channels), g_read,
    )


def solution(mesh):
    atoms = ("cell", "blk")
    in_specs = (
        P(atoms, None), P(None, atoms, None), P(None, atoms), P(atoms), P(atoms, None, None),
        P(atoms, None, None), P(atoms, None, None, None), P(atoms, None),
        P(), P(), P(), P(), P(), P(), P(), P(), P(), P(),
        P(atoms, None), P(None, atoms, None), P(atoms),
    )
    out_specs = (
        P(atoms, None), P(None, atoms, None), P(atoms), P(atoms, None), P(None, atoms, None),
        P("cell", None, None, None), P("cell", None, None), P("cell", None, None, None),
        P("cell", None, None), P("cell", None, None, None), P("cell", None, None, None),
        P("cell", None, None, None), P("cell", None, None, None),
        P("cell", None, None, None, None), P("cell", None),
    )
    return jax.shard_map(
        per_device, mesh=mesh, in_specs=in_specs, out_specs=out_specs, check_vma=False
    )
```
